512 devices in a mesh: dp: 2 (over core), tensor: 16 (over z), expert: 16 (over y, x).
Axes of the slice: x: 4, y: 4, z: 16, core: 2. Of those that a mesh axis runs over, the one named last changes fastest.
Arguments:
- queries: bfloat16 [4096, 8192], P(('dp', 'expert'), 'tensor'), parts along dimension 0, may hold values from -120 to 120
- all_key_rows: bfloat16 [4096, 512], P(('dp', 'expert')), parts along dimension 0, may hold values from -6 to 6
- all_value_rows: bfloat16 [4096, 512], P(('dp', 'expert')), parts along dimension 0, may hold values from -6 to 6
- out_weight: bfloat16 [8192, 4096], P('tensor', 'expert'), may hold values from -0.5 to 0.5
- residual: bfloat16 [4096, 4096], P(('dp', 'expert')), parts along dimension 0, may hold values from -6 to 6
- post_gain: float32 [4096], replicated, may hold values from 0.4 to 2.5
- routes: int32 [4096, 2], P(('dp', 'expert')), parts along dimension 0, may hold values from 0 to 15, all different within a row; in each aligned block of 128 rows (0 to 127, 128 to 255, ...) at most 32 rows name the same one
- route_weight: float32 [4096, 2], P(('dp', 'expert')), parts along dimension 0, may hold values from 0.1 to 1
- gate_weight: bfloat16 [16, 4096, 1536], P('expert', None, 'tensor'), may hold values from -0.09375 to 0.09375
- up_weight: bfloat16 [16, 4096, 1536], P('expert', None, 'tensor'), may hold values from -0.09375 to 0.09375
- down_weight: bfloat16 [16, 1536, 4096], P('expert', None, 'tensor'), may hold values from -0.15625 to 0.15625
Outputs:
- layer_out: bfloat16 [4096, 4096], P(('dp', 'expert'), 'tensor'), parts along dimension 0
The draws below stay inside these ranges and needn't reach their ends.
There are 2 independent parts, one for each index of `dp`. The reference program is written for one: setup_inputs(seed, part) draws one part's arguments, and reference() takes and returns one part's arrays. A program takes and returns all parts, laid end to end along the dimension named above; an argument that names none is the same for every part. Nothing has to cross between parts.
Inputs may be any that keep to these rules, and one draw needn't show every extreme that they name: `routes`: each row names 2 different experts. The rows of one device name any expert at most 32 times, and in every draw some expert is named exactly 32 times by the rows of some device.
All inputs are finite; a program needn't handle non-finite values.
Results may differ from the reference program's by a relative error of at most 0.023.
Values may be sent and summed in bfloat16 or wider, within the bound.
No kernel may reach another device: no remote copies, remote signals or barrier semaphores. Data moves between devices by JAX's collectives and lax.ppermute only.
A program may use at most 64 MiB of HBM per device.

```python
import math
import jax
import jax.numpy as jnp
import numpy as np
from jax import lax

D = 4096
QUERY_HEADS = 64
KEY_VALUE_HEADS = 4
HEAD_WIDTH = 128
FF = 1536
TOP = 2
TOK_DEV = 128
PREFILL_TOKENS = 2048
EXPERTS = 16
CAP = 32
N_EXPERT = 16


def drawn_parts(key):
    start_index = jnp.clip(jax.random.normal(jax.random.fold_in(key, 11), (PREFILL_TOKENS, KEY_VALUE_HEADS * HEAD_WIDTH), jnp.float32), -6.0, 6.0)
    return start_index


def draw_all_key_rows(key, part):
    start_index = drawn_parts(key)
    return start_index.astype(jnp.bfloat16)


def draw_queries(key, part):
    key = jax.random.fold_in(key, 5)
    own = jnp.clip(jax.random.normal(key, (PREFILL_TOKENS, QUERY_HEADS * HEAD_WIDTH), jnp.float32), -6.0, 6.0)
    return own.astype(jnp.bfloat16)


def level_of(own_key, dims, cuts, low, largest):
    def one(dim, blocks):
        draws = jax.random.uniform(jax.random.fold_in(jax.random.fold_in(own_key, 6), dim), (blocks,), jnp.float32, low / len(cuts), largest / len(cuts))
        return jnp.repeat(jnp.exp(draws), dims[dim] // blocks).reshape((-1,) + (1,) * (len(dims) - dim - 1))

    factor_of = one(*cuts[0])
    for cut in cuts[1:]:
        factor_of = factor_of * one(*cut)
    return factor_of


def routed_block(own_key, own, number, rows, amount, top, limit, lean):
    sequence = jax.random.permutation(own_key, amount)
    heavy_load, ordinary = shares(amount, rows * top, limit, lean, True), shares(amount, rows * top, limit, lean, False)
    places = jnp.arange(amount)

    def named(tallies, turn):
        used = int((tallies > 0).sum())
        fixed = max(1, used // 4)
        moved = fixed + (places - fixed + turn * (used - fixed)) % max(1, amount - fixed)
        return jnp.zeros((amount,), jnp.int32).at[sequence[jnp.where(places < fixed, places, moved)]].set(jnp.asarray(tallies, jnp.int32))

    tallies = jnp.where(number % 4 == 0, named(heavy_load, number // 4), named(ordinary, number - number // 4 - 1))
    mixed = jax.random.permutation(jax.random.fold_in(own, 3), amount)
    donor, sink = mixed[0:amount // 2 * 2:2], mixed[1:amount // 2 * 2:2]
    room = jnp.minimum(tallies[donor] - 1, limit - tallies[sink]) // 2
    room = jnp.where((donor == sequence[0]) | (sink == sequence[0]) | (tallies[sink] == 0), 0, jnp.maximum(room, 0))
    moved = jax.random.randint(jax.random.fold_in(own, 4), (amount // 2,), 0, 1 << 20) % (room + 1)
    tallies = tallies.at[donor].add(-moved).at[sink].add(moved)
    items = jnp.searchsorted(jnp.cumsum(tallies), jnp.arange(rows * top), side="right").astype(jnp.int32)
    table = items.reshape(top, rows).T
    table = table[jax.random.permutation(jax.random.fold_in(own, 1), rows)]
    turn = jax.random.randint(jax.random.fold_in(own, 2), (rows, 1), 0, top)
    return jnp.take_along_axis(table, (jnp.arange(top)[None, :] + turn) % top, axis=1)


def shares(number_of, total, bound, lean, full):
    portions = [(1 << 20) // math.isqrt(grade ** lean) + 1 for grade in range(1, number_of + 1)]
    largest = bound if full else min(bound, max(-(-total // number_of), total * portions[0] // sum(portions)))
    least = 1 if total - largest >= number_of - 1 else 0
    counts, spare = [largest] + [least] * (number_of - 1), total - largest - least * (number_of - 1)
    while spare > 0:
        free = [i for i in range(1, number_of) if counts[i] < largest] or [i for i in range(1, number_of) if counts[i] < bound]
        mass, left = sum([portions[i] for i in free]), spare
        for i in free:
            more = min(bound - counts[i], max(1, left * portions[i] // mass), spare)
            counts[i] = counts[i] + more
            spare = spare - more
    return np.array(counts)


def gaussian(stream_key, dims, width, bound, split=(), kind=jnp.bfloat16):
    factor_of = level_of(stream_key, dims, split, -0.22, 0.18) if split else 1.0
    entries = jax.random.normal(stream_key, dims, jnp.float32) * width * factor_of
    return jnp.minimum(jnp.maximum(entries, -bound), bound).astype(kind)


def setup_inputs(seed: int = 0, part: int = 0) -> dict:
    splits = jax.random.split(jax.random.key(seed), 12)
    part_splits = jax.random.split(jax.random.fold_in(splits[11], part), 12)
    queries = draw_queries(jax.random.fold_in(jax.random.fold_in(splits[11], part), 71), part)
    all_key_rows = draw_all_key_rows(jax.random.fold_in(jax.random.fold_in(splits[11], part), 71), part)
    all_value_rows = gaussian(part_splits[2], (PREFILL_TOKENS, KEY_VALUE_HEADS * HEAD_WIDTH), 1.0, 6.0, ((0, 16),))
    out_weight = gaussian(splits[3], (QUERY_HEADS * HEAD_WIDTH, D), HEAD_WIDTH ** -0.5, 0.5, ((0, 16), (1, 16)))
    residual = gaussian(part_splits[4], (PREFILL_TOKENS, D), 1.0, 6.0, ((0, 16),))
    post_gain = jnp.clip(jnp.exp(jax.random.uniform(splits[5], (D,), jnp.float32, math.log(0.4), math.log(2.5))), 0.4, 2.5)
    routes_keys = jax.random.split(jax.random.fold_in(part_splits[6], 1), PREFILL_TOKENS // TOK_DEV)
    routes_turns = jax.random.permutation(jax.random.fold_in(part_splits[6], 3), PREFILL_TOKENS // TOK_DEV)
    routes = jax.vmap(lambda own, number: routed_block(jax.random.fold_in(part_splits[6], 2), own, number, TOK_DEV, EXPERTS, TOP, CAP, 2))(routes_keys, routes_turns).reshape((PREFILL_TOKENS, TOP))
    route_weight = jnp.clip(jnp.exp(math.log(1.0) - 2.3025851 * jax.random.uniform(part_splits[7], (PREFILL_TOKENS, TOP), jnp.float32) ** level_of(part_splits[7], (PREFILL_TOKENS, TOP), ((0, 16),), -0.2, 0.2)), 0.1, 1.0)
    gate_weight = gaussian(splits[8], (EXPERTS, D, FF), D ** -0.5, 0.09375, ((0, 16), (2, 16)))
    up_weight = gaussian(splits[9], (EXPERTS, D, FF), D ** -0.5, 0.09375, ((0, 16), (2, 16)))
    down_weight = gaussian(splits[10], (EXPERTS, FF, D), FF ** -0.5, 0.15625, ((0, 16), (2, 16)))
    return dict(queries=queries, all_key_rows=all_key_rows, all_value_rows=all_value_rows, out_weight=out_weight, residual=residual, post_gain=post_gain, routes=routes, route_weight=route_weight, gate_weight=gate_weight, up_weight=up_weight, down_weight=down_weight)


def attention_heads(queries, all_key_rows, all_value_rows):
    group_width = QUERY_HEADS // KEY_VALUE_HEADS
    query_heads = queries.reshape(PREFILL_TOKENS, QUERY_HEADS, HEAD_WIDTH)
    head_keys = all_key_rows.reshape(PREFILL_TOKENS, KEY_VALUE_HEADS, HEAD_WIDTH)
    head_values = all_value_rows.reshape(PREFILL_TOKENS, KEY_VALUE_HEADS, HEAD_WIDTH)
    position = jnp.arange(PREFILL_TOKENS, dtype=jnp.int32)
    visible = position[:, None] >= position[None, :]

    def one_head(head_index):
        shared = head_index // group_width
        query_one = lax.dynamic_index_in_dim(query_heads, head_index, 1, keepdims=False)
        key_one = lax.dynamic_index_in_dim(head_keys, shared, 1, keepdims=False)
        value_one = lax.dynamic_index_in_dim(head_values, shared, 1, keepdims=False)
        scores = jnp.dot(query_one, key_one.T, preferred_element_type=jnp.float32) * HEAD_WIDTH ** (-0.5)
        masked = jnp.where(visible, scores, -jnp.inf)
        row_max = lax.optimization_barrier(jnp.max(masked, axis=1, keepdims=True))
        exponent = jnp.where(visible, jnp.exp(masked - row_max), 0.0)
        row_total = lax.optimization_barrier(jnp.sum(exponent, axis=1, keepdims=True))
        weights = exponent.astype(jnp.bfloat16)
        summed = jnp.dot(weights, value_one, preferred_element_type=jnp.float32)
        return (summed / row_total).astype(jnp.bfloat16)
    stacked = lax.map(one_head, jnp.arange(QUERY_HEADS, dtype=jnp.int32))
    return jnp.transpose(stacked, (1, 0, 2)).reshape(PREFILL_TOKENS, QUERY_HEADS * HEAD_WIDTH)

def expert_apply(operands):
    buffer_rows, gate_one, up_one, down_one = operands
    gate_values = jnp.dot(buffer_rows, gate_one, preferred_element_type=jnp.float32)
    up_values = jnp.dot(buffer_rows, up_one, preferred_element_type=jnp.float32)
    activation = (jax.nn.silu(gate_values) * up_values).astype(jnp.bfloat16)
    return jnp.dot(activation, down_one, preferred_element_type=jnp.float32).astype(jnp.bfloat16)

def reference(queries, all_key_rows, all_value_rows, out_weight, residual, post_gain, routes, route_weight, gate_weight, up_weight, down_weight):
    attended = attention_heads(queries, all_key_rows, all_value_rows)
    hidden = residual.astype(jnp.float32) + jnp.dot(attended, out_weight, preferred_element_type=jnp.float32)
    mean_square = lax.optimization_barrier(jnp.mean(hidden * hidden, axis=1, keepdims=True))
    normed = (hidden * lax.rsqrt(mean_square + 1e-06) * post_gain).astype(jnp.bfloat16)
    capacity = N_EXPERT * CAP
    flat_routes = routes.reshape(-1).astype(jnp.int32)
    onehot = (flat_routes[:, None] == jnp.arange(EXPERTS, dtype=jnp.int32)[None, :]).astype(jnp.int32)
    ranking = (jnp.cumsum(onehot, axis=0) - 1).astype(jnp.int32)
    slot_index = lax.optimization_barrier(jnp.sum(ranking * onehot, axis=1)).astype(jnp.int32)
    target = (flat_routes * capacity + slot_index).astype(jnp.int32)
    source_row = jnp.arange(PREFILL_TOKENS * TOP, dtype=jnp.int32) // TOP
    buffers = jnp.zeros((EXPERTS * capacity, D), jnp.bfloat16).at[target].set(normed[source_row])
    buffers = buffers.reshape(EXPERTS, capacity, D)
    results = lax.map(expert_apply, (buffers, gate_weight, up_weight, down_weight))
    picked = results.reshape(EXPERTS * capacity, D)[target].astype(jnp.float32).reshape(PREFILL_TOKENS, TOP, D)
    mixed = lax.optimization_barrier(jnp.sum(picked * route_weight[:, :, None], axis=1))
    return (hidden + mixed).astype(jnp.bfloat16)
```

```python
import jax
import jax.numpy as jnp
from jax import lax
from jax.sharding import PartitionSpec as P

D = 4096
QUERY_HEADS = 64
KEY_VALUE_HEADS = 4
HEAD_WIDTH = 128
TOP = 2
QUARTER = 4
CLOSE = [[QUARTER * i + j for j in range(QUARTER)] for i in range(QUARTER)]
SPREAD = [[QUARTER * j + i for j in range(QUARTER)] for i in range(QUARTER)]
SWAP = [(0, 1), (1, 0)]


def route_slots(routes, experts_count, capacity):
    flat_routes = routes.reshape(-1)
    onehot = (
        flat_routes[:, None] == jnp.arange(experts_count, dtype=jnp.int32)[None, :]
    ).astype(jnp.bfloat16)
    order = jnp.arange(flat_routes.shape[0], dtype=jnp.int32)
    before = (order[:, None] > order[None, :]).astype(jnp.bfloat16)
    ranking = jnp.dot(before, onehot, preferred_element_type=jnp.float32)
    slot_index = jnp.sum(ranking * onehot.astype(jnp.float32), axis=1).astype(jnp.int32)
    return flat_routes, slot_index


def local(
    queries,
    all_key_rows,
    all_value_rows,
    out_weight,
    residual,
    post_gain,
    routes,
    route_weight,
    gate_weight,
    up_weight,
    down_weight,
):
    tokens = queries.shape[0]
    local_heads = queries.shape[1] // HEAD_WIDTH
    group_width = QUERY_HEADS // KEY_VALUE_HEADS
    tensor_count = lax.axis_size("tensor")
    expert_count = lax.axis_size("expert")
    tensor_index = lax.axis_index("tensor")
    expert_index = lax.axis_index("expert")
    core = lax.axis_index("dp")
    columns = D // tensor_count
    capacity = 2 * tokens * TOP // expert_count
    slot_count = expert_count * capacity
    part = capacity // QUARTER
    rows = expert_count * part

    gate_or_up = jnp.where(core == 0, gate_weight[0], up_weight[0]).T
    first_own = lax.all_gather(gate_or_up, "tensor", axis=0, tiled=True, axis_index_groups=CLOSE)
    first_other = lax.ppermute(first_own, "dp", SWAP)
    hidden_units = down_weight.shape[1]
    half_units = hidden_units // 2
    down_half = lax.dynamic_slice_in_dim(down_weight[0], core * half_units, half_units, 0)
    down_own = lax.all_gather(down_half, "tensor", axis=0, axis_index_groups=CLOSE)
    down_other = lax.ppermute(down_own, "dp", SWAP)

    shared = tensor_index * local_heads // group_width
    key_head = lax.dynamic_slice_in_dim(all_key_rows, shared * HEAD_WIDTH, HEAD_WIDTH, 1)
    value_head = lax.dynamic_slice_in_dim(all_value_rows, shared * HEAD_WIDTH, HEAD_WIDTH, 1)
    half_rows = out_weight.shape[0] // 2
    weight_half = lax.dynamic_slice_in_dim(out_weight, core * half_rows, half_rows, 0)
    message = jnp.concatenate([jnp.concatenate([key_head, value_head], axis=1), weight_half], axis=0)
    gathered = lax.all_to_all(
        jnp.broadcast_to(message[None], (expert_count,) + message.shape),
        "expert",
        split_axis=0,
        concat_axis=0,
        tiled=True,
    )
    weight_own = gathered[:, tokens:, :]
    weight_other = lax.ppermute(weight_own, "dp", SWAP)
    key_piece = gathered[:, :tokens, :HEAD_WIDTH].reshape(expert_count * tokens, HEAD_WIDTH)
    value_piece = gathered[:, :tokens, HEAD_WIDTH:].reshape(expert_count * tokens, HEAD_WIDTH)

    query_heads = queries.reshape(tokens, local_heads, HEAD_WIDTH)
    query_place = expert_index * tokens + jnp.arange(tokens, dtype=jnp.int32)
    scores = jnp.einsum(
        "thd,sd->hts", query_heads, key_piece, preferred_element_type=jnp.float32
    ) * HEAD_WIDTH ** (-0.5)
    key_place = jnp.arange(key_piece.shape[0], dtype=jnp.int32)
    visible = (query_place[:, None] >= key_place[None, :])[None, :, :]
    masked = jnp.where(visible, scores, -1e30)
    row_max = jnp.max(masked, axis=2)
    exponent = jnp.where(visible, jnp.exp(masked - row_max[:, :, None]), 0.0)
    row_total = jnp.sum(exponent, axis=2)
    accumulated = jnp.einsum(
        "hts,sd->htd",
        exponent.astype(jnp.bfloat16),
        value_piece,
        preferred_element_type=jnp.float32,
    )
    attended = (accumulated / row_total[:, :, None]).astype(jnp.bfloat16)
    attended = jnp.transpose(attended, (1, 0, 2)).reshape(tokens, local_heads * HEAD_WIDTH)

    attended_own = lax.dynamic_slice_in_dim(attended, core * half_rows, half_rows, 1)
    attended_other = lax.dynamic_slice_in_dim(attended, (1 - core) * half_rows, half_rows, 1)
    partial_value = jnp.einsum(
        "tk,ekn->etn", attended_own, weight_own, preferred_element_type=jnp.float32
    ) + jnp.einsum(
        "tk,ekn->etn", attended_other, weight_other, preferred_element_type=jnp.float32
    )
    partial_sums = lax.all_to_all(
        partial_value.astype(jnp.bfloat16), "tensor", split_axis=0, concat_axis=0, tiled=True
    )
    head_total = jnp.sum(partial_sums.astype(jnp.float32), axis=0)
    residual_share = lax.dynamic_slice_in_dim(residual, tensor_index * columns, columns, 1)
    hidden_share = residual_share.astype(jnp.float32) + head_total

    flat_routes, slot_index = route_slots(routes, expert_count, capacity)
    target = flat_routes * capacity + slot_index
    slot_place = jnp.arange(slot_count, dtype=jnp.int32)
    packing = jnp.any(
        target.reshape(tokens, TOP)[None, :, :] == slot_place[:, None, None], axis=2
    ).astype(jnp.bfloat16)
    packed = jnp.dot(
        packing, hidden_share.astype(jnp.bfloat16), preferred_element_type=jnp.float32
    ).astype(jnp.bfloat16)
    arrived = lax.all_to_all(
        packed.reshape(expert_count, capacity, columns),
        "expert",
        split_axis=0,
        concat_axis=0,
        tiled=True,
    )
    quarters = jnp.transpose(
        arrived.reshape(expert_count, QUARTER, part, columns), (1, 0, 2, 3)
    ).reshape(1, QUARTER, rows, columns)
    quarters = jnp.broadcast_to(quarters, (tensor_count // QUARTER, QUARTER, rows, columns))
    full_rows = lax.all_to_all(
        quarters.reshape(tensor_count, rows, columns),
        "tensor",
        split_axis=0,
        concat_axis=0,
        tiled=True,
    )
    full_rows = jnp.transpose(full_rows, (1, 0, 2)).reshape(rows, D).astype(jnp.float32)
    mean_square = jnp.mean(full_rows * full_rows, axis=1, keepdims=True)
    normed = (full_rows * lax.rsqrt(mean_square + 1e-06) * post_gain).astype(jnp.bfloat16)

    contract_last = (((1,), (1,)), ((), ()))
    product_own = lax.dot_general(
        normed, first_own, contract_last, preferred_element_type=jnp.float32
    )
    product_other = lax.dot_general(
        normed, first_other, contract_last, preferred_element_type=jnp.float32
    )
    gate_values = jnp.where(core == 0, product_own, product_other)
    up_values = jnp.where(core == 0, product_other, product_own)
    activation = (jax.nn.silu(gate_values) * up_values).astype(jnp.bfloat16)
    activation = lax.all_to_all(
        jnp.broadcast_to(activation[None], (QUARTER,) + activation.shape),
        "tensor",
        split_axis=0,
        concat_axis=0,
        tiled=True,
        axis_index_groups=SPREAD,
    )
    activation = jnp.transpose(activation, (1, 0, 2)).reshape(rows, hidden_units)
    activation_own = lax.dynamic_slice_in_dim(activation, core * half_units, half_units, 1)
    activation_other = lax.dynamic_slice_in_dim(activation, (1 - core) * half_units, half_units, 1)
    expert_out = jnp.einsum(
        "rk,ckn->crn", activation_own, down_own, preferred_element_type=jnp.float32
    ) + jnp.einsum(
        "rk,ckn->crn", activation_other, down_other, preferred_element_type=jnp.float32
    )
    together = [
        [
            (QUARTER * far + near) * expert_count + place
            for near in range(QUARTER)
            for place in range(expert_count)
        ]
        for far in range(tensor_count // QUARTER)
    ]
    returned = lax.all_to_all(
        expert_out.astype(jnp.bfloat16).reshape(QUARTER * expert_count, part, columns),
        ("tensor", "expert"),
        split_axis=0,
        concat_axis=0,
        tiled=True,
        axis_index_groups=together,
    ).reshape(slot_count, columns)
    place = (slot_index // part * expert_count + flat_routes) * part + slot_index % part
    picking = (place[:, None] == slot_place[None, :]).astype(jnp.bfloat16)
    picked = jnp.dot(picking, returned, preferred_element_type=jnp.float32)
    picked = picked.reshape(tokens, TOP, columns)
    mixed = jnp.sum(picked * route_weight[:, :, None], axis=1)
    return (hidden_share + mixed).astype(jnp.bfloat16)


def solution(mesh):
    return jax.shard_map(
        local,
        mesh=mesh,
        in_specs=(
            P(("dp", "expert"), "tensor"),
            P(("dp", "expert"), None),
            P(("dp", "expert"), None),
            P("tensor", "expert"),
            P(("dp", "expert"), None),
            P(),
            P(("dp", "expert"), None),
            P(("dp", "expert"), None),
            P("expert", None, "tensor"),
            P("expert", None, "tensor"),
            P("expert", None, "tensor"),
        ),
        out_specs=P(("dp", "expert"), "tensor"),
        check_vma=False,
    )
```

```python
import jax
import jax.numpy as jnp
from jax import lax
from jax.experimental import pallas as pl
from jax.experimental.pallas import tpu as pltpu
from jax.sharding import PartitionSpec as P

D = 4096
QUERY_HEADS = 64
KEY_VALUE_HEADS = 4
HEAD_WIDTH = 128
TOP = 2
QUARTER = 4
CLOSE = [[QUARTER * i + j for j in range(QUARTER)] for i in range(QUARTER)]
SPREAD = [[QUARTER * j + i for j in range(QUARTER)] for i in range(QUARTER)]
SWAP = [(0, 1), (1, 0)]
CHUNK = 512
UNIT = 96


def route_slots(routes, experts_count, capacity):
    flat_routes = routes.reshape(-1)
    onehot = (
        flat_routes[:, None] == jnp.arange(experts_count, dtype=jnp.int32)[None, :]
    ).astype(jnp.bfloat16)
    order = jnp.arange(flat_routes.shape[0], dtype=jnp.int32)
    before = (order[:, None] > order[None, :]).astype(jnp.bfloat16)
    ranking = jnp.dot(before, onehot, preferred_element_type=jnp.float32)
    slot_index = jnp.sum(ranking * onehot.astype(jnp.float32), axis=1).astype(jnp.int32)
    return flat_routes, slot_index


CONTRACT_LAST = (((1,), (1,)), ((), ()))


def attend(place_ref, query_ref, piece_ref, out_ref, score_ref):
    tokens = query_ref.shape[0]
    heads = query_ref.shape[1] // HEAD_WIDTH
    rows = heads * tokens
    blocks = CHUNK // tokens
    place = place_ref[0]
    stacked = jnp.concatenate(
        [query_ref[:, HEAD_WIDTH * h : HEAD_WIDTH * (h + 1)] for h in range(heads)], axis=0
    )
    token = place * tokens + lax.broadcasted_iota(jnp.int32, (rows, CHUNK), 0) % tokens
    offset = token - lax.broadcasted_iota(jnp.int32, (rows, CHUNK), 1)

    def score(step, row_max):
        keys = piece_ref[pl.ds(step * blocks, blocks), :, :HEAD_WIDTH].reshape(CHUNK, HEAD_WIDTH)
        scores = lax.dot_general(
            stacked, keys, CONTRACT_LAST, preferred_element_type=jnp.float32
        ) * HEAD_WIDTH ** (-0.5)
        masked = jnp.where(offset >= step * CHUNK, scores, -1e30)
        score_ref[step] = masked
        return jnp.maximum(row_max, jnp.max(masked, axis=1, keepdims=True))

    def weigh(step, carry):
        total, summed = carry
        exponent = jnp.exp(score_ref[step] - row_max)
        values = piece_ref[pl.ds(step * blocks, blocks), :, HEAD_WIDTH:].reshape(CHUNK, HEAD_WIDTH)
        return (
            total + jnp.sum(exponent, axis=1, keepdims=True),
            summed
            + jnp.dot(exponent.astype(jnp.bfloat16), values, preferred_element_type=jnp.float32),
        )

    steps = place // blocks + 1
    row_max = lax.fori_loop(0, steps, score, jnp.full((rows, 1), -1e30, jnp.float32))
    total, summed = lax.fori_loop(
        0,
        steps,
        weigh,
        (jnp.zeros((rows, 1), jnp.float32), jnp.zeros((rows, HEAD_WIDTH), jnp.float32)),
    )
    attended = (summed / total).astype(out_ref.dtype)
    halves = heads // 2
    for h in range(heads):
        out_ref[h // halves, :, HEAD_WIDTH * (h % halves) : HEAD_WIDTH * (h % halves + 1)] = (
            attended[tokens * h : tokens * (h + 1)]
        )


def project(core_ref, attended_ref, own_ref, other_ref, out_ref):
    core = core_ref[0]
    for block in range(own_ref.shape[0]):
        out_ref[block] = (
            jnp.dot(attended_ref[core], own_ref[block], preferred_element_type=jnp.float32)
            + jnp.dot(attended_ref[1 - core], other_ref[block], preferred_element_type=jnp.float32)
        ).astype(out_ref.dtype)


def gate_up(core_ref, rows_ref, gain_ref, own_ref, other_ref, out_ref, square, first, second):
    step = pl.program_id(0)
    units = own_ref.shape[0] * own_ref.shape[2]
    width = own_ref.shape[3]

    @pl.when(step == 0)
    def _():
        square[...] = jnp.zeros_like(square)
        first[...] = jnp.zeros_like(first)
        second[...] = jnp.zeros_like(second)

    rows = rows_ref[0].astype(jnp.float32)
    square[...] += jnp.sum(rows * rows, axis=1, keepdims=True)
    scaled = (rows * gain_ref[0]).astype(jnp.bfloat16)
    first[...] += lax.dot_general(
        scaled,
        own_ref[...].reshape(units, width),
        CONTRACT_LAST,
        preferred_element_type=jnp.float32,
    )
    second[...] += lax.dot_general(
        scaled,
        other_ref[...].reshape(units, width),
        CONTRACT_LAST,
        preferred_element_type=jnp.float32,
    )

    @pl.when(step == pl.num_programs(0) - 1)
    def _():
        scale = lax.rsqrt(square[...] / D + 1e-06)
        own, other = first[...] * scale, second[...] * scale
        gates_here = core_ref[0] == 0
        gate_values = jnp.where(gates_here, own, other)
        up_values = jnp.where(gates_here, other, own)
        silu = gate_values / (1.0 + jnp.exp(-gate_values))
        out_ref[...] = (silu * up_values).astype(out_ref.dtype)


def down(core_ref, activation_ref, own_ref, other_ref, out_ref):
    core = core_ref[0]
    width = own_ref.shape[3]
    units = activation_ref.shape[2]
    own = own_ref[0].reshape(2, units, width)
    other = other_ref[0].reshape(2, units, width)
    total = jnp.zeros(out_ref.shape[1:], jnp.float32)
    for part in range(2):
        total += jnp.dot(
            activation_ref[2 * core + part], own[part], preferred_element_type=jnp.float32
        )
        total += jnp.dot(
            activation_ref[2 * (1 - core) + part], other[part], preferred_element_type=jnp.float32
        )
    out_ref[0] = total.astype(out_ref.dtype)


SCALAR = pl.BlockSpec(memory_space=pltpu.SMEM)
LIMIT = pltpu.CompilerParams(vmem_limit_bytes=32 * 1024 * 1024)


def exchange(message, axis, groups=None):
    return lax.all_to_all(
        message, axis, split_axis=0, concat_axis=0, tiled=True, axis_index_groups=groups
    )


def local(
    queries,
    all_key_rows,
    all_value_rows,
    out_weight,
    residual,
    post_gain,
    routes,
    route_weight,
    gate_weight,
    up_weight,
    down_weight,
):
    tokens = queries.shape[0]
    local_heads = queries.shape[1] // HEAD_WIDTH
    group_width = QUERY_HEADS // KEY_VALUE_HEADS
    tensor_count = lax.axis_size("tensor")
    expert_count = lax.axis_size("expert")
    tensor_index = lax.axis_index("tensor")
    expert_index = lax.axis_index("expert")
    core = lax.axis_index("dp")
    columns = D // tensor_count
    capacity = 2 * tokens * TOP // expert_count
    slot_count = expert_count * capacity
    part = capacity // QUARTER
    rows = expert_count * part

    core_scalar = core.astype(jnp.int32).reshape(1)
    hidden_units = down_weight.shape[1]
    half_units = hidden_units // 2
    local_units = gate_weight.shape[2]
    first_blocks = D // columns
    blocks = first_blocks + half_units // local_units

    gate_or_up = jnp.where(core == 0, gate_weight[0], up_weight[0]).T
    gate_or_up = jnp.transpose(gate_or_up.reshape(local_units, first_blocks, columns), (1, 0, 2))
    down_half = lax.dynamic_slice_in_dim(down_weight[0], core * half_units, half_units, 0)
    weights_here = jnp.concatenate(
        [gate_or_up.reshape(D // columns * local_units, columns), down_half], axis=0
    )

    shared = tensor_index * local_heads // group_width
    key_head = lax.dynamic_slice_in_dim(all_key_rows, shared * HEAD_WIDTH, HEAD_WIDTH, 1)
    value_head = lax.dynamic_slice_in_dim(all_value_rows, shared * HEAD_WIDTH, HEAD_WIDTH, 1)
    half_rows = out_weight.shape[0] // 2
    weight_half = lax.dynamic_slice_in_dim(out_weight, core * half_rows, half_rows, 0)
    message = jnp.concatenate([weight_half, jnp.concatenate([key_head, value_head], axis=1)], axis=0)
    message, weights_here = lax.optimization_barrier((message, weights_here))
    weights_own = lax.all_gather(weights_here, "tensor", axis=0, axis_index_groups=CLOSE)
    gathered = exchange(jnp.broadcast_to(message[None], (expert_count,) + message.shape), "expert")
    weight_own = gathered[:, :half_rows, :]
    weight_other = lax.ppermute(weight_own, "dp", SWAP)

    attended = pl.pallas_call(
        attend,
        out_shape=jax.ShapeDtypeStruct((2, tokens, half_rows), jnp.bfloat16),
        grid=(1,),
        in_specs=[
            SCALAR,
            pl.BlockSpec((tokens, local_heads * HEAD_WIDTH), lambda i: (0, 0)),
            pl.BlockSpec(
                (expert_count, tokens, 2 * HEAD_WIDTH), lambda i: (0, half_rows // tokens, 0)
            ),
        ],
        out_specs=pl.BlockSpec((2, tokens, half_rows), lambda i: (0, 0, 0)),
        scratch_shapes=[
            pltpu.VMEM((expert_count * tokens // CHUNK, local_heads * tokens, CHUNK), jnp.float32)
        ],
        compiler_params=LIMIT,
        name="attend",
    )(expert_index.astype(jnp.int32).reshape(1), queries, gathered)

    wide = 4
    partial_value = pl.pallas_call(
        project,
        out_shape=jax.ShapeDtypeStruct((tensor_count, tokens, columns), jnp.bfloat16),
        grid=(tensor_count // wide,),
        in_specs=[
            SCALAR,
            pl.BlockSpec((2, tokens, half_rows), lambda i: (0, 0, 0)),
            pl.BlockSpec((wide, half_rows, columns), lambda i: (i, 0, 0)),
            pl.BlockSpec((wide, half_rows, columns), lambda i: (i, 0, 0)),
        ],
        out_specs=pl.BlockSpec((wide, tokens, columns), lambda i: (i, 0, 0)),
        compiler_params=LIMIT,
        name="project",
    )(core_scalar, attended, gathered, weight_other)
    partial_value, weights_own = lax.optimization_barrier((partial_value, weights_own))
    partial_sums = exchange(partial_value, "tensor")
    weights_other = lax.ppermute(weights_own, "dp", SWAP)
    shape = (QUARTER, blocks, local_units, columns)
    weights_own, weights_other = weights_own.reshape(shape), weights_other.reshape(shape)
    head_total = jnp.sum(partial_sums.astype(jnp.float32), axis=0)
    residual_share = lax.dynamic_slice_in_dim(residual, tensor_index * columns, columns, 1)
    hidden_share = residual_share.astype(jnp.float32) + head_total

    flat_routes, slot_index = route_slots(routes, expert_count, capacity)
    target = flat_routes * capacity + slot_index
    slot_place = jnp.arange(slot_count, dtype=jnp.int32)
    packing = jnp.any(
        target.reshape(tokens, TOP)[None, :, :] == slot_place[:, None, None], axis=2
    ).astype(jnp.bfloat16)
    packed = jnp.dot(
        packing, hidden_share.astype(jnp.bfloat16), preferred_element_type=jnp.float32
    ).astype(jnp.bfloat16)
    arrived = exchange(packed.reshape(expert_count, capacity, columns), "expert")
    quarters = jnp.transpose(
        arrived.reshape(expert_count, QUARTER, part, columns), (1, 0, 2, 3)
    ).reshape(1, QUARTER, rows, columns)
    quarters = jnp.broadcast_to(quarters, (tensor_count // QUARTER, QUARTER, rows, columns))
    full_rows = exchange(quarters.reshape(tensor_count, rows, columns), "tensor")

    weight_spec = pl.BlockSpec((QUARTER, 1, local_units, columns), lambda i: (0, i, 0, 0))
    activation = pl.pallas_call(
        gate_up,
        out_shape=jax.ShapeDtypeStruct((rows, QUARTER * local_units), jnp.bfloat16),
        grid=(first_blocks,),
        in_specs=[
            SCALAR,
            pl.BlockSpec((1, rows, columns), lambda i: (i, 0, 0)),
            pl.BlockSpec((1, 1, columns), lambda i: (i, 0, 0)),
            weight_spec,
            weight_spec,
        ],
        out_specs=pl.BlockSpec((rows, QUARTER * local_units), lambda i: (0, 0)),
        scratch_shapes=[
            pltpu.VMEM((rows, 1), jnp.float32),
            pltpu.VMEM((rows, QUARTER * local_units), jnp.float32),
            pltpu.VMEM((rows, QUARTER * local_units), jnp.float32),
        ],
        compiler_params=LIMIT,
        name="gate_up",
    )(core_scalar, full_rows, post_gain.reshape(first_blocks, 1, columns), weights_own, weights_other)
    activation = exchange(
        jnp.broadcast_to(activation[None], (QUARTER,) + activation.shape), "tensor", SPREAD
    )
    down_blocks = half_units // local_units
    weight_spec = pl.BlockSpec(
        (1, down_blocks, local_units, columns), lambda i: (i, first_blocks // down_blocks, 0, 0)
    )
    expert_out = pl.pallas_call(
        down,
        out_shape=jax.ShapeDtypeStruct((QUARTER, rows, columns), jnp.bfloat16),
        grid=(QUARTER,),
        in_specs=[
            SCALAR,
            pl.BlockSpec((QUARTER, rows, QUARTER * local_units), lambda i: (0, 0, 0)),
            weight_spec,
            weight_spec,
        ],
        out_specs=pl.BlockSpec((1, rows, columns), lambda i: (i, 0, 0)),
        compiler_params=LIMIT,
        name="down",
    )(core_scalar, activation, weights_own, weights_other)
    together = [
        [
            (QUARTER * far + near) * expert_count + place
            for near in range(QUARTER)
            for place in range(expert_count)
        ]
        for far in range(tensor_count // QUARTER)
    ]
    returned = exchange(
        expert_out.reshape(QUARTER * expert_count, part, columns), ("tensor", "expert"), together
    ).reshape(slot_count, columns)
    place = (slot_index // part * expert_count + flat_routes) * part + slot_index % part
    picking = (place[:, None] == slot_place[None, :]).astype(jnp.bfloat16)
    picked = jnp.dot(picking, returned, preferred_element_type=jnp.float32)
    picked = picked.reshape(tokens, TOP, columns)
    mixed = jnp.sum(picked * route_weight[:, :, None], axis=1)
    return (hidden_share + mixed).astype(jnp.bfloat16)


def solution(mesh):
    return jax.shard_map(
        local,
        mesh=mesh,
        in_specs=(
            P(("dp", "expert"), "tensor"),
            P(("dp", "expert"), None),
            P(("dp", "expert"), None),
            P("tensor", "expert"),
            P(("dp", "expert"), None),
            P(),
            P(("dp", "expert"), None),
            P(("dp", "expert"), None),
            P("expert", None, "tensor"),
            P("expert", None, "tensor"),
            P("expert", None, "tensor"),
        ),
        out_specs=P(("dp", "expert"), "tensor"),
        check_vma=False,
    )
```

```python
import jax
import jax.numpy as jnp
from jax import lax
from jax.experimental import pallas as pl
from jax.experimental.pallas import tpu as pltpu
from jax.sharding import PartitionSpec as P

D = 4096
QUERY_HEADS = 64
KEY_VALUE_HEADS = 4
HEAD_WIDTH = 128
TOP = 2
SWAP = [(0, 1), (1, 0)]
CHUNK = 512


CONTRACT_LAST = (((1,), (1,)), ((), ()))


def attend(place_ref, query_ref, piece_ref, out_ref, score_ref):
    tokens = query_ref.shape[0]
    heads = query_ref.shape[1] // HEAD_WIDTH
    rows = heads * tokens
    blocks = CHUNK // tokens
    place = place_ref[0]
    stacked = jnp.concatenate(
        [query_ref[:, HEAD_WIDTH * h : HEAD_WIDTH * (h + 1)] for h in range(heads)], axis=0
    )
    token = place * tokens + lax.broadcasted_iota(jnp.int32, (rows, CHUNK), 0) % tokens
    offset = token - lax.broadcasted_iota(jnp.int32, (rows, CHUNK), 1)

    def score(step, row_max):
        keys = piece_ref[pl.ds(step * blocks, blocks), :, :HEAD_WIDTH].reshape(CHUNK, HEAD_WIDTH)
        scores = lax.dot_general(
            stacked, keys, CONTRACT_LAST, preferred_element_type=jnp.float32
        ) * HEAD_WIDTH ** (-0.5)
        masked = jnp.where(offset >= step * CHUNK, scores, -1e30)
        score_ref[step] = masked
        return jnp.maximum(row_max, jnp.max(masked, axis=1, keepdims=True))

    def weigh(step, carry):
        total, summed = carry
        exponent = jnp.exp(score_ref[step] - row_max)
        values = piece_ref[pl.ds(step * blocks, blocks), :, HEAD_WIDTH:].reshape(CHUNK, HEAD_WIDTH)
        return (
            total + jnp.sum(exponent, axis=1, keepdims=True),
            summed
            + jnp.dot(exponent.astype(jnp.bfloat16), values, preferred_element_type=jnp.float32),
        )

    steps = place // blocks + 1
    row_max = lax.fori_loop(0, steps, score, jnp.full((rows, 1), -1e30, jnp.float32))
    total, summed = lax.fori_loop(
        0,
        steps,
        weigh,
        (jnp.zeros((rows, 1), jnp.float32), jnp.zeros((rows, HEAD_WIDTH), jnp.float32)),
    )
    attended = (summed / total).astype(out_ref.dtype)
    halves = heads // 2
    for h in range(heads):
        out_ref[h // halves, :, HEAD_WIDTH * (h % halves) : HEAD_WIDTH * (h % halves + 1)] = (
            attended[tokens * h : tokens * (h + 1)]
        )


def project(core_ref, attended_ref, own_ref, other_ref, out_ref):
    core = core_ref[0]
    for block in range(own_ref.shape[0]):
        out_ref[block] = (
            jnp.dot(attended_ref[core], own_ref[block], preferred_element_type=jnp.float32)
            + jnp.dot(attended_ref[1 - core], other_ref[block], preferred_element_type=jnp.float32)
        ).astype(out_ref.dtype)


def gate_up(
    core_ref, rows_ref, gain_ref, routes_ref, own_ref, other_ref, out_ref, normed, first, second
):
    step = pl.program_id(0)
    experts, units, depth = own_ref.shape
    pieces, tokens, columns = rows_ref.shape
    per_step = depth // columns

    @pl.when(step == 0)
    def _():
        square = jnp.zeros((tokens, 1), jnp.float32)
        for piece in range(pieces):
            rows = rows_ref[piece].astype(jnp.float32)
            square += jnp.sum(rows * rows, axis=1, keepdims=True)
        scale = lax.rsqrt(square / D + 1e-06)
        for piece in range(pieces):
            start = piece % per_step * columns
            normed[piece // per_step, :, start : start + columns] = (
                rows_ref[piece].astype(jnp.float32) * scale * gain_ref[piece]
            ).astype(jnp.bfloat16)
        first[...] = jnp.zeros_like(first)
        second[...] = jnp.zeros_like(second)

    rows = normed[step]
    first[...] += lax.dot_general(
        own_ref[...].reshape(experts * units, depth),
        rows,
        CONTRACT_LAST,
        preferred_element_type=jnp.float32,
    )
    second[...] += lax.dot_general(
        other_ref[...].reshape(experts * units, depth),
        rows,
        CONTRACT_LAST,
        preferred_element_type=jnp.float32,
    )

    @pl.when(step == pl.num_programs(0) - 1)
    def _():
        gates_here = core_ref[0] == 0
        chosen = [jnp.zeros((units, tokens), jnp.float32) for _ in range(TOP)]
        for expert in range(experts):
            own = first[expert * units : (expert + 1) * units]
            other = second[expert * units : (expert + 1) * units]
            gate_values = jnp.where(gates_here, own, other)
            up_values = jnp.where(gates_here, other, own)
            activation = gate_values / (1.0 + jnp.exp(-gate_values)) * up_values
            for k in range(TOP):
                chosen[k] = jnp.where(routes_ref[k : k + 1] == expert, activation, chosen[k])
        for k in range(TOP):
            out_ref[k * units : (k + 1) * units] = chosen[k].astype(out_ref.dtype)


def down(
    core_ref,
    activation_ref,
    routes_ref,
    route_weight_ref,
    hidden_ref,
    own_ref,
    other_ref,
    out_ref,
    turned,
    mixed,
):
    step = pl.program_id(0)
    core = core_ref[0]
    per_step = own_ref.shape[0]
    pieces = activation_ref.shape[0] // 2
    units = activation_ref.shape[1] // TOP

    @pl.when(step == 0)
    def _():
        for half in range(2):
            for k in range(TOP):
                part = activation_ref[pieces * half : pieces * (half + 1), k * units : (k + 1) * units]
                part = part.reshape(pieces * units, part.shape[2]).astype(jnp.float32)
                turned[half, k] = jnp.transpose(part).astype(turned.dtype)
        mixed[...] = jnp.zeros_like(mixed)

    for place in range(per_step):
        expert = step * per_step + place
        here = [routes_ref[:, k : k + 1] == expert for k in range(TOP)]
        share = sum(jnp.where(here[k], route_weight_ref[:, k : k + 1], 0.0) for k in range(TOP))
        masks = [here[k].astype(jnp.bfloat16) for k in range(TOP)]
        total = jnp.zeros(mixed.shape, jnp.float32)
        for half, weight_ref in ((core, own_ref), (1 - core, other_ref)):
            rows = sum(turned[half, k] * masks[k] for k in range(TOP))
            total += jnp.dot(rows, weight_ref[place], preferred_element_type=jnp.float32)
        mixed[...] += total.astype(jnp.bfloat16).astype(jnp.float32) * share

    @pl.when(step == pl.num_programs(0) - 1)
    def _():
        out_ref[...] = (hidden_ref[...] + mixed[...]).astype(out_ref.dtype)


SCALAR = pl.BlockSpec(memory_space=pltpu.SMEM)
LIMIT = pltpu.CompilerParams(vmem_limit_bytes=40 * 1024 * 1024)


def exchange(message, axis):
    return lax.all_to_all(message, axis, split_axis=0, concat_axis=0, tiled=True)


def spread(rows, axis):
    return exchange(jnp.broadcast_to(rows[None], (lax.axis_size(axis),) + rows.shape), axis)


def local(
    queries,
    all_key_rows,
    all_value_rows,
    out_weight,
    residual,
    post_gain,
    routes,
    route_weight,
    gate_weight,
    up_weight,
    down_weight,
):
    tokens = queries.shape[0]
    local_heads = queries.shape[1] // HEAD_WIDTH
    group_width = QUERY_HEADS // KEY_VALUE_HEADS
    tensor_count = lax.axis_size("tensor")
    expert_count = lax.axis_size("expert")
    tensor_index = lax.axis_index("tensor")
    expert_index = lax.axis_index("expert")
    core = lax.axis_index("dp")
    columns = D // tensor_count
    core_scalar = core.astype(jnp.int32).reshape(1)
    hidden_units = down_weight.shape[1]
    half_units = hidden_units // 2
    local_units = gate_weight.shape[2]

    gate_or_up = jnp.where(core == 0, gate_weight[0], up_weight[0]).T
    down_half = lax.dynamic_slice_in_dim(down_weight[0], core * half_units, half_units, 0)

    shared = tensor_index * local_heads // group_width
    key_head = lax.dynamic_slice_in_dim(all_key_rows, shared * HEAD_WIDTH, HEAD_WIDTH, 1)
    value_head = lax.dynamic_slice_in_dim(all_value_rows, shared * HEAD_WIDTH, HEAD_WIDTH, 1)
    half_rows = out_weight.shape[0] // 2
    weight_half = lax.dynamic_slice_in_dim(out_weight, core * half_rows, half_rows, 0)
    message = jnp.concatenate([weight_half, jnp.concatenate([key_head, value_head], axis=1)], axis=0)
    message, gate_or_up, down_half = lax.optimization_barrier((message, gate_or_up, down_half))
    first_own = lax.all_gather(gate_or_up, "expert", axis=0)
    down_own = lax.all_gather(down_half, "expert", axis=0)
    gathered = spread(message, "expert")
    weight_own = gathered[:, :half_rows, :]
    weight_other = lax.ppermute(weight_own, "dp", SWAP)

    attended = pl.pallas_call(
        attend,
        out_shape=jax.ShapeDtypeStruct((2, tokens, half_rows), jnp.bfloat16),
        grid=(1,),
        in_specs=[
            SCALAR,
            pl.BlockSpec((tokens, local_heads * HEAD_WIDTH), lambda i: (0, 0)),
            pl.BlockSpec(
                (expert_count, tokens, 2 * HEAD_WIDTH), lambda i: (0, half_rows // tokens, 0)
            ),
        ],
        out_specs=pl.BlockSpec((2, tokens, half_rows), lambda i: (0, 0, 0)),
        scratch_shapes=[
            pltpu.VMEM((expert_count * tokens // CHUNK, local_heads * tokens, CHUNK), jnp.float32)
        ],
        compiler_params=LIMIT,
        name="attend",
    )(expert_index.astype(jnp.int32).reshape(1), queries, gathered)

    wide = 4
    partial_value = pl.pallas_call(
        project,
        out_shape=jax.ShapeDtypeStruct((tensor_count, tokens, columns), jnp.bfloat16),
        grid=(tensor_count // wide,),
        in_specs=[
            SCALAR,
            pl.BlockSpec((2, tokens, half_rows), lambda i: (0, 0, 0)),
            pl.BlockSpec((wide, half_rows, columns), lambda i: (i, 0, 0)),
            pl.BlockSpec((wide, half_rows, columns), lambda i: (i, 0, 0)),
        ],
        out_specs=pl.BlockSpec((wide, tokens, columns), lambda i: (i, 0, 0)),
        compiler_params=LIMIT,
        name="project",
    )(core_scalar, attended, gathered, weight_other)
    partial_sums = exchange(partial_value, "tensor")
    head_total = jnp.sum(partial_sums.astype(jnp.float32), axis=0)
    residual_share = lax.dynamic_slice_in_dim(residual, tensor_index * columns, columns, 1)
    hidden_share = residual_share.astype(jnp.float32) + head_total
    hidden_share, first_own = lax.optimization_barrier((hidden_share, first_own))
    full_rows = spread(hidden_share.astype(jnp.bfloat16), "tensor")

    first_other = lax.ppermute(first_own, "dp", SWAP)
    depth = 512
    steps = D // depth
    weight_spec = pl.BlockSpec((expert_count, local_units, depth), lambda i: (0, 0, i))
    activation = pl.pallas_call(
        gate_up,
        out_shape=jax.ShapeDtypeStruct((TOP * local_units, tokens), jnp.bfloat16),
        grid=(steps,),
        in_specs=[
            SCALAR,
            pl.BlockSpec((tensor_count, tokens, columns), lambda i: (0, 0, 0)),
            pl.BlockSpec((tensor_count, 1, columns), lambda i: (0, 0, 0)),
            pl.BlockSpec((TOP, tokens), lambda i: (0, 0)),
            weight_spec,
            weight_spec,
        ],
        out_specs=pl.BlockSpec((TOP * local_units, tokens), lambda i: (0, 0)),
        scratch_shapes=[
            pltpu.VMEM((steps, tokens, depth), jnp.bfloat16),
            pltpu.VMEM((expert_count * local_units, tokens), jnp.float32),
            pltpu.VMEM((expert_count * local_units, tokens), jnp.float32),
        ],
        compiler_params=LIMIT,
        name="gate_up",
    )(
        core_scalar,
        full_rows,
        post_gain.reshape(tensor_count, 1, columns),
        routes.T,
        first_own,
        first_other,
    )
    activation, down_own = lax.optimization_barrier((activation, down_own))
    activation = spread(activation, "tensor")

    down_other = lax.ppermute(down_own, "dp", SWAP)
    per_step = 2
    weight_spec = pl.BlockSpec((per_step, half_units, columns), lambda i: (i, 0, 0))
    return pl.pallas_call(
        down,
        out_shape=jax.ShapeDtypeStruct((tokens, columns), jnp.bfloat16),
        grid=(expert_count // per_step,),
        in_specs=[
            SCALAR,
            pl.BlockSpec((tensor_count, TOP * local_units, tokens), lambda i: (0, 0, 0)),
            pl.BlockSpec((tokens, TOP), lambda i: (0, 0)),
            pl.BlockSpec((tokens, TOP), lambda i: (0, 0)),
            pl.BlockSpec((tokens, columns), lambda i: (0, 0)),
            weight_spec,
            weight_spec,
        ],
        out_specs=pl.BlockSpec((tokens, columns), lambda i: (0, 0)),
        scratch_shapes=[
            pltpu.VMEM((2, TOP, tokens, half_units), jnp.bfloat16),
            pltpu.VMEM((tokens, columns), jnp.float32),
        ],
        compiler_params=LIMIT,
        name="down",
    )(core_scalar, activation, routes, route_weight, hidden_share, down_own, down_other)


def solution(mesh):
    return jax.shard_map(
        local,
        mesh=mesh,
        in_specs=(
            P(("dp", "expert"), "tensor"),
            P(("dp", "expert"), None),
            P(("dp", "expert"), None),
            P("tensor", "expert"),
            P(("dp", "expert"), None),
            P(),
            P(("dp", "expert"), None),
            P(("dp", "expert"), None),
            P("expert", None, "tensor"),
            P("expert", None, "tensor"),
            P("expert", None, "tensor"),
        ),
        out_specs=P(("dp", "expert"), "tensor"),
        check_vma=False,
    )
```

```python
import jax
import jax.numpy as jnp
from jax import lax
from jax.experimental import pallas as pl
from jax.experimental.pallas import tpu as pltpu
from jax.sharding import PartitionSpec as P

D = 4096
QUERY_HEADS = 64
KEY_VALUE_HEADS = 4
HEAD_WIDTH = 128
TOP = 2
SWAP = [(0, 1), (1, 0)]
CHUNK = 512


CONTRACT_LAST = (((1,), (1,)), ((), ()))


def attend(place_ref, query_ref, piece_ref, out_ref, score_ref):
    tokens = query_ref.shape[0]
    heads = query_ref.shape[1] // HEAD_WIDTH
    rows = heads * tokens
    blocks = CHUNK // tokens
    place = place_ref[0]
    stacked = jnp.concatenate(
        [query_ref[:, HEAD_WIDTH * h : HEAD_WIDTH * (h + 1)] for h in range(heads)], axis=0
    )
    token = place * tokens + lax.broadcasted_iota(jnp.int32, (rows, CHUNK), 0) % tokens
    offset = token - lax.broadcasted_iota(jnp.int32, (rows, CHUNK), 1)

    def score(step, row_max):
        keys = piece_ref[pl.ds(step * blocks, blocks), :, :HEAD_WIDTH].reshape(CHUNK, HEAD_WIDTH)
        scores = lax.dot_general(
            stacked, keys, CONTRACT_LAST, preferred_element_type=jnp.float32
        ) * HEAD_WIDTH ** (-0.5)
        masked = jnp.where(offset >= step * CHUNK, scores, -1e30)
        score_ref[step] = masked
        return jnp.maximum(row_max, jnp.max(masked, axis=1, keepdims=True))

    def weigh(step, carry):
        total, summed = carry
        exponent = jnp.exp(score_ref[step] - row_max)
        values = piece_ref[pl.ds(step * blocks, blocks), :, HEAD_WIDTH:].reshape(CHUNK, HEAD_WIDTH)
        return (
            total + jnp.sum(exponent, axis=1, keepdims=True),
            summed
            + jnp.dot(exponent.astype(jnp.bfloat16), values, preferred_element_type=jnp.float32),
        )

    steps = place // blocks + 1
    row_max = lax.fori_loop(0, steps, score, jnp.full((rows, 1), -1e30, jnp.float32))
    total, summed = lax.fori_loop(
        0,
        steps,
        weigh,
        (jnp.zeros((rows, 1), jnp.float32), jnp.zeros((rows, HEAD_WIDTH), jnp.float32)),
    )
    attended = (summed / total).astype(out_ref.dtype)
    halves = heads // 2
    for h in range(heads):
        out_ref[h // halves, :, HEAD_WIDTH * (h % halves) : HEAD_WIDTH * (h % halves + 1)] = (
            attended[tokens * h : tokens * (h + 1)]
        )


def project(core_ref, attended_ref, own_ref, other_ref, out_ref):
    core = core_ref[0]
    for block in range(own_ref.shape[0]):
        out_ref[block] = (
            jnp.dot(attended_ref[core], own_ref[block], preferred_element_type=jnp.float32)
            + jnp.dot(attended_ref[1 - core], other_ref[block], preferred_element_type=jnp.float32)
        ).astype(out_ref.dtype)


def gate_up(rows_ref, gain_ref, routes_ref, *refs):
    parts = (len(refs) - 4) // 2
    gate_refs, up_refs = refs[:parts], refs[parts : 2 * parts]
    out_ref, normed, first, second = refs[2 * parts :]
    step = pl.program_id(0)
    experts, per_step, units, columns = gate_refs[0].shape
    pieces, tokens, _ = rows_ref.shape

    @pl.when(step == 0)
    def _():
        square = jnp.zeros((tokens, 1), jnp.float32)
        for piece in range(pieces):
            rows = rows_ref[piece].astype(jnp.float32)
            square += jnp.sum(rows * rows, axis=1, keepdims=True)
        scale = lax.rsqrt(square / D + 1e-06)
        for piece in range(pieces):
            normed[piece] = (
                rows_ref[piece].astype(jnp.float32) * scale * gain_ref[piece]
            ).astype(jnp.bfloat16)
        first[...] = jnp.zeros_like(first)
        second[...] = jnp.zeros_like(second)

    for weight_refs, total in ((gate_refs, first), (up_refs, second)):
        for part, weight_ref in enumerate(weight_refs):
            place = pl.ds(part * experts * units, experts * units)
            product = total[place]
            for piece in range(per_step):
                product += lax.dot_general(
                    weight_ref[:, piece].reshape(experts * units, columns),
                    normed[step * per_step + piece],
                    CONTRACT_LAST,
                    preferred_element_type=jnp.float32,
                )
            total[place] = product

    @pl.when(step == pl.num_programs(0) - 1)
    def _():
        chosen = [jnp.zeros((units, tokens), jnp.float32) for _ in range(TOP)]
        for expert in range(parts * experts):
            gate_values = first[expert * units : (expert + 1) * units]
            up_values = second[expert * units : (expert + 1) * units]
            activation = gate_values / (1.0 + jnp.exp(-gate_values)) * up_values
            for k in range(TOP):
                chosen[k] = jnp.where(routes_ref[k : k + 1] == expert, activation, chosen[k])
        for k in range(TOP):
            out_ref[k * units : (k + 1) * units] = chosen[k].astype(out_ref.dtype)


def down(activation_ref, routes_ref, route_weight_ref, hidden_ref, *refs):
    parts = (len(refs) - 3) // 2
    half_refs = refs[:parts], refs[parts : 2 * parts]
    out_ref, turned, mixed = refs[2 * parts :]
    step = pl.program_id(0)
    per_part, blocks, units, columns = refs[0].shape

    @pl.when(step == 0)
    def _():
        for half in range(2):
            for k in range(TOP):
                part = activation_ref[blocks * half : blocks * (half + 1), k * units : (k + 1) * units]
                part = part.reshape(blocks * units, part.shape[2]).astype(jnp.float32)
                turned[half, k] = jnp.transpose(part).astype(turned.dtype)
        mixed[...] = jnp.zeros_like(mixed)

    for part in range(parts):
        for place in range(per_part):
            expert = (step * parts + part) * per_part + place
            here = [routes_ref[:, k : k + 1] == expert for k in range(TOP)]
            share = sum(jnp.where(here[k], route_weight_ref[:, k : k + 1], 0.0) for k in range(TOP))
            masks = [here[k].astype(jnp.bfloat16) for k in range(TOP)]
            total = jnp.zeros(mixed.shape, jnp.float32)
            for half in range(2):
                rows = sum(turned[half, k] * masks[k] for k in range(TOP))
                weight = half_refs[half][part][place].reshape(blocks * units, columns)
                total += jnp.dot(rows, weight, preferred_element_type=jnp.float32)
            mixed[...] += total.astype(jnp.bfloat16).astype(jnp.float32) * share

    @pl.when(step == pl.num_programs(0) - 1)
    def _():
        out_ref[...] = (hidden_ref[...] + mixed[...]).astype(out_ref.dtype)


SCALAR = pl.BlockSpec(memory_space=pltpu.SMEM)
LIMIT = pltpu.CompilerParams(vmem_limit_bytes=32 * 1024 * 1024)
WIDE = pltpu.CompilerParams(vmem_limit_bytes=56 * 1024 * 1024)


def exchange(message, axis):
    return lax.all_to_all(message, axis, split_axis=0, concat_axis=0, tiled=True)


def spread(rows, axis):
    return exchange(jnp.broadcast_to(rows[None], (lax.axis_size(axis),) + rows.shape), axis)


def local(
    queries,
    all_key_rows,
    all_value_rows,
    out_weight,
    residual,
    post_gain,
    routes,
    route_weight,
    gate_weight,
    up_weight,
    down_weight,
):
    tokens = queries.shape[0]
    local_heads = queries.shape[1] // HEAD_WIDTH
    group_width = QUERY_HEADS // KEY_VALUE_HEADS
    tensor_count = lax.axis_size("tensor")
    expert_count = lax.axis_size("expert")
    tensor_index = lax.axis_index("tensor")
    expert_index = lax.axis_index("expert")
    core = lax.axis_index("dp")
    columns = D // tensor_count
    core_scalar = core.astype(jnp.int32).reshape(1)
    hidden_units = down_weight.shape[1]
    half_units = hidden_units // 2
    local_units = gate_weight.shape[2]

    first_blocks = D // columns
    down_blocks = half_units // local_units
    blocks = first_blocks + down_blocks

    gate_or_up = jnp.where(core == 0, gate_weight[0], up_weight[0]).T
    gate_or_up = jnp.transpose(gate_or_up.reshape(local_units, first_blocks, columns), (1, 0, 2))
    down_half = lax.dynamic_slice_in_dim(down_weight[0], core * half_units, half_units, 0)
    weights_here = jnp.concatenate(
        [gate_or_up.reshape(first_blocks * local_units, columns), down_half], axis=0
    )

    shared = tensor_index * local_heads // group_width
    key_head = lax.dynamic_slice_in_dim(all_key_rows, shared * HEAD_WIDTH, HEAD_WIDTH, 1)
    value_head = lax.dynamic_slice_in_dim(all_value_rows, shared * HEAD_WIDTH, HEAD_WIDTH, 1)
    half_rows = out_weight.shape[0] // 2
    weight_half = lax.dynamic_slice_in_dim(out_weight, core * half_rows, half_rows, 0)
    message = jnp.concatenate([weight_half, jnp.concatenate([key_head, value_head], axis=1)], axis=0)
    message, weights_here = lax.optimization_barrier((message, weights_here))
    weights = lax.all_gather(weights_here, ("dp", "expert"), axis=0)
    gathered = spread(message, "expert")
    weight_own = gathered[:, :half_rows, :]
    weight_other = lax.ppermute(weight_own, "dp", SWAP)

    attended = pl.pallas_call(
        attend,
        out_shape=jax.ShapeDtypeStruct((2, tokens, half_rows), jnp.bfloat16),
        grid=(1,),
        in_specs=[
            SCALAR,
            pl.BlockSpec((tokens, local_heads * HEAD_WIDTH), lambda i: (0, 0)),
            pl.BlockSpec(
                (expert_count, tokens, 2 * HEAD_WIDTH), lambda i: (0, half_rows // tokens, 0)
            ),
        ],
        out_specs=pl.BlockSpec((2, tokens, half_rows), lambda i: (0, 0, 0)),
        scratch_shapes=[
            pltpu.VMEM((expert_count * tokens // CHUNK, local_heads * tokens, CHUNK), jnp.float32)
        ],
        compiler_params=WIDE,
        name="attend",
    )(expert_index.astype(jnp.int32).reshape(1), queries, gathered)

    wide = 4
    partial_value = pl.pallas_call(
        project,
        out_shape=jax.ShapeDtypeStruct((tensor_count, tokens, columns), jnp.bfloat16),
        grid=(tensor_count // wide,),
        in_specs=[
            SCALAR,
            pl.BlockSpec((2, tokens, half_rows), lambda i: (0, 0, 0)),
            pl.BlockSpec((wide, half_rows, columns), lambda i: (i, 0, 0)),
            pl.BlockSpec((wide, half_rows, columns), lambda i: (i, 0, 0)),
        ],
        out_specs=pl.BlockSpec((wide, tokens, columns), lambda i: (i, 0, 0)),
        compiler_params=WIDE,
        name="project",
    )(core_scalar, attended, gathered, weight_other)
    partial_sums = exchange(partial_value, "tensor")
    head_total = jnp.sum(partial_sums.astype(jnp.float32), axis=0)
    residual_share = lax.dynamic_slice_in_dim(residual, tensor_index * columns, columns, 1)
    hidden_share = residual_share.astype(jnp.float32) + head_total
    full_rows = spread(hidden_share.astype(jnp.bfloat16), "tensor")
    full_rows, weights = lax.optimization_barrier((full_rows, weights))
    weights = weights.reshape(2 * expert_count, blocks, local_units, columns)

    parts = 2
    per_part = expert_count // parts
    per_step = 2

    def first_spec(place):
        return pl.BlockSpec((per_part, per_step, local_units, columns), lambda i: (place, i, 0, 0))

    activation = pl.pallas_call(
        gate_up,
        out_shape=jax.ShapeDtypeStruct((TOP * local_units, tokens), jnp.bfloat16),
        grid=(first_blocks // per_step,),
        in_specs=[
            pl.BlockSpec((tensor_count, tokens, columns), lambda i: (0, 0, 0)),
            pl.BlockSpec((tensor_count, 1, columns), lambda i: (0, 0, 0)),
            pl.BlockSpec((TOP, tokens), lambda i: (0, 0)),
        ]
        + [first_spec(place) for place in range(2 * parts)],
        out_specs=pl.BlockSpec((TOP * local_units, tokens), lambda i: (0, 0)),
        scratch_shapes=[
            pltpu.VMEM((first_blocks, tokens, columns), jnp.bfloat16),
            pltpu.VMEM((expert_count * local_units, tokens), jnp.float32),
            pltpu.VMEM((expert_count * local_units, tokens), jnp.float32),
        ],
        compiler_params=LIMIT,
        name="gate_up",
    )(
        full_rows,
        post_gain.reshape(tensor_count, 1, columns),
        routes.T,
        *[weights] * (2 * parts),
    )
    activation = spread(activation, "tensor")

    per_part = 2
    down_steps = expert_count // (parts * per_part)

    def down_spec(half, part):
        return pl.BlockSpec(
            (per_part, down_blocks, local_units, columns),
            lambda i: ((half * down_steps + i) * parts + part, first_blocks // down_blocks, 0, 0),
        )

    return pl.pallas_call(
        down,
        out_shape=jax.ShapeDtypeStruct((tokens, columns), jnp.bfloat16),
        grid=(down_steps,),
        in_specs=[
            pl.BlockSpec((tensor_count, TOP * local_units, tokens), lambda i: (0, 0, 0)),
            pl.BlockSpec((tokens, TOP), lambda i: (0, 0)),
            pl.BlockSpec((tokens, TOP), lambda i: (0, 0)),
            pl.BlockSpec((tokens, columns), lambda i: (0, 0)),
        ]
        + [down_spec(half, part) for half in range(2) for part in range(parts)],
        out_specs=pl.BlockSpec((tokens, columns), lambda i: (0, 0)),
        scratch_shapes=[
            pltpu.VMEM((2, TOP, tokens, half_units), jnp.bfloat16),
            pltpu.VMEM((tokens, columns), jnp.float32),
        ],
        compiler_params=LIMIT,
        name="down",
    )(activation, routes, route_weight, hidden_share, *[weights] * (2 * parts))


def solution(mesh):
    return jax.shard_map(
        local,
        mesh=mesh,
        in_specs=(
            P(("dp", "expert"), "tensor"),
            P(("dp", "expert"), None),
            P(("dp", "expert"), None),
            P("tensor", "expert"),
            P(("dp", "expert"), None),
            P(),
            P(("dp", "expert"), None),
            P(("dp", "expert"), None),
            P("expert", None, "tensor"),
            P("expert", None, "tensor"),
            P("expert", None, "tensor"),
        ),
        out_specs=P(("dp", "expert"), "tensor"),
        check_vma=False,
    )
```

```python
import jax
import jax.numpy as jnp
from jax import lax
from jax.experimental import pallas as pl
from jax.experimental.pallas import tpu as pltpu
from jax.sharding import PartitionSpec as P

D = 4096
QUERY_HEADS = 64
KEY_VALUE_HEADS = 4
HEAD_WIDTH = 128
TOP = 2
SWAP = [(0, 1), (1, 0)]
CHUNK = 512


CONTRACT_LAST = (((1,), (1,)), ((), ()))


def attend(place_ref, query_ref, piece_ref, out_ref, score_ref):
    tokens = query_ref.shape[0]
    heads = query_ref.shape[1] // HEAD_WIDTH
    rows = heads * tokens
    blocks = CHUNK // tokens
    place = place_ref[0]
    stacked = jnp.concatenate(
        [query_ref[:, HEAD_WIDTH * h : HEAD_WIDTH * (h + 1)] for h in range(heads)], axis=0
    )
    token = place * tokens + lax.broadcasted_iota(jnp.int32, (rows, CHUNK), 0) % tokens
    offset = token - lax.broadcasted_iota(jnp.int32, (rows, CHUNK), 1)

    def score(step, row_max):
        keys = piece_ref[pl.ds(step * blocks, blocks), :, :HEAD_WIDTH].reshape(CHUNK, HEAD_WIDTH)
        scores = lax.dot_general(
            stacked, keys, CONTRACT_LAST, preferred_element_type=jnp.float32
        ) * HEAD_WIDTH ** (-0.5)
        masked = jnp.where(offset >= step * CHUNK, scores, -1e30)
        score_ref[step] = masked
        return jnp.maximum(row_max, jnp.max(masked, axis=1, keepdims=True))

    def weigh(step, carry):
        total, summed = carry
        exponent = jnp.exp(score_ref[step] - row_max)
        values = piece_ref[pl.ds(step * blocks, blocks), :, HEAD_WIDTH:].reshape(CHUNK, HEAD_WIDTH)
        return (
            total + jnp.sum(exponent, axis=1, keepdims=True),
            summed
            + jnp.dot(exponent.astype(jnp.bfloat16), values, preferred_element_type=jnp.float32),
        )

    steps = place // blocks + 1
    row_max = lax.fori_loop(0, steps, score, jnp.full((rows, 1), -1e30, jnp.float32))
    total, summed = lax.fori_loop(
        0,
        steps,
        weigh,
        (jnp.zeros((rows, 1), jnp.float32), jnp.zeros((rows, HEAD_WIDTH), jnp.float32)),
    )
    attended = (summed / total).astype(out_ref.dtype)
    halves = heads // 2
    for h in range(heads):
        out_ref[h // halves, :, HEAD_WIDTH * (h % halves) : HEAD_WIDTH * (h % halves + 1)] = (
            attended[tokens * h : tokens * (h + 1)]
        )


def project(core_ref, attended_ref, own_ref, other_ref, out_ref):
    core = core_ref[0]
    for block in range(own_ref.shape[0]):
        out_ref[block] = (
            jnp.dot(attended_ref[core], own_ref[block], preferred_element_type=jnp.float32)
            + jnp.dot(attended_ref[1 - core], other_ref[block], preferred_element_type=jnp.float32)
        ).astype(out_ref.dtype)


def gate_up(rows_ref, gain_ref, routes_ref, *refs):
    parts = (len(refs) - 4) // 2
    gate_refs, up_refs = refs[:parts], refs[parts : 2 * parts]
    out_ref, normed, first, second = refs[2 * parts :]
    step = pl.program_id(0)
    experts, per_step, units, columns = gate_refs[0].shape
    pieces, tokens, _ = rows_ref.shape

    @pl.when(step == 0)
    def _():
        square = jnp.zeros((tokens, 1), jnp.float32)
        for piece in range(pieces):
            rows = rows_ref[piece].astype(jnp.float32)
            square += jnp.sum(rows * rows, axis=1, keepdims=True)
        scale = lax.rsqrt(square / D + 1e-06)
        for piece in range(pieces):
            normed[piece] = (
                rows_ref[piece].astype(jnp.float32) * scale * gain_ref[piece]
            ).astype(jnp.bfloat16)
        first[...] = jnp.zeros_like(first)
        second[...] = jnp.zeros_like(second)

    for weight_refs, total in ((gate_refs, first), (up_refs, second)):
        for part, weight_ref in enumerate(weight_refs):
            place = pl.ds(part * experts * units, experts * units)
            product = total[place]
            for piece in range(per_step):
                product += lax.dot_general(
                    weight_ref[:, piece].reshape(experts * units, columns),
                    normed[step * per_step + piece],
                    CONTRACT_LAST,
                    preferred_element_type=jnp.float32,
                )
            total[place] = product

    @pl.when(step == pl.num_programs(0) - 1)
    def _():
        chosen = [jnp.zeros((units, tokens), jnp.float32) for _ in range(TOP)]
        for expert in range(parts * experts):
            gate_values = first[expert * units : (expert + 1) * units]
            up_values = second[expert * units : (expert + 1) * units]
            activation = gate_values / (1.0 + jnp.exp(-gate_values)) * up_values
            for k in range(TOP):
                chosen[k] = jnp.where(routes_ref[k : k + 1] == expert, activation, chosen[k])
        for k in range(TOP):
            out_ref[k * units : (k + 1) * units] = chosen[k].astype(out_ref.dtype)


def down(activation_ref, routes_ref, route_weight_ref, hidden_ref, *refs):
    parts = (len(refs) - 3) // 2
    half_refs = refs[:parts], refs[parts : 2 * parts]
    out_ref, turned, mixed = refs[2 * parts :]
    step = pl.program_id(0)
    per_part, blocks, units, columns = refs[0].shape

    @pl.when(step == 0)
    def _():
        for half in range(2):
            for k in range(TOP):
                part = activation_ref[blocks * half : blocks * (half + 1), k * units : (k + 1) * units]
                part = part.reshape(blocks * units, part.shape[2]).astype(jnp.float32)
                turned[half, k] = jnp.transpose(part).astype(turned.dtype)
        mixed[...] = jnp.zeros_like(mixed)

    for part in range(parts):
        for place in range(per_part):
            expert = (step * parts + part) * per_part + place
            here = [routes_ref[:, k : k + 1] == expert for k in range(TOP)]
            share = sum(jnp.where(here[k], route_weight_ref[:, k : k + 1], 0.0) for k in range(TOP))
            masks = [here[k].astype(jnp.bfloat16) for k in range(TOP)]
            total = jnp.zeros(mixed.shape, jnp.float32)
            for half in range(2):
                rows = sum(turned[half, k] * masks[k] for k in range(TOP))
                weight = half_refs[half][part][place].reshape(blocks * units, columns)
                total += jnp.dot(rows, weight, preferred_element_type=jnp.float32)
            mixed[...] += total.astype(jnp.bfloat16).astype(jnp.float32) * share

    @pl.when(step == pl.num_programs(0) - 1)
    def _():
        out_ref[...] = (hidden_ref[...] + mixed[...]).astype(out_ref.dtype)


SCALAR = pl.BlockSpec(memory_space=pltpu.SMEM)
LIMIT = pltpu.CompilerParams(vmem_limit_bytes=32 * 1024 * 1024)
WIDE = pltpu.CompilerParams(vmem_limit_bytes=56 * 1024 * 1024)


def exchange(message, axis):
    return lax.all_to_all(message, axis, split_axis=0, concat_axis=0, tiled=True)


def spread(rows, axis):
    return exchange(jnp.broadcast_to(rows[None], (lax.axis_size(axis),) + rows.shape), axis)


def local(
    queries,
    all_key_rows,
    all_value_rows,
    out_weight,
    residual,
    post_gain,
    routes,
    route_weight,
    gate_weight,
    up_weight,
    down_weight,
):
    tokens = queries.shape[0]
    local_heads = queries.shape[1] // HEAD_WIDTH
    group_width = QUERY_HEADS // KEY_VALUE_HEADS
    tensor_count = lax.axis_size("tensor")
    expert_count = lax.axis_size("expert")
    tensor_index = lax.axis_index("tensor")
    expert_index = lax.axis_index("expert")
    core = lax.axis_index("dp")
    columns = D // tensor_count
    core_scalar = core.astype(jnp.int32).reshape(1)
    hidden_units = down_weight.shape[1]
    half_units = hidden_units // 2
    local_units = gate_weight.shape[2]

    first_blocks = D // columns
    down_blocks = half_units // local_units
    blocks = first_blocks + down_blocks

    gate_or_up = jnp.where(core == 0, gate_weight[0], up_weight[0]).T
    gate_or_up = jnp.transpose(gate_or_up.reshape(local_units, first_blocks, columns), (1, 0, 2))
    down_half = lax.dynamic_slice_in_dim(down_weight[0], core * half_units, half_units, 0)
    weights_here = jnp.concatenate(
        [gate_or_up.reshape(first_blocks * local_units, columns), down_half], axis=0
    )

    shared = tensor_index * local_heads // group_width
    key_head = lax.dynamic_slice_in_dim(all_key_rows, shared * HEAD_WIDTH, HEAD_WIDTH, 1)
    value_head = lax.dynamic_slice_in_dim(all_value_rows, shared * HEAD_WIDTH, HEAD_WIDTH, 1)
    half_rows = out_weight.shape[0] // 2
    weight_half = lax.dynamic_slice_in_dim(out_weight, core * half_rows, half_rows, 0)
    message = jnp.concatenate([weight_half, jnp.concatenate([key_head, value_head], axis=1)], axis=0)
    message, weights_here = lax.optimization_barrier((message, weights_here))
    gathered = spread(message, "expert")
    gathered, weights_here = lax.optimization_barrier((gathered, weights_here))
    weights = lax.all_gather(weights_here, ("dp", "expert"), axis=0)
    weight_own = gathered[:, :half_rows, :]
    weight_other = lax.ppermute(weight_own, "dp", SWAP)

    attended = pl.pallas_call(
        attend,
        out_shape=jax.ShapeDtypeStruct((2, tokens, half_rows), jnp.bfloat16),
        grid=(1,),
        in_specs=[
            SCALAR,
            pl.BlockSpec((tokens, local_heads * HEAD_WIDTH), lambda i: (0, 0)),
            pl.BlockSpec(
                (expert_count, tokens, 2 * HEAD_WIDTH), lambda i: (0, half_rows // tokens, 0)
            ),
        ],
        out_specs=pl.BlockSpec((2, tokens, half_rows), lambda i: (0, 0, 0)),
        scratch_shapes=[
            pltpu.VMEM((expert_count * tokens // CHUNK, local_heads * tokens, CHUNK), jnp.float32)
        ],
        compiler_params=WIDE,
        name="attend",
    )(expert_index.astype(jnp.int32).reshape(1), queries, gathered)

    wide = 4
    partial_value = pl.pallas_call(
        project,
        out_shape=jax.ShapeDtypeStruct((tensor_count, tokens, columns), jnp.bfloat16),
        grid=(tensor_count // wide,),
        in_specs=[
            SCALAR,
            pl.BlockSpec((2, tokens, half_rows), lambda i: (0, 0, 0)),
            pl.BlockSpec((wide, half_rows, columns), lambda i: (i, 0, 0)),
            pl.BlockSpec((wide, half_rows, columns), lambda i: (i, 0, 0)),
        ],
        out_specs=pl.BlockSpec((wide, tokens, columns), lambda i: (i, 0, 0)),
        compiler_params=WIDE,
        name="project",
    )(core_scalar, attended, gathered, weight_other)
    partial_sums = exchange(partial_value, "tensor")
    head_total = jnp.sum(partial_sums.astype(jnp.float32), axis=0)
    residual_share = lax.dynamic_slice_in_dim(residual, tensor_index * columns, columns, 1)
    hidden_share = residual_share.astype(jnp.float32) + head_total
    full_rows = spread(hidden_share.astype(jnp.bfloat16), "tensor")
    full_rows, weights = lax.optimization_barrier((full_rows, weights))
    weights = weights.reshape(2 * expert_count, blocks, local_units, columns)

    parts = 2
    per_part = expert_count // parts
    per_step = 2

    def first_spec(place):
        return pl.BlockSpec((per_part, per_step, local_units, columns), lambda i: (place, i, 0, 0))

    activation = pl.pallas_call(
        gate_up,
        out_shape=jax.ShapeDtypeStruct((TOP * local_units, tokens), jnp.bfloat16),
        grid=(first_blocks // per_step,),
        in_specs=[
            pl.BlockSpec((tensor_count, tokens, columns), lambda i: (0, 0, 0)),
            pl.BlockSpec((tensor_count, 1, columns), lambda i: (0, 0, 0)),
            pl.BlockSpec((TOP, tokens), lambda i: (0, 0)),
        ]
        + [first_spec(place) for place in range(2 * parts)],
        out_specs=pl.BlockSpec((TOP * local_units, tokens), lambda i: (0, 0)),
        scratch_shapes=[
            pltpu.VMEM((first_blocks, tokens, columns), jnp.bfloat16),
            pltpu.VMEM((expert_count * local_units, tokens), jnp.float32),
            pltpu.VMEM((expert_count * local_units, tokens), jnp.float32),
        ],
        compiler_params=LIMIT,
        name="gate_up",
    )(
        full_rows,
        post_gain.reshape(tensor_count, 1, columns),
        routes.T,
        *[weights] * (2 * parts),
    )
    activation = spread(activation, "tensor")

    per_part = 2
    down_steps = expert_count // (parts * per_part)

    def down_spec(half, part):
        return pl.BlockSpec(
            (per_part, down_blocks, local_units, columns),
            lambda i: ((half * down_steps + i) * parts + part, first_blocks // down_blocks, 0, 0),
        )

    return pl.pallas_call(
        down,
        out_shape=jax.ShapeDtypeStruct((tokens, columns), jnp.bfloat16),
        grid=(down_steps,),
        in_specs=[
            pl.BlockSpec((tensor_count, TOP * local_units, tokens), lambda i: (0, 0, 0)),
            pl.BlockSpec((tokens, TOP), lambda i: (0, 0)),
            pl.BlockSpec((tokens, TOP), lambda i: (0, 0)),
            pl.BlockSpec((tokens, columns), lambda i: (0, 0)),
        ]
        + [down_spec(half, part) for half in range(2) for part in range(parts)],
        out_specs=pl.BlockSpec((tokens, columns), lambda i: (0, 0)),
        scratch_shapes=[
            pltpu.VMEM((2, TOP, tokens, half_units), jnp.bfloat16),
            pltpu.VMEM((tokens, columns), jnp.float32),
        ],
        compiler_params=LIMIT,
        name="down",
    )(activation, routes, route_weight, hidden_share, *[weights] * (2 * parts))


def solution(mesh):
    return jax.shard_map(
        local,
        mesh=mesh,
        in_specs=(
            P(("dp", "expert"), "tensor"),
            P(("dp", "expert"), None),
            P(("dp", "expert"), None),
            P("tensor", "expert"),
            P(("dp", "expert"), None),
            P(),
            P(("dp", "expert"), None),
            P(("dp", "expert"), None),
            P("expert", None, "tensor"),
            P("expert", None, "tensor"),
            P("expert", None, "tensor"),
        ),
        out_specs=P(("dp", "expert"), "tensor"),
        check_vma=False,
    )
```

```python
import functools

import jax
import jax.numpy as jnp
from jax import lax
from jax.experimental import pallas as pl
from jax.experimental.pallas import tpu as pltpu
from jax.sharding import PartitionSpec as P

D = 4096
QUERY_HEADS = 64
KEY_VALUE_HEADS = 4
HEAD_WIDTH = 128
TOP = 2
PAIRS = 8
SWAP = [(0, 1), (1, 0)]
NEIGHBOUR = [(i, i ^ 1) for i in range(2 * PAIRS)]
PARITY = [[2 * pair + odd for pair in range(PAIRS)] for odd in range(2)]
CHUNK = 512


CONTRACT_LAST = (((1,), (1,)), ((), ()))


def attend(place_ref, query_ref, piece_ref, out_ref, score_ref):
    tokens = query_ref.shape[0]
    heads = query_ref.shape[1] // HEAD_WIDTH
    rows = heads * tokens
    blocks = CHUNK // tokens
    place = place_ref[0]
    stacked = jnp.concatenate(
        [query_ref[:, HEAD_WIDTH * h : HEAD_WIDTH * (h + 1)] for h in range(heads)], axis=0
    )
    token = place * tokens + lax.broadcasted_iota(jnp.int32, (rows, CHUNK), 0) % tokens
    offset = token - lax.broadcasted_iota(jnp.int32, (rows, CHUNK), 1)

    def score(step, row_max):
        keys = piece_ref[pl.ds(step * blocks, blocks), :, :HEAD_WIDTH].reshape(CHUNK, HEAD_WIDTH)
        scores = lax.dot_general(
            stacked, keys, CONTRACT_LAST, preferred_element_type=jnp.float32
        ) * HEAD_WIDTH ** (-0.5)
        masked = jnp.where(offset >= step * CHUNK, scores, -1e30)
        score_ref[step] = masked
        return jnp.maximum(row_max, jnp.max(masked, axis=1, keepdims=True))

    def weigh(step, carry):
        total, summed = carry
        exponent = jnp.exp(score_ref[step] - row_max)
        values = piece_ref[pl.ds(step * blocks, blocks), :, HEAD_WIDTH:].reshape(CHUNK, HEAD_WIDTH)
        return (
            total + jnp.sum(exponent, axis=1, keepdims=True),
            summed
            + jnp.dot(exponent.astype(jnp.bfloat16), values, preferred_element_type=jnp.float32),
        )

    steps = place // blocks + 1
    row_max = lax.fori_loop(0, steps, score, jnp.full((rows, 1), -1e30, jnp.float32))
    total, summed = lax.fori_loop(
        0,
        steps,
        weigh,
        (jnp.zeros((rows, 1), jnp.float32), jnp.zeros((rows, HEAD_WIDTH), jnp.float32)),
    )
    attended = (summed / total).astype(out_ref.dtype)
    halves = heads // 2
    for h in range(heads):
        out_ref[h // halves, :, HEAD_WIDTH * (h % halves) : HEAD_WIDTH * (h % halves + 1)] = (
            attended[tokens * h : tokens * (h + 1)]
        )


def project(scalar_ref, attended_ref, own_ref, other_ref, out_ref):
    core = scalar_ref[0]
    for block in range(own_ref.shape[0]):
        out_ref[block] = (
            jnp.dot(attended_ref[core], own_ref[block, 0], preferred_element_type=jnp.float32)
            + jnp.dot(
                attended_ref[1 - core], other_ref[block, 0], preferred_element_type=jnp.float32
            )
        ).astype(out_ref.dtype)


def gate_up(last, parts, scalar_ref, rows_ref, gain_ref, *refs):
    gate_refs, up_refs, refs = refs[:parts], refs[parts : 2 * parts], refs[2 * parts :]
    if last:
        before, before_square, routes_ref, out_ref, scaled, totals, square = refs
    else:
        totals, square, scaled = refs
    step = pl.program_id(0)
    experts, per_step, _, units, columns = gate_refs[0].shape
    pieces, tokens, _ = rows_ref.shape

    @pl.when(step == 0)
    def _():
        if last:
            square[...] = before_square[...]
            totals[...] = before[...]
        else:
            square[...] = jnp.zeros_like(square)
            totals[...] = jnp.zeros_like(totals)
        for piece in range(pieces):
            rows = rows_ref[piece].astype(jnp.float32)
            square[...] += jnp.sum(rows * rows, axis=1, keepdims=True)
            scaled[piece] = (rows * gain_ref[piece, scalar_ref[0]]).astype(jnp.bfloat16)

    for which, weight_refs in enumerate((gate_refs, up_refs)):
        for part, weight_ref in enumerate(weight_refs):
            place = pl.ds(part * experts * units, experts * units)
            product = totals[which, place]
            for piece in range(per_step):
                product += lax.dot_general(
                    weight_ref[:, piece, 0].reshape(experts * units, columns),
                    scaled[step * per_step + piece],
                    CONTRACT_LAST,
                    preferred_element_type=jnp.float32,
                )
            totals[which, place] = product

    if last:

        @pl.when(step == pl.num_programs(0) - 1)
        def _():
            scale = lax.rsqrt(square[...] / D + 1e-06)
            scale = jnp.transpose(jnp.broadcast_to(scale, (tokens, tokens)))[:1]
            chosen = [jnp.zeros((units, tokens), jnp.float32) for _ in range(TOP)]
            for expert in range(parts * experts):
                gate_values = totals[0, expert * units : (expert + 1) * units] * scale
                up_values = totals[1, expert * units : (expert + 1) * units] * scale
                activation = gate_values / (1.0 + jnp.exp(-gate_values)) * up_values
                for k in range(TOP):
                    chosen[k] = jnp.where(routes_ref[k : k + 1] == expert, activation, chosen[k])
            for k in range(TOP):
                out_ref[k * units : (k + 1) * units] = chosen[k].astype(out_ref.dtype)


def down(parts, scalar_ref, activation_ref, routes_ref, route_weight_ref, start_ref, *refs):
    half_refs = refs[:parts], refs[parts : 2 * parts]
    out_ref, turned, mixed = refs[2 * parts :]
    step = pl.program_id(0)
    per_part, blocks, _, units, columns = refs[0].shape

    @pl.when(step == 0)
    def _():
        for half in range(2):
            for k in range(TOP):
                part = activation_ref[blocks * half : blocks * (half + 1), k * units : (k + 1) * units]
                part = part.reshape(blocks * units, part.shape[2]).astype(jnp.float32)
                turned[half, k] = jnp.transpose(part).astype(turned.dtype)
        mixed[...] = start_ref[...]

    for part in range(parts):
        for place in range(per_part):
            expert = (step * parts + part) * per_part + place
            here = [routes_ref[:, k : k + 1] == expert for k in range(TOP)]
            share = sum(jnp.where(here[k], route_weight_ref[:, k : k + 1], 0.0) for k in range(TOP))
            masks = [here[k].astype(jnp.bfloat16) for k in range(TOP)]
            total = jnp.zeros(mixed.shape, jnp.float32)
            for half in range(2):
                rows = sum(turned[half, k] * masks[k] for k in range(TOP))
                weight = half_refs[half][part][place].reshape(blocks * units, columns)
                total += jnp.dot(rows, weight, preferred_element_type=jnp.float32)
            mixed[...] += total * share

    @pl.when(step == pl.num_programs(0) - 1)
    def _():
        out_ref[...] = mixed[...].astype(out_ref.dtype)


SCALAR = pl.BlockSpec(memory_space=pltpu.SMEM)
LIMIT = pltpu.CompilerParams(vmem_limit_bytes=32 * 1024 * 1024)
WIDE = pltpu.CompilerParams(vmem_limit_bytes=56 * 1024 * 1024)


def whole(*shape):
    return pl.BlockSpec(shape, lambda i, scalar_ref: (0,) * len(shape))


def cost(flops, size):
    return pl.CostEstimate(flops=flops, bytes_accessed=size, transcendentals=0)


def exchange(message, axis, groups=None):
    return lax.all_to_all(
        message, axis, split_axis=0, concat_axis=0, tiled=True, axis_index_groups=groups
    )


def spread(rows, axis, count, groups=None):
    return exchange(jnp.broadcast_to(rows[None], (count,) + rows.shape), axis, groups)


def local(
    queries,
    all_key_rows,
    all_value_rows,
    out_weight,
    residual,
    post_gain,
    routes,
    route_weight,
    gate_weight,
    up_weight,
    down_weight,
):
    tokens = queries.shape[0]
    local_heads = queries.shape[1] // HEAD_WIDTH
    group_width = QUERY_HEADS // KEY_VALUE_HEADS
    tensor_count = lax.axis_size("tensor")
    expert_count = lax.axis_size("expert")
    tensor_index = lax.axis_index("tensor")
    expert_index = lax.axis_index("expert")
    core = lax.axis_index("dp")
    columns = D // tensor_count
    odd = (tensor_index % 2).astype(jnp.int32)
    core = core.astype(jnp.int32)
    hidden_units = down_weight.shape[1]
    half_units = hidden_units // 2
    local_units = gate_weight.shape[2]

    first_blocks = D // columns
    down_blocks = half_units // local_units
    blocks = first_blocks + down_blocks

    gate_or_up = jnp.where(core == 0, gate_weight[0], up_weight[0]).T
    gate_or_up = jnp.transpose(gate_or_up.reshape(local_units, first_blocks, columns), (1, 0, 2))
    down_half = lax.dynamic_slice_in_dim(down_weight[0], core * half_units, half_units, 0)
    weights_here = jnp.concatenate(
        [gate_or_up.reshape(first_blocks * local_units, columns), down_half], axis=0
    )

    shared = tensor_index * local_heads // group_width
    key_head = lax.dynamic_slice_in_dim(all_key_rows, shared * HEAD_WIDTH, HEAD_WIDTH, 1)
    value_head = lax.dynamic_slice_in_dim(all_value_rows, shared * HEAD_WIDTH, HEAD_WIDTH, 1)
    half_rows = out_weight.shape[0] // 2
    weight_half = lax.dynamic_slice_in_dim(out_weight, core * half_rows, half_rows, 0)
    message = jnp.concatenate([weight_half, jnp.concatenate([key_head, value_head], axis=1)], axis=0)
    message, weights_here = lax.optimization_barrier((message, weights_here))
    weights = lax.all_gather(weights_here, ("dp", "expert"), axis=0)
    gathered = spread(message, "expert", expert_count)
    gathered_other = lax.ppermute(gathered, "dp", SWAP)

    attended = pl.pallas_call(
        attend,
        out_shape=jax.ShapeDtypeStruct((2, tokens, half_rows), jnp.bfloat16),
        grid=(1,),
        in_specs=[
            SCALAR,
            pl.BlockSpec((tokens, local_heads * HEAD_WIDTH), lambda i: (0, 0)),
            pl.BlockSpec(
                (expert_count, tokens, 2 * HEAD_WIDTH), lambda i: (0, half_rows // tokens, 0)
            ),
        ],
        out_specs=pl.BlockSpec((2, tokens, half_rows), lambda i: (0, 0, 0)),
        scratch_shapes=[
            pltpu.VMEM((expert_count * tokens // CHUNK, local_heads * tokens, CHUNK), jnp.float32)
        ],
        compiler_params=WIDE,
        name="attend",
    )(expert_index.astype(jnp.int32).reshape(1), queries, gathered)

    message_rows = message.shape[0]
    pair_shape = (PAIRS, 2, message_rows, columns)
    gathered, gathered_other = gathered.reshape(pair_shape), gathered_other.reshape(pair_shape)
    wide = 4

    def projected(parity, dtype):
        weight_spec = pl.BlockSpec(
            (wide, 1, half_rows, columns), lambda i, scalar_ref: (i, scalar_ref[1], 0, 0)
        )
        return pl.pallas_call(
            project,
            out_shape=jax.ShapeDtypeStruct((PAIRS, tokens, columns), dtype),
            grid_spec=pltpu.PrefetchScalarGridSpec(
                num_scalar_prefetch=1,
                grid=(PAIRS // wide,),
                in_specs=[whole(2, tokens, half_rows), weight_spec, weight_spec],
                out_specs=pl.BlockSpec((wide, tokens, columns), lambda i, scalar_ref: (i, 0, 0)),
            ),
            compiler_params=WIDE,
            cost_estimate=cost(4 * tokens * half_rows * PAIRS * columns, 4 * half_rows * PAIRS * columns),
            name="project",
        )(jnp.stack([core, parity]), attended, gathered, gathered_other)

    given = lax.ppermute(projected(1 - odd, jnp.bfloat16), "tensor", NEIGHBOUR)
    kept = projected(odd, jnp.float32)
    pair_sums = (kept + given.astype(jnp.float32)).astype(jnp.bfloat16)
    partial_sums = exchange(pair_sums, "tensor", PARITY)
    head_total = jnp.sum(partial_sums.astype(jnp.float32), axis=0)
    residual_share = lax.dynamic_slice_in_dim(residual, tensor_index * columns, columns, 1)
    hidden_share = residual_share.astype(jnp.float32) + head_total
    rows_own = spread(hidden_share.astype(jnp.bfloat16), "tensor", PAIRS, PARITY)
    rows_own, weights = lax.optimization_barrier((rows_own, weights))
    rows_other = lax.ppermute(rows_own, "tensor", NEIGHBOUR)
    weights = weights.reshape(2 * expert_count, blocks // 2, 2, local_units, columns)

    parts = 2
    per_part = expert_count // parts
    per_step = 2
    gains = post_gain.reshape(PAIRS, 2, 1, columns)
    totals_shape = (2, expert_count * local_units, tokens)

    def first_spec(place):
        return pl.BlockSpec(
            (per_part, per_step, 1, local_units, columns),
            lambda i, scalar_ref: (place, i, scalar_ref[0], 0, 0),
        )

    def gated(parity, rows, *before):
        last = bool(before)
        totals_spec = [whole(*totals_shape), whole(tokens, 1)]
        totals_types = [
            jax.ShapeDtypeStruct(totals_shape, jnp.float32),
            jax.ShapeDtypeStruct((tokens, 1), jnp.float32),
        ]
        scaled = [pltpu.VMEM((PAIRS, tokens, columns), jnp.bfloat16)]
        totals_scratch = [pltpu.VMEM(kind.shape, kind.dtype) for kind in totals_types]
        out = (TOP * local_units, tokens)
        return pl.pallas_call(
            functools.partial(gate_up, last, parts),
            out_shape=jax.ShapeDtypeStruct(out, jnp.bfloat16) if last else totals_types,
            grid_spec=pltpu.PrefetchScalarGridSpec(
                num_scalar_prefetch=1,
                grid=(PAIRS // per_step,),
                in_specs=[whole(PAIRS, tokens, columns), whole(PAIRS, 2, 1, columns)]
                + [first_spec(place) for place in range(2 * parts)]
                + (totals_spec + [whole(TOP, tokens)] if last else []),
                out_specs=whole(*out) if last else totals_spec,
                scratch_shapes=scaled + totals_scratch if last else scaled,
            ),
            compiler_params=LIMIT,
            cost_estimate=cost(
                2 * tokens * 2 * expert_count * local_units * D // 2,
                2 * 2 * expert_count * local_units * D // 2,
            ),
            name="gate_up",
        )(parity.reshape(1), rows, gains, *[weights] * (2 * parts), *before)

    before = gated(odd, rows_own)
    activation = gated(1 - odd, rows_other, *before, routes.T)

    activation_own = spread(activation, "tensor", PAIRS, PARITY)
    activation_other = lax.ppermute(activation_own, "tensor", NEIGHBOUR)
    per_part = 2
    down_steps = expert_count // (parts * per_part)
    quarter = PAIRS // 2

    def down_spec(half, part):
        return pl.BlockSpec(
            (per_part, quarter, 1, local_units, columns),
            lambda i, scalar_ref: (
                (half * down_steps + i) * parts + part,
                first_blocks // (2 * quarter),
                scalar_ref[0],
                0,
                0,
            ),
        )

    def lowered(parity, rows, start, dtype):
        return pl.pallas_call(
            functools.partial(down, parts),
            out_shape=jax.ShapeDtypeStruct((tokens, columns), dtype),
            grid_spec=pltpu.PrefetchScalarGridSpec(
                num_scalar_prefetch=1,
                grid=(down_steps,),
                in_specs=[
                    whole(PAIRS, TOP * local_units, tokens),
                    whole(tokens, TOP),
                    whole(tokens, TOP),
                    whole(tokens, columns),
                ]
                + [down_spec(half, part) for half in range(2) for part in range(parts)],
                out_specs=whole(tokens, columns),
                scratch_shapes=[
                    pltpu.VMEM((2, TOP, tokens, quarter * local_units), jnp.bfloat16),
                    pltpu.VMEM((tokens, columns), jnp.float32),
                ],
            ),
            compiler_params=LIMIT,
            cost_estimate=cost(
                2 * tokens * expert_count * hidden_units * columns // 2,
                2 * expert_count * hidden_units * columns // 2,
            ),
            name="down",
        )(parity.reshape(1), rows, routes, route_weight, start, *[weights] * (2 * parts))

    mixed = lowered(odd, activation_own, hidden_share, jnp.float32)
    return lowered(1 - odd, activation_other, mixed, jnp.bfloat16)


def solution(mesh):
    return jax.shard_map(
        local,
        mesh=mesh,
        in_specs=(
            P(("dp", "expert"), "tensor"),
            P(("dp", "expert"), None),
            P(("dp", "expert"), None),
            P("tensor", "expert"),
            P(("dp", "expert"), None),
            P(),
            P(("dp", "expert"), None),
            P(("dp", "expert"), None),
            P("expert", None, "tensor"),
            P("expert", None, "tensor"),
            P("expert", None, "tensor"),
        ),
        out_specs=P(("dp", "expert"), "tensor"),
        check_vma=False,
    )
```

```python
import functools

import jax
import jax.numpy as jnp
from jax import lax
from jax.experimental import pallas as pl
from jax.experimental.pallas import tpu as pltpu
from jax.sharding import PartitionSpec as P

D = 4096
QUERY_HEADS = 64
KEY_VALUE_HEADS = 4
HEAD_WIDTH = 128
TOP = 2
PAIRS = 8
SWAP = [(0, 1), (1, 0)]
NEIGHBOUR = [(i, i ^ 1) for i in range(2 * PAIRS)]
PARITY = [[2 * pair + odd for pair in range(PAIRS)] for odd in range(2)]
CHUNK = 1024
LOG2_E = 1.4426950408889634


CONTRACT_LAST = (((1,), (1,)), ((), ()))


def attend(place_ref, query_ref, piece_ref, out_ref):
    tokens = query_ref.shape[0]
    heads = query_ref.shape[1] // HEAD_WIDTH
    rows = heads * tokens
    blocks = CHUNK // tokens
    place = place_ref[0]
    rate = HEAD_WIDTH ** (-0.5) * LOG2_E
    stacked = jnp.concatenate(
        [query_ref[:, HEAD_WIDTH * h : HEAD_WIDTH * (h + 1)] for h in range(heads)], axis=0
    )

    def take(step, carry, masked):
        row_max, total, summed = carry
        place_here = pl.ds(step * blocks, blocks)
        keys = piece_ref[place_here, :, :HEAD_WIDTH].reshape(CHUNK, HEAD_WIDTH)
        values = piece_ref[place_here, :, HEAD_WIDTH:].reshape(CHUNK, HEAD_WIDTH)
        scores = lax.dot_general(
            stacked, keys, CONTRACT_LAST, preferred_element_type=jnp.float32
        )
        if masked:
            token = place * tokens + lax.broadcasted_iota(jnp.int32, (rows, CHUNK), 0) % tokens
            offset = token - lax.broadcasted_iota(jnp.int32, (rows, CHUNK), 1)
            scores = jnp.where(offset >= step * CHUNK, scores, -1e30)
        new_max = jnp.maximum(row_max, jnp.max(scores, axis=1, keepdims=True))
        shrink = jnp.exp2((row_max - new_max) * rate)
        exponent = jnp.exp2((scores - new_max) * rate)
        total = total * shrink + jnp.sum(exponent, axis=1, keepdims=True)
        summed = summed * shrink + jnp.dot(
            exponent.astype(jnp.bfloat16), values, preferred_element_type=jnp.float32
        )
        return new_max, total, summed

    full = place // blocks
    carry = (
        jnp.full((rows, 1), -1e30, jnp.float32),
        jnp.zeros((rows, 1), jnp.float32),
        jnp.zeros((rows, HEAD_WIDTH), jnp.float32),
    )
    carry = lax.fori_loop(0, full, lambda step, held: take(step, held, False), carry)
    _, total, summed = take(full, carry, True)
    attended = (summed / total).astype(out_ref.dtype)
    halves = heads // 2
    for h in range(heads):
        out_ref[h // halves, :, HEAD_WIDTH * (h % halves) : HEAD_WIDTH * (h % halves + 1)] = (
            attended[tokens * h : tokens * (h + 1)]
        )


def project(core_ref, parity_ref, attended_ref, own_ref, other_ref, out_ref):
    core = core_ref[0]
    for block in range(own_ref.shape[0]):
        out_ref[block] = (
            jnp.dot(attended_ref[core], own_ref[block, 0], preferred_element_type=jnp.float32)
            + jnp.dot(
                attended_ref[1 - core], other_ref[block, 0], preferred_element_type=jnp.float32
            )
        ).astype(out_ref.dtype)


def gate_up(last, scalar_ref, rows_ref, gain_ref, gate_ref, up_ref, *refs):
    if last:
        before, before_square, routes_ref, out_ref, scaled, totals, square = refs
    else:
        totals, square, scaled = refs
    step = pl.program_id(0)
    experts, per_step, _, units, columns = gate_ref.shape
    pieces, tokens, _ = rows_ref.shape
    together = 2 * units

    @pl.when(step == 0)
    def _():
        squares = jnp.zeros((tokens, columns), jnp.float32)
        for piece in range(pieces):
            rows = rows_ref[piece].astype(jnp.float32)
            squares += rows * rows
            scaled[piece] = (rows * gain_ref[piece, scalar_ref[0]]).astype(jnp.bfloat16)
        sums = jnp.sum(squares, axis=1, keepdims=True)
        square[...] = before_square[...] + sums if last else sums

    def multiply(start):
        for which, weight_ref in enumerate((gate_ref, up_ref)):
            for expert in range(0, experts, 2):
                place = pl.ds(expert * units, together)
                product = None if start is None else start[which, place]
                for piece in range(per_step):
                    part = lax.dot_general(
                        weight_ref[expert : expert + 2, piece, 0].reshape(together, columns),
                        scaled[step * per_step + piece],
                        CONTRACT_LAST,
                        preferred_element_type=jnp.float32,
                    )
                    product = part if product is None else product + part
                totals[which, place] = product

    @pl.when(step == 0)
    def _():
        multiply(before if last else None)

    @pl.when(step > 0)
    def _():
        multiply(totals)

    if last:

        @pl.when(step == pl.num_programs(0) - 1)
        def _():
            scale = lax.rsqrt(square[...] / D + 1e-06)
            scale = jnp.transpose(jnp.broadcast_to(scale, (tokens, tokens)))[:1]
            chosen = [jnp.zeros((units, tokens), jnp.float32) for _ in range(TOP)]
            for expert in range(experts):
                gate_values = totals[0, expert * units : (expert + 1) * units] * scale
                up_values = totals[1, expert * units : (expert + 1) * units] * scale
                activation = gate_values / (1.0 + jnp.exp(-gate_values)) * up_values
                for k in range(TOP):
                    chosen[k] = jnp.where(routes_ref[k : k + 1] == expert, activation, chosen[k])
            for k in range(TOP):
                out_ref[k * units : (k + 1) * units] = chosen[k].astype(out_ref.dtype)


def down(parts, scalar_ref, activation_ref, routes_ref, route_weight_ref, start_ref, *refs):
    half_refs = refs[:parts], refs[parts : 2 * parts]
    out_ref, turned, mixed = refs[2 * parts :]
    step = pl.program_id(0)
    per_part, blocks, _, units, columns = refs[0].shape

    @pl.when(step == 0)
    def _():
        for half in range(2):
            for k in range(TOP):
                part = activation_ref[blocks * half : blocks * (half + 1), k * units : (k + 1) * units]
                part = part.reshape(blocks * units, part.shape[2]).astype(jnp.float32)
                turned[half, k] = jnp.transpose(part).astype(turned.dtype)
        mixed[...] = start_ref[...]

    for part in range(parts):
        for place in range(per_part):
            expert = (step * parts + part) * per_part + place
            here = [routes_ref[:, k : k + 1] == expert for k in range(TOP)]
            share = sum(jnp.where(here[k], route_weight_ref[:, k : k + 1], 0.0) for k in range(TOP))
            masks = [here[k].astype(jnp.bfloat16) for k in range(TOP)]
            total = jnp.zeros(mixed.shape, jnp.float32)
            for half in range(2):
                rows = sum(turned[half, k] * masks[k] for k in range(TOP))
                weight = half_refs[half][part][place].reshape(blocks * units, columns)
                total += jnp.dot(rows, weight, preferred_element_type=jnp.float32)
            mixed[...] += total * share

    @pl.when(step == pl.num_programs(0) - 1)
    def _():
        out_ref[...] = mixed[...].astype(out_ref.dtype)


SCALAR = pl.BlockSpec(memory_space=pltpu.SMEM)
HERE = pl.BlockSpec(memory_space=pltpu.VMEM)
LIMIT = pltpu.CompilerParams(vmem_limit_bytes=32 * 1024 * 1024)
WIDE = pltpu.CompilerParams(vmem_limit_bytes=56 * 1024 * 1024)


def whole(*shape):
    return pl.BlockSpec(shape, lambda i, *_: (0,) * len(shape))


def cost(flops, size):
    return pl.CostEstimate(flops=flops, bytes_accessed=size, transcendentals=0)


def exchange(message, axis, groups=None):
    return lax.all_to_all(
        message, axis, split_axis=0, concat_axis=0, tiled=True, axis_index_groups=groups
    )


def spread(rows, axis, count, groups=None):
    return exchange(jnp.broadcast_to(rows[None], (count,) + rows.shape), axis, groups)


def local(
    queries,
    all_key_rows,
    all_value_rows,
    out_weight,
    residual,
    post_gain,
    routes,
    route_weight,
    gate_weight,
    up_weight,
    down_weight,
):
    tokens = queries.shape[0]
    local_heads = queries.shape[1] // HEAD_WIDTH
    group_width = QUERY_HEADS // KEY_VALUE_HEADS
    tensor_count = lax.axis_size("tensor")
    expert_count = lax.axis_size("expert")
    tensor_index = lax.axis_index("tensor")
    expert_index = lax.axis_index("expert")
    core = lax.axis_index("dp")
    columns = D // tensor_count
    odd = (tensor_index % 2).astype(jnp.int32)
    core = core.astype(jnp.int32)
    hidden_units = down_weight.shape[1]
    half_units = hidden_units // 2
    local_units = gate_weight.shape[2]

    first_blocks = D // columns
    down_blocks = half_units // local_units
    blocks = first_blocks + down_blocks

    gate_or_up = jnp.where(core == 0, gate_weight[0], up_weight[0]).T
    gate_or_up = jnp.transpose(gate_or_up.reshape(local_units, first_blocks, columns), (1, 0, 2))
    down_half = lax.dynamic_slice_in_dim(down_weight[0], core * half_units, half_units, 0)
    weights_here = jnp.concatenate(
        [gate_or_up.reshape(first_blocks * local_units, columns), down_half], axis=0
    )

    shared = tensor_index * local_heads // group_width
    key_head = lax.dynamic_slice_in_dim(all_key_rows, shared * HEAD_WIDTH, HEAD_WIDTH, 1)
    value_head = lax.dynamic_slice_in_dim(all_value_rows, shared * HEAD_WIDTH, HEAD_WIDTH, 1)
    half_rows = out_weight.shape[0] // 2
    weight_half = lax.dynamic_slice_in_dim(out_weight, core * half_rows, half_rows, 0)
    message = jnp.concatenate([weight_half, jnp.concatenate([key_head, value_head], axis=1)], axis=0)
    weights = lax.all_gather(weights_here, ("dp", "expert"), axis=0)
    gathered = spread(message, "expert", expert_count)
    gathered_other = lax.ppermute(gathered, "dp", SWAP)

    attended = pl.pallas_call(
        attend,
        out_shape=jax.ShapeDtypeStruct((2, tokens, half_rows), jnp.bfloat16),
        grid=(1,),
        in_specs=[
            SCALAR,
            pl.BlockSpec((tokens, local_heads * HEAD_WIDTH), lambda i: (0, 0)),
            pl.BlockSpec(
                (expert_count, tokens, 2 * HEAD_WIDTH), lambda i: (0, half_rows // tokens, 0)
            ),
        ],
        out_specs=pl.BlockSpec((2, tokens, half_rows), lambda i: (0, 0, 0)),
        compiler_params=WIDE,
        name="attend",
    )(expert_index.astype(jnp.int32).reshape(1), queries, gathered)

    message_rows = message.shape[0]
    pair_shape = (PAIRS, 2, message_rows, columns)
    gathered, gathered_other = gathered.reshape(pair_shape), gathered_other.reshape(pair_shape)
    wide = 4

    def projected(parity, dtype):
        weight_spec = pl.BlockSpec(
            (wide, 1, half_rows, columns), lambda i, core_ref, parity_ref: (i, parity_ref[0], 0, 0)
        )
        return pl.pallas_call(
            project,
            out_shape=jax.ShapeDtypeStruct((PAIRS, tokens, columns), dtype),
            grid_spec=pltpu.PrefetchScalarGridSpec(
                num_scalar_prefetch=2,
                grid=(PAIRS // wide,),
                in_specs=[whole(2, tokens, half_rows), weight_spec, weight_spec],
                out_specs=pl.BlockSpec((wide, tokens, columns), lambda i, *_: (i, 0, 0)),
            ),
            compiler_params=LIMIT,
            cost_estimate=cost(4 * tokens * half_rows * PAIRS * columns, 4 * half_rows * PAIRS * columns),
            name="project",
        )(core.reshape(1), parity.reshape(1), attended, gathered, gathered_other)

    given = lax.ppermute(projected(1 - odd, jnp.bfloat16), "tensor", NEIGHBOUR)
    kept = projected(odd, jnp.float32)
    pair_sums = (kept + given.astype(jnp.float32)).astype(jnp.bfloat16)
    partial_sums = exchange(pair_sums, "tensor", PARITY)
    head_total = jnp.sum(partial_sums.astype(jnp.float32), axis=0)
    residual_share = lax.dynamic_slice_in_dim(residual, tensor_index * columns, columns, 1)
    hidden_share = residual_share.astype(jnp.float32) + head_total
    rows_own = spread(hidden_share.astype(jnp.bfloat16), "tensor", PAIRS, PARITY)
    rows_own, weights = lax.optimization_barrier((rows_own, weights))
    rows_other = lax.ppermute(rows_own, "tensor", NEIGHBOUR)
    weights = weights.reshape(2 * expert_count, blocks // 2, 2, local_units, columns)

    per_step = 4
    gains = post_gain.reshape(PAIRS, 2, 1, columns)
    totals_types = [
        jax.ShapeDtypeStruct((2, expert_count * local_units, tokens), jnp.float32),
        jax.ShapeDtypeStruct((tokens, 1), jnp.float32),
    ]
    out_type = jax.ShapeDtypeStruct((TOP * local_units, tokens), jnp.bfloat16)

    def first_spec(which):
        return pl.BlockSpec(
            (expert_count, per_step, 1, local_units, columns),
            lambda i, parity_ref: (which, i, parity_ref[0], 0, 0),
        )

    def gated(parity, rows, *before):
        last = bool(before)
        scratch = [pltpu.VMEM((PAIRS, tokens, columns), jnp.bfloat16)]
        if last:
            scratch += [pltpu.VMEM(kind.shape, kind.dtype) for kind in totals_types]
        return pl.pallas_call(
            functools.partial(gate_up, last),
            out_shape=out_type if last else totals_types,
            grid_spec=pltpu.PrefetchScalarGridSpec(
                num_scalar_prefetch=1,
                grid=(PAIRS // per_step,),
                in_specs=[HERE, HERE, first_spec(0), first_spec(1)] + [HERE] * len(before),
                out_specs=HERE if last else [HERE] * 2,
                scratch_shapes=scratch,
            ),
            compiler_params=LIMIT,
            cost_estimate=cost(
                2 * tokens * 2 * expert_count * local_units * D // 2,
                2 * 2 * expert_count * local_units * D // 2,
            ),
            name="gate_up",
        )(parity.reshape(1), rows, gains, weights, weights, *before)

    before = gated(odd, rows_own)
    activation = gated(1 - odd, rows_other, *before, routes.T)

    activation_own = spread(activation, "tensor", PAIRS, PARITY)
    activation_other = lax.ppermute(activation_own, "tensor", NEIGHBOUR)
    parts = 2
    per_part = 4
    down_steps = expert_count // (parts * per_part)
    quarter = PAIRS // 2

    def down_spec(half, part):
        return pl.BlockSpec(
            (per_part, quarter, 1, local_units, columns),
            lambda i, scalar_ref: (
                (half * down_steps + i) * parts + part,
                first_blocks // (2 * quarter),
                scalar_ref[0],
                0,
                0,
            ),
        )

    def lowered(parity, rows, start, dtype):
        return pl.pallas_call(
            functools.partial(down, parts),
            out_shape=jax.ShapeDtypeStruct((tokens, columns), dtype),
            grid_spec=pltpu.PrefetchScalarGridSpec(
                num_scalar_prefetch=1,
                grid=(down_steps,),
                in_specs=[
                    whole(PAIRS, TOP * local_units, tokens),
                    whole(tokens, TOP),
                    whole(tokens, TOP),
                    whole(tokens, columns),
                ]
                + [down_spec(half, part) for half in range(2) for part in range(parts)],
                out_specs=whole(tokens, columns),
                scratch_shapes=[
                    pltpu.VMEM((2, TOP, tokens, quarter * local_units), jnp.bfloat16),
                    pltpu.VMEM((tokens, columns), jnp.float32),
                ],
            ),
            compiler_params=LIMIT,
            cost_estimate=cost(
                2 * tokens * expert_count * hidden_units * columns // 2,
                2 * expert_count * hidden_units * columns // 2,
            ),
            name="down",
        )(parity.reshape(1), rows, routes, route_weight, start, *[weights] * (2 * parts))

    mixed = lowered(odd, activation_own, hidden_share, jnp.float32)
    return lowered(1 - odd, activation_other, mixed, jnp.bfloat16)


def solution(mesh):
    return jax.shard_map(
        local,
        mesh=mesh,
        in_specs=(
            P(("dp", "expert"), "tensor"),
            P(("dp", "expert"), None),
            P(("dp", "expert"), None),
            P("tensor", "expert"),
            P(("dp", "expert"), None),
            P(),
            P(("dp", "expert"), None),
            P(("dp", "expert"), None),
            P("expert", None, "tensor"),
            P("expert", None, "tensor"),
            P("expert", None, "tensor"),
        ),
        out_specs=P(("dp", "expert"), "tensor"),
        check_vma=False,
    )
```

```python
import functools

import jax
import jax.numpy as jnp
from jax import lax
from jax.experimental import pallas as pl
from jax.experimental.pallas import tpu as pltpu
from jax.sharding import PartitionSpec as P

D = 4096
QUERY_HEADS = 64
KEY_VALUE_HEADS = 4
HEAD_WIDTH = 128
TOP = 2
PAIRS = 8
SWAP = [(0, 1), (1, 0)]
NEIGHBOUR = [(i, i ^ 1) for i in range(2 * PAIRS)]
PARITY = [[2 * pair + odd for pair in range(PAIRS)] for odd in range(2)]
CHUNK = 1024
LOG2_E = 1.4426950408889634


CONTRACT_LAST = (((1,), (1,)), ((), ()))


def attend(place_ref, query_ref, piece_ref, out_ref):
    tokens = query_ref.shape[0]
    heads = query_ref.shape[1] // HEAD_WIDTH
    rows = heads * tokens
    half = tokens // 2
    blocks = CHUNK // tokens
    place = place_ref[0]
    rate = HEAD_WIDTH ** (-0.5) * LOG2_E
    stacked = jnp.concatenate(
        [query_ref[:, HEAD_WIDTH * h : HEAD_WIDTH * (h + 1)] for h in range(heads)], axis=0
    )

    def take(step, carry, masked):
        row_max, total, summed = carry
        place_here = pl.ds(step * blocks, blocks)
        keys = piece_ref[:, place_here, :half].reshape(CHUNK, HEAD_WIDTH)
        values = piece_ref[:, place_here, half:].reshape(CHUNK, HEAD_WIDTH)
        scores = lax.dot_general(
            stacked, keys, CONTRACT_LAST, preferred_element_type=jnp.float32
        )
        if masked:
            token = lax.broadcasted_iota(jnp.int32, (rows, 1), 0) % tokens + place * tokens
            key = lax.broadcasted_iota(jnp.int32, (1, CHUNK), 1)
            odd_half, rest = key // (blocks * half), key % (blocks * half)
            key_place = (step * blocks + rest // half) * tokens + odd_half * half + rest % half
            scores = jnp.where(token >= key_place, scores, -1e30)
        new_max = jnp.maximum(row_max, jnp.max(scores, axis=1, keepdims=True))
        shrink = jnp.exp2((row_max - new_max) * rate)
        exponent = jnp.exp2((scores - new_max) * rate)
        total = total * shrink + jnp.sum(exponent, axis=1, keepdims=True)
        summed = summed * shrink + jnp.dot(
            exponent.astype(jnp.bfloat16), values, preferred_element_type=jnp.float32
        )
        return new_max, total, summed

    full = place // blocks
    carry = (
        jnp.full((rows, 1), -1e30, jnp.float32),
        jnp.zeros((rows, 1), jnp.float32),
        jnp.zeros((rows, HEAD_WIDTH), jnp.float32),
    )
    carry = lax.fori_loop(0, full, lambda step, held: take(step, held, False), carry)
    _, total, summed = take(full, carry, True)
    attended = (summed / total).astype(out_ref.dtype)
    halves = heads // 2
    for h in range(heads):
        out_ref[h // halves, :, HEAD_WIDTH * (h % halves) : HEAD_WIDTH * (h % halves + 1)] = (
            attended[tokens * h : tokens * (h + 1)]
        )


def project(last, core_ref, source_ref, attended_ref, own_ref, other_ref, *refs):
    core = core_ref[0]
    out_ref = refs[-1]
    for block in range(own_ref.shape[1]):
        own = jnp.concatenate([own_ref[0, block, 0], own_ref[0, block, 1]], axis=1)
        other = jnp.concatenate([other_ref[0, block, 0], other_ref[0, block, 1]], axis=1)
        total = jnp.dot(attended_ref[core], own, preferred_element_type=jnp.float32) + jnp.dot(
            attended_ref[1 - core], other, preferred_element_type=jnp.float32
        )
        if last:
            total += refs[0][block]
        out_ref[block] = total.astype(out_ref.dtype)


def gate_up(last, scalar_ref, rows_ref, gain_ref, gate_ref, up_ref, *refs):
    if last:
        before, before_square, routes_ref, out_ref, scaled, totals, square = refs
    else:
        totals, square, scaled = refs
    step = pl.program_id(0)
    experts, per_step, _, units, columns = gate_ref.shape
    pieces, tokens, _ = rows_ref.shape
    together = 2 * units

    @pl.when(step == 0)
    def _():
        squares = jnp.zeros((tokens, columns), jnp.float32)
        for piece in range(pieces):
            rows = rows_ref[piece].astype(jnp.float32)
            squares += rows * rows
            scaled[piece] = (rows * gain_ref[piece, scalar_ref[0]]).astype(jnp.bfloat16)
        sums = jnp.sum(squares, axis=1, keepdims=True)
        square[...] = before_square[...] + sums if last else sums

    def multiply(start):
        for which, weight_ref in enumerate((gate_ref, up_ref)):
            for expert in range(0, experts, 2):
                place = pl.ds(expert * units, together)
                product = None if start is None else start[which, place]
                for piece in range(per_step):
                    part = lax.dot_general(
                        weight_ref[expert : expert + 2, piece, 0].reshape(together, columns),
                        scaled[step * per_step + piece],
                        CONTRACT_LAST,
                        preferred_element_type=jnp.float32,
                    )
                    product = part if product is None else product + part
                totals[which, place] = product

    @pl.when(step == 0)
    def _():
        multiply(before if last else None)

    @pl.when(step > 0)
    def _():
        multiply(totals)

    if last:

        @pl.when(step == pl.num_programs(0) - 1)
        def _():
            scale = lax.rsqrt(square[...] / D + 1e-06)
            scale = jnp.transpose(jnp.broadcast_to(scale, (tokens, tokens)))[:1]
            chosen = [jnp.zeros((units, tokens), jnp.float32) for _ in range(TOP)]
            for expert in range(experts):
                gate_values = totals[0, expert * units : (expert + 1) * units] * scale
                up_values = totals[1, expert * units : (expert + 1) * units] * scale
                activation = gate_values / (1.0 + jnp.exp(-gate_values)) * up_values
                for k in range(TOP):
                    chosen[k] = jnp.where(routes_ref[k : k + 1] == expert, activation, chosen[k])
            for k in range(TOP):
                out_ref[k * units : (k + 1) * units] = chosen[k].astype(out_ref.dtype)


def down(parts, scalar_ref, activation_ref, routes_ref, route_weight_ref, start_ref, *refs):
    half_refs = refs[:parts], refs[parts : 2 * parts]
    out_ref, turned, mixed = refs[2 * parts :]
    step = pl.program_id(0)
    per_part, blocks, _, units, columns = refs[0].shape

    @pl.when(step == 0)
    def _():
        for half in range(2):
            for k in range(TOP):
                part = activation_ref[blocks * half : blocks * (half + 1), k * units : (k + 1) * units]
                part = part.reshape(blocks * units, part.shape[2]).astype(jnp.float32)
                turned[half, k] = jnp.transpose(part).astype(turned.dtype)
        mixed[...] = start_ref[...]

    for part in range(parts):
        for place in range(per_part):
            expert = (step * parts + part) * per_part + place
            here = [routes_ref[:, k : k + 1] == expert for k in range(TOP)]
            share = sum(jnp.where(here[k], route_weight_ref[:, k : k + 1], 0.0) for k in range(TOP))
            masks = [here[k].astype(jnp.bfloat16) for k in range(TOP)]
            total = jnp.zeros(mixed.shape, jnp.float32)
            for half in range(2):
                rows = sum(turned[half, k] * masks[k] for k in range(TOP))
                weight = half_refs[half][part][place].reshape(blocks * units, columns)
                total += jnp.dot(rows, weight, preferred_element_type=jnp.float32)
            mixed[...] += total * share

    @pl.when(step == pl.num_programs(0) - 1)
    def _():
        out_ref[...] = mixed[...].astype(out_ref.dtype)


SCALAR = pl.BlockSpec(memory_space=pltpu.SMEM)
HERE = pl.BlockSpec(memory_space=pltpu.VMEM)
LIMIT = pltpu.CompilerParams(vmem_limit_bytes=32 * 1024 * 1024)
WIDE = pltpu.CompilerParams(vmem_limit_bytes=56 * 1024 * 1024)


def whole(*shape):
    return pl.BlockSpec(shape, lambda i, *_: (0,) * len(shape))


def cost(flops, size):
    return pl.CostEstimate(flops=flops, bytes_accessed=size, transcendentals=0)


def exchange(message, axis, groups=None):
    return lax.all_to_all(
        message, axis, split_axis=0, concat_axis=0, tiled=True, axis_index_groups=groups
    )


def spread(rows, axis, count, groups=None):
    return exchange(jnp.broadcast_to(rows[None], (count,) + rows.shape), axis, groups)


def local(
    queries,
    all_key_rows,
    all_value_rows,
    out_weight,
    residual,
    post_gain,
    routes,
    route_weight,
    gate_weight,
    up_weight,
    down_weight,
):
    tokens = queries.shape[0]
    local_heads = queries.shape[1] // HEAD_WIDTH
    group_width = QUERY_HEADS // KEY_VALUE_HEADS
    tensor_count = lax.axis_size("tensor")
    expert_count = lax.axis_size("expert")
    tensor_index = lax.axis_index("tensor")
    expert_index = lax.axis_index("expert")
    core = lax.axis_index("dp")
    columns = D // tensor_count
    odd = (tensor_index % 2).astype(jnp.int32)
    core = core.astype(jnp.int32)
    hidden_units = down_weight.shape[1]
    half_units = hidden_units // 2
    local_units = gate_weight.shape[2]

    first_blocks = D // columns
    down_blocks = half_units // local_units
    blocks = first_blocks + down_blocks

    gate_or_up = jnp.where(core == 0, gate_weight[0], up_weight[0]).T
    gate_or_up = jnp.transpose(
        gate_or_up.reshape(local_units, PAIRS, 2, 2, columns // 2), (1, 3, 0, 2, 4)
    )
    down_half = lax.dynamic_slice_in_dim(down_weight[0], core * half_units, half_units, 0)
    weights_here = jnp.concatenate(
        [gate_or_up.reshape(first_blocks * local_units, columns), down_half], axis=0
    )

    shared = tensor_index * local_heads // group_width
    key_head = lax.dynamic_slice_in_dim(all_key_rows, shared * HEAD_WIDTH, HEAD_WIDTH, 1)
    value_head = lax.dynamic_slice_in_dim(all_value_rows, shared * HEAD_WIDTH, HEAD_WIDTH, 1)
    half_rows = out_weight.shape[0] // 2
    weight_half = lax.dynamic_slice_in_dim(out_weight, core * half_rows, half_rows, 0)
    half_tokens = tokens // 2
    half_columns = columns // 2
    key_half = lax.dynamic_slice_in_dim(key_head, odd * half_tokens, half_tokens, 0)
    value_half = lax.dynamic_slice_in_dim(value_head, odd * half_tokens, half_tokens, 0)
    message = jnp.stack(
        [
            jnp.concatenate(
                [weight_half[:, side * half_columns : (side + 1) * half_columns], key_half, value_half],
                axis=0,
            )
            for side in range(2)
        ]
    )
    message_rows = message.shape[1]
    both = [
        [(2 * pair + side) * expert_count + place for side in range(2) for place in range(expert_count)]
        for pair in range(PAIRS)
    ]
    weights = lax.all_gather(weights_here, ("dp", "expert"), axis=0)
    gathered = exchange(
        jnp.broadcast_to(message[:, None], (2, expert_count) + message.shape[1:]).reshape(
            2 * expert_count, message_rows, half_columns
        ),
        ("tensor", "expert"),
        both,
    )
    gathered_other = lax.ppermute(gathered, "dp", SWAP)

    attended = pl.pallas_call(
        attend,
        out_shape=jax.ShapeDtypeStruct((2, tokens, half_rows), jnp.bfloat16),
        grid=(1,),
        in_specs=[
            SCALAR,
            pl.BlockSpec((tokens, local_heads * HEAD_WIDTH), lambda i: (0, 0)),
            pl.BlockSpec(
                (2, expert_count, tokens, HEAD_WIDTH), lambda i: (0, 0, half_rows // tokens, 0)
            ),
        ],
        out_specs=pl.BlockSpec((2, tokens, half_rows), lambda i: (0, 0, 0)),
        compiler_params=WIDE,
        name="attend",
    )(
        expert_index.astype(jnp.int32).reshape(1),
        queries,
        gathered.reshape(2, expert_count, message_rows, half_columns),
    )

    attended_other = lax.ppermute(attended, "tensor", NEIGHBOUR)
    pair_shape = (2, PAIRS, 2, message_rows, half_columns)
    gathered, gathered_other = gathered.reshape(pair_shape), gathered_other.reshape(pair_shape)
    wide = 8

    def projected(source, rows, dtype, *before):
        weight_spec = pl.BlockSpec(
            (1, wide, 2, half_rows, half_columns),
            lambda i, core_ref, source_ref: (source_ref[0], i, 0, 0, 0),
        )
        return pl.pallas_call(
            functools.partial(project, bool(before)),
            out_shape=jax.ShapeDtypeStruct((PAIRS, tokens, columns), dtype),
            grid_spec=pltpu.PrefetchScalarGridSpec(
                num_scalar_prefetch=2,
                grid=(PAIRS // wide,),
                in_specs=[HERE, weight_spec, weight_spec] + [HERE] * len(before),
                out_specs=HERE,
            ),
            compiler_params=LIMIT,
            cost_estimate=cost(4 * tokens * half_rows * PAIRS * columns, 4 * half_rows * PAIRS * columns),
            name="project",
        )(core.reshape(1), source.reshape(1), rows, gathered, gathered_other, *before)

    kept = projected(odd, attended, jnp.float32)
    pair_sums = projected(1 - odd, attended_other, jnp.bfloat16, kept)
    partial_sums = exchange(pair_sums, "tensor", PARITY)
    head_total = jnp.sum(partial_sums.astype(jnp.float32), axis=0)
    pair_start = tensor_index // 2 * 2 * columns + odd * half_columns
    residual_share = jnp.concatenate(
        [
            lax.dynamic_slice_in_dim(residual, pair_start + side * columns, half_columns, 1)
            for side in range(2)
        ],
        axis=1,
    )
    hidden_share = residual_share.astype(jnp.float32) + head_total
    rows_own = spread(hidden_share.astype(jnp.bfloat16), "tensor", PAIRS, PARITY)
    rows_own, weights = lax.optimization_barrier((rows_own, weights))
    rows_other = lax.ppermute(rows_own, "tensor", NEIGHBOUR)
    weights = weights.reshape(2 * expert_count, blocks // 2, 2, local_units, columns)

    per_step = 4
    gains = jnp.transpose(post_gain.reshape(PAIRS, 2, 2, half_columns), (0, 2, 1, 3)).reshape(
        PAIRS, 2, 1, columns
    )
    totals_types = [
        jax.ShapeDtypeStruct((2, expert_count * local_units, tokens), jnp.float32),
        jax.ShapeDtypeStruct((tokens, 1), jnp.float32),
    ]
    out_type = jax.ShapeDtypeStruct((TOP * local_units, tokens), jnp.bfloat16)

    def first_spec(which):
        return pl.BlockSpec(
            (expert_count, per_step, 1, local_units, columns),
            lambda i, parity_ref: (which, i, parity_ref[0], 0, 0),
        )

    def gated(parity, rows, *before):
        last = bool(before)
        scratch = [pltpu.VMEM((PAIRS, tokens, columns), jnp.bfloat16)]
        if last:
            scratch += [pltpu.VMEM(kind.shape, kind.dtype) for kind in totals_types]
        return pl.pallas_call(
            functools.partial(gate_up, last),
            out_shape=out_type if last else totals_types,
            grid_spec=pltpu.PrefetchScalarGridSpec(
                num_scalar_prefetch=1,
                grid=(PAIRS // per_step,),
                in_specs=[HERE, HERE, first_spec(0), first_spec(1)] + [HERE] * len(before),
                out_specs=HERE if last else [HERE] * 2,
                scratch_shapes=scratch,
            ),
            compiler_params=LIMIT,
            cost_estimate=cost(
                2 * tokens * 2 * expert_count * local_units * D // 2,
                2 * 2 * expert_count * local_units * D // 2,
            ),
            name="gate_up",
        )(parity.reshape(1), rows, gains, weights, weights, *before)

    before = gated(odd, rows_own)
    activation = gated(1 - odd, rows_other, *before, routes.T)

    activation_own = spread(activation, "tensor", PAIRS, PARITY)
    activation_other = lax.ppermute(activation_own, "tensor", NEIGHBOUR)
    parts = 2
    per_part = 4
    down_steps = expert_count // (parts * per_part)
    quarter = PAIRS // 2

    def down_spec(half, part):
        return pl.BlockSpec(
            (per_part, quarter, 1, local_units, columns),
            lambda i, scalar_ref: (
                (half * down_steps + i) * parts + part,
                first_blocks // (2 * quarter),
                scalar_ref[0],
                0,
                0,
            ),
        )

    def lowered(parity, rows, start, dtype):
        return pl.pallas_call(
            functools.partial(down, parts),
            out_shape=jax.ShapeDtypeStruct((tokens, columns), dtype),
            grid_spec=pltpu.PrefetchScalarGridSpec(
                num_scalar_prefetch=1,
                grid=(down_steps,),
                in_specs=[
                    whole(PAIRS, TOP * local_units, tokens),
                    whole(tokens, TOP),
                    whole(tokens, TOP),
                    whole(tokens, columns),
                ]
                + [down_spec(half, part) for half in range(2) for part in range(parts)],
                out_specs=whole(tokens, columns),
                scratch_shapes=[
                    pltpu.VMEM((2, TOP, tokens, quarter * local_units), jnp.bfloat16),
                    pltpu.VMEM((tokens, columns), jnp.float32),
                ],
            ),
            compiler_params=LIMIT,
            cost_estimate=cost(
                2 * tokens * expert_count * hidden_units * columns // 2,
                2 * expert_count * hidden_units * columns // 2,
            ),
            name="down",
        )(parity.reshape(1), rows, routes, route_weight, start, *[weights] * (2 * parts))

    shares = [
        lax.dynamic_slice(
            rows, (tensor_index // 2, 0, odd * half_columns), (1, tokens, half_columns)
        )[0].astype(jnp.float32)
        for rows in (rows_own, rows_other)
    ]
    hidden_here = jnp.where(
        odd == 0, jnp.concatenate(shares, axis=1), jnp.concatenate(shares[::-1], axis=1)
    )
    mixed = lowered(odd, activation_own, hidden_here, jnp.float32)
    return lowered(1 - odd, activation_other, mixed, jnp.bfloat16)


def solution(mesh):
    return jax.shard_map(
        local,
        mesh=mesh,
        in_specs=(
            P(("dp", "expert"), "tensor"),
            P(("dp", "expert"), None),
            P(("dp", "expert"), None),
            P("tensor", "expert"),
            P(("dp", "expert"), None),
            P(),
            P(("dp", "expert"), None),
            P(("dp", "expert"), None),
            P("expert", None, "tensor"),
            P("expert", None, "tensor"),
            P("expert", None, "tensor"),
        ),
        out_specs=P(("dp", "expert"), "tensor"),
        check_vma=False,
    )
```

```python
import functools

import jax
import jax.numpy as jnp
from jax import lax
from jax.experimental import pallas as pl
from jax.experimental.pallas import tpu as pltpu
from jax.sharding import PartitionSpec as P

D = 4096
QUERY_HEADS = 64
KEY_VALUE_HEADS = 4
HEAD_WIDTH = 128
TOP = 2
PAIRS = 8
SWAP = [(0, 1), (1, 0)]
NEIGHBOUR = [(i, i ^ 1) for i in range(2 * PAIRS)]
PARITY = [[2 * pair + odd for pair in range(PAIRS)] for odd in range(2)]
CHUNK = 1024
LOG2_E = 1.4426950408889634


CONTRACT_LAST = (((1,), (1,)), ((), ()))


def attend(place_ref, query_ref, piece_ref, out_ref):
    tokens = query_ref.shape[0]
    heads = query_ref.shape[1] // HEAD_WIDTH
    rows = heads * tokens
    half = tokens // 2
    blocks = CHUNK // tokens
    place = place_ref[0]
    rate = HEAD_WIDTH ** (-0.5) * LOG2_E
    stacked = jnp.concatenate(
        [query_ref[:, HEAD_WIDTH * h : HEAD_WIDTH * (h + 1)] for h in range(heads)], axis=0
    )

    def take(step, carry, masked):
        row_max, total, summed = carry
        place_here = pl.ds(step * blocks, blocks)
        keys = piece_ref[:, place_here, :half].reshape(CHUNK, HEAD_WIDTH)
        values = piece_ref[:, place_here, half:].reshape(CHUNK, HEAD_WIDTH)
        scores = lax.dot_general(
            stacked, keys, CONTRACT_LAST, preferred_element_type=jnp.float32
        )
        if masked:
            token = lax.broadcasted_iota(jnp.int32, (rows, 1), 0) % tokens + place * tokens
            key = lax.broadcasted_iota(jnp.int32, (1, CHUNK), 1)
            odd_half, rest = key // (blocks * half), key % (blocks * half)
            key_place = (step * blocks + rest // half) * tokens + odd_half * half + rest % half
            scores = jnp.where(token >= key_place, scores, -1e30)
        new_max = jnp.maximum(row_max, jnp.max(scores, axis=1, keepdims=True))
        shrink = jnp.exp2((row_max - new_max) * rate)
        exponent = jnp.exp2((scores - new_max) * rate)
        total = total * shrink + jnp.sum(exponent, axis=1, keepdims=True)
        summed = summed * shrink + jnp.dot(
            exponent.astype(jnp.bfloat16), values, preferred_element_type=jnp.float32
        )
        return new_max, total, summed

    full = place // blocks
    carry = (
        jnp.full((rows, 1), -1e30, jnp.float32),
        jnp.zeros((rows, 1), jnp.float32),
        jnp.zeros((rows, HEAD_WIDTH), jnp.float32),
    )
    carry = lax.fori_loop(0, full, lambda step, held: take(step, held, False), carry)
    _, total, summed = take(full, carry, True)
    attended = (summed / total).astype(out_ref.dtype)
    halves = heads // 2
    for h in range(heads):
        out_ref[h // halves, :, HEAD_WIDTH * (h % halves) : HEAD_WIDTH * (h % halves + 1)] = (
            attended[tokens * h : tokens * (h + 1)]
        )


def project(last, core_ref, source_ref, attended_ref, own_ref, other_ref, *refs):
    core = core_ref[0]
    out_ref = refs[-1]
    for block in range(own_ref.shape[1]):
        own = jnp.concatenate([own_ref[0, block, 0], own_ref[0, block, 1]], axis=1)
        other = jnp.concatenate([other_ref[0, block, 0], other_ref[0, block, 1]], axis=1)
        total = jnp.dot(attended_ref[core], own, preferred_element_type=jnp.float32) + jnp.dot(
            attended_ref[1 - core], other, preferred_element_type=jnp.float32
        )
        if last:
            total += refs[0][block]
        out_ref[block] = total.astype(out_ref.dtype)


def gate_up(last, scalar_ref, rows_ref, gain_ref, gate_ref, up_ref, *refs):
    if last:
        before, before_square, routes_ref, out_ref, scaled, totals, square = refs
    else:
        totals, square, scaled = refs
    step = pl.program_id(0)
    experts, per_step, _, units, columns = gate_ref.shape
    pieces, tokens, _ = rows_ref.shape
    together = 2 * units

    @pl.when(step == 0)
    def _():
        squares = jnp.zeros((tokens, columns), jnp.float32)
        for piece in range(pieces):
            rows = rows_ref[piece].astype(jnp.float32)
            squares += rows * rows
            scaled[piece] = (rows * gain_ref[piece, scalar_ref[0]]).astype(jnp.bfloat16)
        sums = jnp.sum(squares, axis=1, keepdims=True)
        square[...] = before_square[...] + sums if last else sums

    def multiply(start):
        for which, weight_ref in enumerate((gate_ref, up_ref)):
            for expert in range(0, experts, 2):
                place = pl.ds(expert * units, together)
                product = None if start is None else start[which, place]
                for piece in range(per_step):
                    part = lax.dot_general(
                        weight_ref[expert : expert + 2, piece, 0].reshape(together, columns),
                        scaled[step * per_step + piece],
                        CONTRACT_LAST,
                        preferred_element_type=jnp.float32,
                    )
                    product = part if product is None else product + part
                totals[which, place] = product

    @pl.when(step == 0)
    def _():
        multiply(before if last else None)

    @pl.when(step > 0)
    def _():
        multiply(totals)

    if last:

        @pl.when(step == pl.num_programs(0) - 1)
        def _():
            scale = lax.rsqrt(square[...] / D + 1e-06)
            scale = jnp.transpose(jnp.broadcast_to(scale, (tokens, tokens)))[:1]
            chosen = [jnp.zeros((units, tokens), jnp.float32) for _ in range(TOP)]
            for expert in range(experts):
                gate_values = totals[0, expert * units : (expert + 1) * units] * scale
                up_values = totals[1, expert * units : (expert + 1) * units] * scale
                activation = gate_values / (1.0 + jnp.exp(-gate_values)) * up_values
                for k in range(TOP):
                    chosen[k] = jnp.where(routes_ref[k : k + 1] == expert, activation, chosen[k])
            for k in range(TOP):
                out_ref[k * units : (k + 1) * units] = chosen[k].astype(out_ref.dtype)


def down(parts, scalar_ref, activation_ref, routes_ref, route_weight_ref, start_ref, *refs):
    half_refs = refs[:parts], refs[parts : 2 * parts]
    out_ref, turned, mixed = refs[2 * parts :]
    step = pl.program_id(0)
    per_part, blocks, _, units, columns = refs[0].shape

    @pl.when(step == 0)
    def _():
        for half in range(2):
            for k in range(TOP):
                part = activation_ref[blocks * half : blocks * (half + 1), k * units : (k + 1) * units]
                part = part.reshape(blocks * units, part.shape[2]).astype(jnp.float32)
                turned[half, k] = jnp.transpose(part).astype(turned.dtype)
        mixed[...] = start_ref[...]

    for part in range(parts):
        for place in range(per_part):
            expert = (step * parts + part) * per_part + place
            here = [routes_ref[:, k : k + 1] == expert for k in range(TOP)]
            share = sum(jnp.where(here[k], route_weight_ref[:, k : k + 1], 0.0) for k in range(TOP))
            masks = [here[k].astype(jnp.bfloat16) for k in range(TOP)]
            total = jnp.zeros(mixed.shape, jnp.float32)
            for half in range(2):
                rows = sum(turned[half, k] * masks[k] for k in range(TOP))
                weight = half_refs[half][part][place].reshape(blocks * units, columns)
                total += jnp.dot(rows, weight, preferred_element_type=jnp.float32)
            mixed[...] += total * share

    @pl.when(step == pl.num_programs(0) - 1)
    def _():
        out_ref[...] = mixed[...].astype(out_ref.dtype)


SCALAR = pl.BlockSpec(memory_space=pltpu.SMEM)
HERE = pl.BlockSpec(memory_space=pltpu.VMEM)
LIMIT = pltpu.CompilerParams(vmem_limit_bytes=32 * 1024 * 1024)
WIDE = pltpu.CompilerParams(vmem_limit_bytes=56 * 1024 * 1024)


def whole(*shape):
    return pl.BlockSpec(shape, lambda i, *_: (0,) * len(shape))


def cost(flops, size):
    return pl.CostEstimate(flops=flops, bytes_accessed=size, transcendentals=0)


def exchange(message, axis, groups=None):
    return lax.all_to_all(
        message, axis, split_axis=0, concat_axis=0, tiled=True, axis_index_groups=groups
    )


def spread(rows, axis, count, groups=None):
    return exchange(jnp.broadcast_to(rows[None], (count,) + rows.shape), axis, groups)


def local(
    queries,
    all_key_rows,
    all_value_rows,
    out_weight,
    residual,
    post_gain,
    routes,
    route_weight,
    gate_weight,
    up_weight,
    down_weight,
):
    tokens = queries.shape[0]
    local_heads = queries.shape[1] // HEAD_WIDTH
    group_width = QUERY_HEADS // KEY_VALUE_HEADS
    tensor_count = lax.axis_size("tensor")
    expert_count = lax.axis_size("expert")
    tensor_index = lax.axis_index("tensor")
    expert_index = lax.axis_index("expert")
    core = lax.axis_index("dp")
    columns = D // tensor_count
    odd = (tensor_index % 2).astype(jnp.int32)
    core = core.astype(jnp.int32)
    hidden_units = down_weight.shape[1]
    half_units = hidden_units // 2
    local_units = gate_weight.shape[2]

    first_blocks = D // columns

    gate_or_up = jnp.where(core == 0, gate_weight[0], up_weight[0]).T
    gate_or_up = jnp.transpose(
        gate_or_up.reshape(local_units, PAIRS, 2, 2, columns // 2), (1, 3, 0, 2, 4)
    )
    down_half = lax.dynamic_slice_in_dim(down_weight[0], core * half_units, half_units, 0)
    gate_or_up = gate_or_up.reshape(first_blocks * local_units, columns)

    shared = tensor_index * local_heads // group_width
    key_head = lax.dynamic_slice_in_dim(all_key_rows, shared * HEAD_WIDTH, HEAD_WIDTH, 1)
    value_head = lax.dynamic_slice_in_dim(all_value_rows, shared * HEAD_WIDTH, HEAD_WIDTH, 1)
    half_rows = out_weight.shape[0] // 2
    weight_half = lax.dynamic_slice_in_dim(out_weight, core * half_rows, half_rows, 0)
    half_tokens = tokens // 2
    half_columns = columns // 2
    key_half = lax.dynamic_slice_in_dim(key_head, odd * half_tokens, half_tokens, 0)
    value_half = lax.dynamic_slice_in_dim(value_head, odd * half_tokens, half_tokens, 0)
    message = jnp.stack(
        [
            jnp.concatenate(
                [weight_half[:, side * half_columns : (side + 1) * half_columns], key_half, value_half],
                axis=0,
            )
            for side in range(2)
        ]
    )
    message_rows = message.shape[1]
    both = [
        [(2 * pair + side) * expert_count + place for side in range(2) for place in range(expert_count)]
        for pair in range(PAIRS)
    ]
    weights = lax.all_gather(gate_or_up, ("dp", "expert"), axis=0)
    down_weights = lax.all_gather(down_half, ("dp", "expert"), axis=0)
    gathered = exchange(
        jnp.broadcast_to(message[:, None], (2, expert_count) + message.shape[1:]).reshape(
            2 * expert_count, message_rows, half_columns
        ),
        ("tensor", "expert"),
        both,
    )
    gathered_other = lax.ppermute(gathered, "dp", SWAP)

    attended = pl.pallas_call(
        attend,
        out_shape=jax.ShapeDtypeStruct((2, tokens, half_rows), jnp.bfloat16),
        grid=(1,),
        in_specs=[
            SCALAR,
            pl.BlockSpec((tokens, local_heads * HEAD_WIDTH), lambda i: (0, 0)),
            pl.BlockSpec(
                (2, expert_count, tokens, HEAD_WIDTH), lambda i: (0, 0, half_rows // tokens, 0)
            ),
        ],
        out_specs=pl.BlockSpec((2, tokens, half_rows), lambda i: (0, 0, 0)),
        compiler_params=WIDE,
        name="attend",
    )(
        expert_index.astype(jnp.int32).reshape(1),
        queries,
        gathered.reshape(2, expert_count, message_rows, half_columns),
    )

    attended_other = lax.ppermute(attended, "tensor", NEIGHBOUR)
    pair_shape = (2, PAIRS, 2, message_rows, half_columns)
    gathered, gathered_other = gathered.reshape(pair_shape), gathered_other.reshape(pair_shape)
    wide = 8

    def projected(source, rows, dtype, *before):
        weight_spec = pl.BlockSpec(
            (1, wide, 2, half_rows, half_columns),
            lambda i, core_ref, source_ref: (source_ref[0], i, 0, 0, 0),
        )
        return pl.pallas_call(
            functools.partial(project, bool(before)),
            out_shape=jax.ShapeDtypeStruct((PAIRS, tokens, columns), dtype),
            grid_spec=pltpu.PrefetchScalarGridSpec(
                num_scalar_prefetch=2,
                grid=(PAIRS // wide,),
                in_specs=[HERE, weight_spec, weight_spec] + [HERE] * len(before),
                out_specs=HERE,
            ),
            compiler_params=LIMIT,
            cost_estimate=cost(4 * tokens * half_rows * PAIRS * columns, 4 * half_rows * PAIRS * columns),
            name="project",
        )(core.reshape(1), source.reshape(1), rows, gathered, gathered_other, *before)

    kept = projected(odd, attended, jnp.float32)
    pair_sums = projected(1 - odd, attended_other, jnp.bfloat16, kept)
    partial_sums = exchange(pair_sums, "tensor", PARITY)
    head_total = jnp.sum(partial_sums.astype(jnp.float32), axis=0)
    pair_start = tensor_index // 2 * 2 * columns + odd * half_columns
    residual_share = jnp.concatenate(
        [
            lax.dynamic_slice_in_dim(residual, pair_start + side * columns, half_columns, 1)
            for side in range(2)
        ],
        axis=1,
    )
    hidden_share = residual_share.astype(jnp.float32) + head_total
    rows_own = spread(hidden_share.astype(jnp.bfloat16), "tensor", PAIRS, PARITY)
    rows_own, weights = lax.optimization_barrier((rows_own, weights))
    rows_other = lax.ppermute(rows_own, "tensor", NEIGHBOUR)
    weights = weights.reshape(2 * expert_count, PAIRS, 2, local_units, columns)

    per_step = 4
    gains = jnp.transpose(post_gain.reshape(PAIRS, 2, 2, half_columns), (0, 2, 1, 3)).reshape(
        PAIRS, 2, 1, columns
    )
    totals_types = [
        jax.ShapeDtypeStruct((2, expert_count * local_units, tokens), jnp.float32),
        jax.ShapeDtypeStruct((tokens, 1), jnp.float32),
    ]
    out_type = jax.ShapeDtypeStruct((TOP * local_units, tokens), jnp.bfloat16)

    def first_spec(which):
        return pl.BlockSpec(
            (expert_count, per_step, 1, local_units, columns),
            lambda i, parity_ref: (which, i, parity_ref[0], 0, 0),
        )

    def gated(parity, rows, *before):
        last = bool(before)
        scratch = [pltpu.VMEM((PAIRS, tokens, columns), jnp.bfloat16)]
        if last:
            scratch += [pltpu.VMEM(kind.shape, kind.dtype) for kind in totals_types]
        return pl.pallas_call(
            functools.partial(gate_up, last),
            out_shape=out_type if last else totals_types,
            grid_spec=pltpu.PrefetchScalarGridSpec(
                num_scalar_prefetch=1,
                grid=(PAIRS // per_step,),
                in_specs=[HERE, HERE, first_spec(0), first_spec(1)] + [HERE] * len(before),
                out_specs=HERE if last else [HERE] * 2,
                scratch_shapes=scratch,
            ),
            compiler_params=LIMIT,
            cost_estimate=cost(
                2 * tokens * 2 * expert_count * local_units * D // 2,
                2 * 2 * expert_count * local_units * D // 2,
            ),
            name="gate_up",
        )(parity.reshape(1), rows, gains, weights, weights, *before)

    before = gated(odd, rows_own)
    activation = gated(1 - odd, rows_other, *before, routes.T)

    activation_own = spread(activation, "tensor", PAIRS, PARITY)
    activation_other = lax.ppermute(activation_own, "tensor", NEIGHBOUR)
    parts = 2
    per_part = 4
    down_steps = expert_count // (parts * per_part)
    quarter = PAIRS // 2
    down_weights = down_weights.reshape(2 * expert_count, quarter, 2, local_units, columns)

    def down_spec(half, part):
        return pl.BlockSpec(
            (per_part, quarter, 1, local_units, columns),
            lambda i, scalar_ref: (
                (half * down_steps + i) * parts + part,
                0,
                scalar_ref[0],
                0,
                0,
            ),
        )

    def lowered(parity, rows, start, dtype):
        return pl.pallas_call(
            functools.partial(down, parts),
            out_shape=jax.ShapeDtypeStruct((tokens, columns), dtype),
            grid_spec=pltpu.PrefetchScalarGridSpec(
                num_scalar_prefetch=1,
                grid=(down_steps,),
                in_specs=[
                    whole(PAIRS, TOP * local_units, tokens),
                    whole(tokens, TOP),
                    whole(tokens, TOP),
                    whole(tokens, columns),
                ]
                + [down_spec(half, part) for half in range(2) for part in range(parts)],
                out_specs=whole(tokens, columns),
                scratch_shapes=[
                    pltpu.VMEM((2, TOP, tokens, quarter * local_units), jnp.bfloat16),
                    pltpu.VMEM((tokens, columns), jnp.float32),
                ],
            ),
            compiler_params=LIMIT,
            cost_estimate=cost(
                2 * tokens * expert_count * hidden_units * columns // 2,
                2 * expert_count * hidden_units * columns // 2,
            ),
            name="down",
        )(parity.reshape(1), rows, routes, route_weight, start, *[down_weights] * (2 * parts))

    shares = [
        lax.dynamic_slice(
            rows, (tensor_index // 2, 0, odd * half_columns), (1, tokens, half_columns)
        )[0].astype(jnp.float32)
        for rows in (rows_own, rows_other)
    ]
    hidden_here = jnp.where(
        odd == 0, jnp.concatenate(shares, axis=1), jnp.concatenate(shares[::-1], axis=1)
    )
    mixed = lowered(odd, activation_own, hidden_here, jnp.float32)
    return lowered(1 - odd, activation_other, mixed, jnp.bfloat16)


def solution(mesh):
    return jax.shard_map(
        local,
        mesh=mesh,
        in_specs=(
            P(("dp", "expert"), "tensor"),
            P(("dp", "expert"), None),
            P(("dp", "expert"), None),
            P("tensor", "expert"),
            P(("dp", "expert"), None),
            P(),
            P(("dp", "expert"), None),
            P(("dp", "expert"), None),
            P("expert", None, "tensor"),
            P("expert", None, "tensor"),
            P("expert", None, "tensor"),
        ),
        out_specs=P(("dp", "expert"), "tensor"),
        check_vma=False,
    )
```

```python
import functools

import jax
import jax.numpy as jnp
from jax import lax
from jax.experimental import pallas as pl
from jax.experimental.pallas import tpu as pltpu
from jax.sharding import PartitionSpec as P

D = 4096
QUERY_HEADS = 64
KEY_VALUE_HEADS = 4
HEAD_WIDTH = 128
TOP = 2
PAIRS = 8
SWAP = [(0, 1), (1, 0)]
NEIGHBOUR = [(i, i ^ 1) for i in range(2 * PAIRS)]
PARITY = [[2 * pair + odd for pair in range(PAIRS)] for odd in range(2)]
CHUNK = 1024
LOG2_E = 1.4426950408889634


CONTRACT_LAST = (((1,), (1,)), ((), ()))


def pack(core_ref, gate_ref, up_ref, out_ref):
    units = gate_ref.shape[0]
    columns = out_ref.shape[1]
    half = columns // 2

    def store(source_ref):
        for pair in range(gate_ref.shape[1] // (2 * columns)):
            for odd in range(2):
                row = (2 * pair + odd) * units
                for side in range(2):
                    start = (2 * pair + side) * columns + odd * half
                    out_ref[row : row + units, side * half : (side + 1) * half] = source_ref[
                        :, start : start + half
                    ]

    @pl.when(core_ref[0] == 0)
    def _():
        store(gate_ref)

    @pl.when(core_ref[0] != 0)
    def _():
        store(up_ref)


def compose(core_ref, odd_ref, shared_ref, weight_ref, key_ref, value_ref, out_ref):
    rows = weight_ref.shape[0]
    half = key_ref.shape[0]
    places = out_ref.shape[0] // 2
    width = out_ref.shape[2]
    for side in range(2):
        for place in range(side * places, (side + 1) * places):
            out_ref[place, :rows] = weight_ref[:, side * width : (side + 1) * width]
            out_ref[place, rows : rows + half] = key_ref[...]
            out_ref[place, rows + half :] = value_ref[...]


def attend(place_ref, query_ref, piece_ref, out_ref):
    tokens = query_ref.shape[0]
    heads = query_ref.shape[1] // HEAD_WIDTH
    rows = heads * tokens
    half = tokens // 2
    blocks = CHUNK // tokens
    place = place_ref[0]
    rate = HEAD_WIDTH ** (-0.5) * LOG2_E
    stacked = jnp.concatenate(
        [query_ref[:, HEAD_WIDTH * h : HEAD_WIDTH * (h + 1)] for h in range(heads)], axis=0
    )

    def take(step, carry, masked):
        row_max, total, summed = carry
        place_here = pl.ds(step * blocks, blocks)
        keys = piece_ref[:, place_here, :half].reshape(CHUNK, HEAD_WIDTH)
        values = piece_ref[:, place_here, half:].reshape(CHUNK, HEAD_WIDTH)
        scores = lax.dot_general(
            stacked, keys, CONTRACT_LAST, preferred_element_type=jnp.float32
        )
        if masked:
            token = lax.broadcasted_iota(jnp.int32, (rows, 1), 0) % tokens + place * tokens
            key = lax.broadcasted_iota(jnp.int32, (1, CHUNK), 1)
            odd_half, rest = key // (blocks * half), key % (blocks * half)
            key_place = (step * blocks + rest // half) * tokens + odd_half * half + rest % half
            scores = jnp.where(token >= key_place, scores, -1e30)
        new_max = jnp.maximum(row_max, jnp.max(scores, axis=1, keepdims=True))
        shrink = jnp.exp2((row_max - new_max) * rate)
        exponent = jnp.exp2((scores - new_max) * rate)
        total = total * shrink + jnp.sum(exponent, axis=1, keepdims=True)
        summed = summed * shrink + jnp.dot(
            exponent.astype(jnp.bfloat16), values, preferred_element_type=jnp.float32
        )
        return new_max, total, summed

    full = place // blocks
    carry = (
        jnp.full((rows, 1), -1e30, jnp.float32),
        jnp.zeros((rows, 1), jnp.float32),
        jnp.zeros((rows, HEAD_WIDTH), jnp.float32),
    )
    carry = lax.fori_loop(0, full, lambda step, held: take(step, held, False), carry)
    _, total, summed = take(full, carry, True)
    attended = (summed / total).astype(out_ref.dtype)
    halves = heads // 2
    for h in range(heads):
        out_ref[h // halves, :, HEAD_WIDTH * (h % halves) : HEAD_WIDTH * (h % halves + 1)] = (
            attended[tokens * h : tokens * (h + 1)]
        )


def project(last, core_ref, source_ref, attended_ref, own_ref, other_ref, *refs):
    core = core_ref[0]
    out_ref = refs[-1]
    for block in range(own_ref.shape[1]):
        own = jnp.concatenate([own_ref[0, block, 0], own_ref[0, block, 1]], axis=1)
        other = jnp.concatenate([other_ref[0, block, 0], other_ref[0, block, 1]], axis=1)
        total = jnp.dot(attended_ref[core], own, preferred_element_type=jnp.float32) + jnp.dot(
            attended_ref[1 - core], other, preferred_element_type=jnp.float32
        )
        if last:
            total += refs[0][block]
        out_ref[block] = total.astype(out_ref.dtype)


def gate_up(last, scalar_ref, rows_ref, gain_ref, gate_ref, up_ref, *refs):
    if last:
        before, before_square, routes_ref, out_ref, scaled, totals, square = refs
    else:
        totals, square, scaled = refs
    step = pl.program_id(0)
    experts, per_step, _, units, columns = gate_ref.shape
    pieces, tokens, _ = rows_ref.shape
    together = 2 * units

    @pl.when(step == 0)
    def _():
        squares = jnp.zeros((tokens, columns), jnp.float32)
        for piece in range(pieces):
            rows = rows_ref[piece].astype(jnp.float32)
            squares += rows * rows
            scaled[piece] = (rows * gain_ref[piece, scalar_ref[0]]).astype(jnp.bfloat16)
        sums = jnp.sum(squares, axis=1, keepdims=True)
        square[...] = before_square[...] + sums if last else sums

    def multiply(start):
        for which, weight_ref in enumerate((gate_ref, up_ref)):
            for expert in range(0, experts, 2):
                place = pl.ds(expert * units, together)
                product = None if start is None else start[which, place]
                for piece in range(per_step):
                    part = lax.dot_general(
                        weight_ref[expert : expert + 2, piece, 0].reshape(together, columns),
                        scaled[step * per_step + piece],
                        CONTRACT_LAST,
                        preferred_element_type=jnp.float32,
                    )
                    product = part if product is None else product + part
                totals[which, place] = product

    @pl.when(step == 0)
    def _():
        multiply(before if last else None)

    @pl.when(step > 0)
    def _():
        multiply(totals)

    if last:

        @pl.when(step == pl.num_programs(0) - 1)
        def _():
            scale = lax.rsqrt(square[...] / D + 1e-06)
            scale = jnp.transpose(jnp.broadcast_to(scale, (tokens, tokens)))[:1]
            chosen = [jnp.zeros((units, tokens), jnp.float32) for _ in range(TOP)]
            for expert in range(experts):
                gate_values = totals[0, expert * units : (expert + 1) * units] * scale
                up_values = totals[1, expert * units : (expert + 1) * units] * scale
                activation = gate_values / (1.0 + jnp.exp(-gate_values)) * up_values
                for k in range(TOP):
                    chosen[k] = jnp.where(routes_ref[k : k + 1] == expert, activation, chosen[k])
            for k in range(TOP):
                out_ref[k * units : (k + 1) * units] = chosen[k].astype(out_ref.dtype)


def down(parts, scalar_ref, activation_ref, routes_ref, route_weight_ref, start_ref, *refs):
    half_refs = refs[:parts], refs[parts : 2 * parts]
    out_ref, turned, mixed = refs[2 * parts :]
    step = pl.program_id(0)
    per_part, blocks, _, units, columns = refs[0].shape

    @pl.when(step == 0)
    def _():
        for half in range(2):
            for k in range(TOP):
                part = activation_ref[blocks * half : blocks * (half + 1), k * units : (k + 1) * units]
                part = part.reshape(blocks * units, part.shape[2]).astype(jnp.float32)
                turned[half, k] = jnp.transpose(part).astype(turned.dtype)
        mixed[...] = start_ref[...]

    for part in range(parts):
        for place in range(per_part):
            expert = (step * parts + part) * per_part + place
            here = [routes_ref[:, k : k + 1] == expert for k in range(TOP)]
            share = sum(jnp.where(here[k], route_weight_ref[:, k : k + 1], 0.0) for k in range(TOP))
            masks = [here[k].astype(jnp.bfloat16) for k in range(TOP)]
            total = jnp.zeros(mixed.shape, jnp.float32)
            for half in range(2):
                rows = sum(turned[half, k] * masks[k] for k in range(TOP))
                weight = half_refs[half][part][place].reshape(blocks * units, columns)
                total += jnp.dot(rows, weight, preferred_element_type=jnp.float32)
            mixed[...] += total * share

    @pl.when(step == pl.num_programs(0) - 1)
    def _():
        out_ref[...] = mixed[...].astype(out_ref.dtype)


SCALAR = pl.BlockSpec(memory_space=pltpu.SMEM)
HERE = pl.BlockSpec(memory_space=pltpu.VMEM)
LIMIT = pltpu.CompilerParams(vmem_limit_bytes=32 * 1024 * 1024)
LARGE = pltpu.CompilerParams(vmem_limit_bytes=52 * 1024 * 1024)
WIDE = pltpu.CompilerParams(vmem_limit_bytes=56 * 1024 * 1024)


def whole(*shape):
    return pl.BlockSpec(shape, lambda i, *_: (0,) * len(shape))


def cost(flops, size):
    return pl.CostEstimate(flops=flops, bytes_accessed=size, transcendentals=0)


def exchange(message, axis, groups=None):
    return lax.all_to_all(
        message, axis, split_axis=0, concat_axis=0, tiled=True, axis_index_groups=groups
    )


def spread(rows, axis, count, groups=None):
    return exchange(jnp.broadcast_to(rows[None], (count,) + rows.shape), axis, groups)


def local(
    queries,
    all_key_rows,
    all_value_rows,
    out_weight,
    residual,
    post_gain,
    routes,
    route_weight,
    gate_weight,
    up_weight,
    down_weight,
):
    tokens = queries.shape[0]
    local_heads = queries.shape[1] // HEAD_WIDTH
    group_width = QUERY_HEADS // KEY_VALUE_HEADS
    tensor_count = lax.axis_size("tensor")
    expert_count = lax.axis_size("expert")
    tensor_index = lax.axis_index("tensor")
    expert_index = lax.axis_index("expert")
    core = lax.axis_index("dp")
    columns = D // tensor_count
    odd = (tensor_index % 2).astype(jnp.int32)
    core = core.astype(jnp.int32)
    hidden_units = down_weight.shape[1]
    half_units = hidden_units // 2
    local_units = gate_weight.shape[2]

    first_blocks = D // columns

    span = 1024
    gate_or_up = pl.pallas_call(
        pack,
        out_shape=jax.ShapeDtypeStruct((first_blocks * local_units, columns), jnp.bfloat16),
        grid_spec=pltpu.PrefetchScalarGridSpec(
            num_scalar_prefetch=1,
            grid=(D // span,),
            in_specs=[pl.BlockSpec((local_units, span), lambda i, core_ref: (0, i))] * 2,
            out_specs=pl.BlockSpec((span // columns * local_units, columns), lambda i, core_ref: (i, 0)),
        ),
        compiler_params=WIDE,
        name="pack",
    )(core.reshape(1), gate_weight[0].T, up_weight[0].T)
    down_half = lax.dynamic_slice_in_dim(down_weight[0], core * half_units, half_units, 0)

    shared = tensor_index * local_heads // group_width
    half_rows = out_weight.shape[0] // 2
    half_tokens = tokens // 2
    half_columns = columns // 2
    message_rows = half_rows + 2 * half_tokens
    half_spec = pl.BlockSpec(
        (half_tokens, HEAD_WIDTH), lambda i, core_ref, odd_ref, shared_ref: (odd_ref[0], shared_ref[0])
    )
    message = pl.pallas_call(
        compose,
        out_shape=jax.ShapeDtypeStruct((2 * expert_count, message_rows, half_columns), jnp.bfloat16),
        grid_spec=pltpu.PrefetchScalarGridSpec(
            num_scalar_prefetch=3,
            grid=(1,),
            in_specs=[
                pl.BlockSpec(
                    (half_rows, columns), lambda i, core_ref, odd_ref, shared_ref: (core_ref[0], 0)
                ),
                half_spec,
                half_spec,
            ],
            out_specs=HERE,
        ),
        compiler_params=LIMIT,
        name="compose",
    )(
        core.reshape(1),
        odd.reshape(1),
        shared.astype(jnp.int32).reshape(1),
        out_weight,
        all_key_rows,
        all_value_rows,
    )
    both = [
        [(2 * pair + side) * expert_count + place for side in range(2) for place in range(expert_count)]
        for pair in range(PAIRS)
    ]
    weights = lax.all_gather(gate_or_up, ("dp", "expert"), axis=0)
    down_weights = lax.all_gather(down_half, ("dp", "expert"), axis=0)
    gathered = exchange(message, ("tensor", "expert"), both)
    gathered_other = lax.ppermute(gathered, "dp", SWAP)

    attended = pl.pallas_call(
        attend,
        out_shape=jax.ShapeDtypeStruct((2, tokens, half_rows), jnp.bfloat16),
        grid=(1,),
        in_specs=[
            SCALAR,
            pl.BlockSpec((tokens, local_heads * HEAD_WIDTH), lambda i: (0, 0)),
            pl.BlockSpec(
                (2, expert_count, tokens, HEAD_WIDTH), lambda i: (0, 0, half_rows // tokens, 0)
            ),
        ],
        out_specs=pl.BlockSpec((2, tokens, half_rows), lambda i: (0, 0, 0)),
        compiler_params=WIDE,
        name="attend",
    )(
        expert_index.astype(jnp.int32).reshape(1),
        queries,
        gathered.reshape(2, expert_count, message_rows, half_columns),
    )

    attended_other = lax.ppermute(attended, "tensor", NEIGHBOUR)
    pair_shape = (2, PAIRS, 2, message_rows, half_columns)
    gathered, gathered_other = gathered.reshape(pair_shape), gathered_other.reshape(pair_shape)
    wide = 8

    def projected(source, rows, dtype, *before):
        weight_spec = pl.BlockSpec(
            (1, wide, 2, half_rows, half_columns),
            lambda i, core_ref, source_ref: (source_ref[0], i, 0, 0, 0),
        )
        return pl.pallas_call(
            functools.partial(project, bool(before)),
            out_shape=jax.ShapeDtypeStruct((PAIRS, tokens, columns), dtype),
            grid_spec=pltpu.PrefetchScalarGridSpec(
                num_scalar_prefetch=2,
                grid=(PAIRS // wide,),
                in_specs=[HERE, weight_spec, weight_spec] + [HERE] * len(before),
                out_specs=HERE,
            ),
            compiler_params=LIMIT,
            cost_estimate=cost(4 * tokens * half_rows * PAIRS * columns, 4 * half_rows * PAIRS * columns),
            name="project",
        )(core.reshape(1), source.reshape(1), rows, gathered, gathered_other, *before)

    kept = projected(odd, attended, jnp.float32)
    pair_sums = projected(1 - odd, attended_other, jnp.bfloat16, kept)
    partial_sums = exchange(pair_sums, "tensor", PARITY)
    head_total = jnp.sum(partial_sums.astype(jnp.float32), axis=0)
    pair_start = tensor_index // 2 * 2 * columns + odd * half_columns
    residual_share = jnp.concatenate(
        [
            lax.dynamic_slice_in_dim(residual, pair_start + side * columns, half_columns, 1)
            for side in range(2)
        ],
        axis=1,
    )
    hidden_share = residual_share.astype(jnp.float32) + head_total
    rows_own = spread(hidden_share.astype(jnp.bfloat16), "tensor", PAIRS, PARITY)
    rows_own, weights = lax.optimization_barrier((rows_own, weights))
    rows_other = lax.ppermute(rows_own, "tensor", NEIGHBOUR)
    weights = weights.reshape(2 * expert_count, PAIRS, 2, local_units, columns)

    per_step = 4
    gains = jnp.transpose(post_gain.reshape(PAIRS, 2, 2, half_columns), (0, 2, 1, 3)).reshape(
        PAIRS, 2, 1, columns
    )
    totals_types = [
        jax.ShapeDtypeStruct((2, expert_count * local_units, tokens), jnp.float32),
        jax.ShapeDtypeStruct((tokens, 1), jnp.float32),
    ]
    out_type = jax.ShapeDtypeStruct((TOP * local_units, tokens), jnp.bfloat16)

    def first_spec(which):
        return pl.BlockSpec(
            (expert_count, per_step, 1, local_units, columns),
            lambda i, parity_ref: (which, i, parity_ref[0], 0, 0),
        )

    def gated(parity, rows, *before):
        last = bool(before)
        scratch = [pltpu.VMEM((PAIRS, tokens, columns), jnp.bfloat16)]
        if last:
            scratch += [pltpu.VMEM(kind.shape, kind.dtype) for kind in totals_types]
        return pl.pallas_call(
            functools.partial(gate_up, last),
            out_shape=out_type if last else totals_types,
            grid_spec=pltpu.PrefetchScalarGridSpec(
                num_scalar_prefetch=1,
                grid=(PAIRS // per_step,),
                in_specs=[HERE, HERE, first_spec(0), first_spec(1)] + [HERE] * len(before),
                out_specs=HERE if last else [HERE] * 2,
                scratch_shapes=scratch,
            ),
            compiler_params=LIMIT,
            cost_estimate=cost(
                2 * tokens * 2 * expert_count * local_units * D // 2,
                2 * 2 * expert_count * local_units * D // 2,
            ),
            name="gate_up",
        )(parity.reshape(1), rows, gains, weights, weights, *before)

    before = gated(odd, rows_own)
    activation = gated(1 - odd, rows_other, *before, routes.T)

    activation_own = spread(activation, "tensor", PAIRS, PARITY)
    activation_other = lax.ppermute(activation_own, "tensor", NEIGHBOUR)
    parts = 2
    per_part = 4
    down_steps = expert_count // (parts * per_part)
    quarter = PAIRS // 2
    down_weights = down_weights.reshape(2 * expert_count, quarter, 2, local_units, columns)

    def down_spec(half, part):
        return pl.BlockSpec(
            (per_part, quarter, 1, local_units, columns),
            lambda i, scalar_ref: (
                (half * down_steps + i) * parts + part,
                0,
                scalar_ref[0],
                0,
                0,
            ),
        )

    def lowered(parity, rows, start, dtype):
        return pl.pallas_call(
            functools.partial(down, parts),
            out_shape=jax.ShapeDtypeStruct((tokens, columns), dtype),
            grid_spec=pltpu.PrefetchScalarGridSpec(
                num_scalar_prefetch=1,
                grid=(down_steps,),
                in_specs=[
                    whole(PAIRS, TOP * local_units, tokens),
                    whole(tokens, TOP),
                    whole(tokens, TOP),
                    whole(tokens, columns),
                ]
                + [down_spec(half, part) for half in range(2) for part in range(parts)],
                out_specs=whole(tokens, columns),
                scratch_shapes=[
                    pltpu.VMEM((2, TOP, tokens, quarter * local_units), jnp.bfloat16),
                    pltpu.VMEM((tokens, columns), jnp.float32),
                ],
            ),
            compiler_params=LARGE,
            cost_estimate=cost(
                2 * tokens * expert_count * hidden_units * columns // 2,
                2 * expert_count * hidden_units * columns // 2,
            ),
            name="down",
        )(parity.reshape(1), rows, routes, route_weight, start, *[down_weights] * (2 * parts))

    shares = [
        lax.dynamic_slice(
            rows, (tensor_index // 2, 0, odd * half_columns), (1, tokens, half_columns)
        )[0].astype(jnp.float32)
        for rows in (rows_own, rows_other)
    ]
    hidden_here = jnp.where(
        odd == 0, jnp.concatenate(shares, axis=1), jnp.concatenate(shares[::-1], axis=1)
    )
    mixed = lowered(odd, activation_own, hidden_here, jnp.float32)
    return lowered(1 - odd, activation_other, mixed, jnp.bfloat16)


def solution(mesh):
    return jax.shard_map(
        local,
        mesh=mesh,
        in_specs=(
            P(("dp", "expert"), "tensor"),
            P(("dp", "expert"), None),
            P(("dp", "expert"), None),
            P("tensor", "expert"),
            P(("dp", "expert"), None),
            P(),
            P(("dp", "expert"), None),
            P(("dp", "expert"), None),
            P("expert", None, "tensor"),
            P("expert", None, "tensor"),
            P("expert", None, "tensor"),
        ),
        out_specs=P(("dp", "expert"), "tensor"),
        check_vma=False,
    )
```

```python
import functools

import jax
import jax.numpy as jnp
from jax import lax
from jax.experimental import pallas as pl
from jax.experimental.pallas import tpu as pltpu
from jax.sharding import PartitionSpec as P

D = 4096
QUERY_HEADS = 64
KEY_VALUE_HEADS = 4
HEAD_WIDTH = 128
TOP = 2
PAIRS = 8
SWAP = [(0, 1), (1, 0)]
NEIGHBOUR = [(i, i ^ 1) for i in range(2 * PAIRS)]
PARITY = [[2 * pair + odd for pair in range(PAIRS)] for odd in range(2)]
CHUNK = 1024
LOG2_E = 1.4426950408889634


CONTRACT_LAST = (((1,), (1,)), ((), ()))


def pack(core_ref, gate_ref, up_ref, out_ref):
    units = gate_ref.shape[0]
    columns = out_ref.shape[1]
    half = columns // 2

    def store(source_ref):
        for pair in range(gate_ref.shape[1] // (2 * columns)):
            for odd in range(2):
                row = (2 * pair + odd) * units
                for side in range(2):
                    start = (2 * pair + side) * columns + odd * half
                    out_ref[row : row + units, side * half : (side + 1) * half] = source_ref[
                        :, start : start + half
                    ]

    @pl.when(core_ref[0] == 0)
    def _():
        store(gate_ref)

    @pl.when(core_ref[0] != 0)
    def _():
        store(up_ref)


def compose(core_ref, odd_ref, shared_ref, weight_ref, key_ref, value_ref, out_ref):
    rows = weight_ref.shape[0]
    half = key_ref.shape[0]
    places = out_ref.shape[0] // 2
    width = out_ref.shape[2]
    for side in range(2):
        for place in range(side * places, (side + 1) * places):
            out_ref[place, :rows] = weight_ref[:, side * width : (side + 1) * width]
            out_ref[place, rows : rows + half] = key_ref[...]
            out_ref[place, rows + half :] = value_ref[...]


def attend(place_ref, query_ref, piece_ref, out_ref):
    tokens = query_ref.shape[0]
    heads = query_ref.shape[1] // HEAD_WIDTH
    rows = heads * tokens
    half = tokens // 2
    blocks = CHUNK // tokens
    place = place_ref[0]
    rate = HEAD_WIDTH ** (-0.5) * LOG2_E
    stacked = jnp.concatenate(
        [query_ref[:, HEAD_WIDTH * h : HEAD_WIDTH * (h + 1)] for h in range(heads)], axis=0
    )

    def take(step, carry, masked):
        row_max, total, summed = carry
        place_here = pl.ds(step * blocks, blocks)
        keys = piece_ref[:, place_here, :half].reshape(CHUNK, HEAD_WIDTH)
        values = piece_ref[:, place_here, half:].reshape(CHUNK, HEAD_WIDTH)
        scores = lax.dot_general(
            stacked, keys, CONTRACT_LAST, preferred_element_type=jnp.float32
        )
        if masked:
            token = lax.broadcasted_iota(jnp.int32, (rows, 1), 0) % tokens + place * tokens
            key = lax.broadcasted_iota(jnp.int32, (1, CHUNK), 1)
            odd_half, rest = key // (blocks * half), key % (blocks * half)
            key_place = (step * blocks + rest // half) * tokens + odd_half * half + rest % half
            scores = jnp.where(token >= key_place, scores, -1e30)
        new_max = jnp.maximum(row_max, jnp.max(scores, axis=1, keepdims=True))
        shrink = jnp.exp2((row_max - new_max) * rate)
        exponent = jnp.exp2((scores - new_max) * rate)
        total = total * shrink + jnp.sum(exponent, axis=1, keepdims=True)
        summed = summed * shrink + jnp.dot(
            exponent.astype(jnp.bfloat16), values, preferred_element_type=jnp.float32
        )
        return new_max, total, summed

    full = place // blocks
    carry = (
        jnp.full((rows, 1), -1e30, jnp.float32),
        jnp.zeros((rows, 1), jnp.float32),
        jnp.zeros((rows, HEAD_WIDTH), jnp.float32),
    )
    carry = lax.fori_loop(0, full, lambda step, held: take(step, held, False), carry)
    _, total, summed = take(full, carry, True)
    attended = (summed / total).astype(out_ref.dtype)
    halves = heads // 2
    for h in range(heads):
        out_ref[h // halves, :, HEAD_WIDTH * (h % halves) : HEAD_WIDTH * (h % halves + 1)] = (
            attended[tokens * h : tokens * (h + 1)]
        )


def project(last, core_ref, source_ref, attended_ref, own_ref, other_ref, *refs):
    core = core_ref[0]
    out_ref = refs[-1]
    for block in range(own_ref.shape[1]):
        own = jnp.concatenate([own_ref[0, block, 0], own_ref[0, block, 1]], axis=1)
        other = jnp.concatenate([other_ref[0, block, 0], other_ref[0, block, 1]], axis=1)
        total = jnp.dot(attended_ref[core], own, preferred_element_type=jnp.float32) + jnp.dot(
            attended_ref[1 - core], other, preferred_element_type=jnp.float32
        )
        if last:
            total += refs[0][block]
        out_ref[block] = total.astype(out_ref.dtype)


def gate_up(last, scalar_ref, rows_ref, gain_ref, gate_ref, up_ref, *refs):
    if last:
        before, before_square, routes_ref, out_ref, scaled, totals, square = refs
    else:
        totals, square, scaled = refs
    step = pl.program_id(0)
    experts, per_step, _, units, columns = gate_ref.shape
    pieces, tokens, _ = rows_ref.shape
    together = 2 * units

    @pl.when(step == 0)
    def _():
        squares = jnp.zeros((tokens, columns), jnp.float32)
        for piece in range(pieces):
            rows = rows_ref[piece].astype(jnp.float32)
            squares += rows * rows
            scaled[piece] = (rows * gain_ref[piece, scalar_ref[0]]).astype(jnp.bfloat16)
        sums = jnp.sum(squares, axis=1, keepdims=True)
        square[...] = before_square[...] + sums if last else sums

    def multiply(start):
        for which, weight_ref in enumerate((gate_ref, up_ref)):
            for expert in range(0, experts, 2):
                place = pl.ds(expert * units, together)
                product = None if start is None else start[which, place]
                for piece in range(per_step):
                    part = lax.dot_general(
                        weight_ref[expert : expert + 2, piece, 0].reshape(together, columns),
                        scaled[step * per_step + piece],
                        CONTRACT_LAST,
                        preferred_element_type=jnp.float32,
                    )
                    product = part if product is None else product + part
                totals[which, place] = product

    @pl.when(step == 0)
    def _():
        multiply(before if last else None)

    @pl.when(step > 0)
    def _():
        multiply(totals)

    if last:

        @pl.when(step == pl.num_programs(0) - 1)
        def _():
            scale = lax.rsqrt(square[...] / D + 1e-06)
            scale = jnp.transpose(jnp.broadcast_to(scale, (tokens, tokens)))[:1]
            chosen = [jnp.zeros((units, tokens), jnp.float32) for _ in range(TOP)]
            for expert in range(experts):
                gate_values = totals[0, expert * units : (expert + 1) * units] * scale
                up_values = totals[1, expert * units : (expert + 1) * units] * scale
                activation = gate_values / (1.0 + jnp.exp(-gate_values)) * up_values
                for k in range(TOP):
                    chosen[k] = jnp.where(routes_ref[k : k + 1] == expert, activation, chosen[k])
            for k in range(TOP):
                out_ref[k * units : (k + 1) * units] = chosen[k].astype(out_ref.dtype)


def down(
    parts, odd_ref, own_ref, neighbour_ref, routes_ref, route_weight_ref, hidden_ref, *refs
):
    half_refs = refs[:parts], refs[parts : 2 * parts]
    out_ref, turned, mixed = refs[2 * parts :]
    step = pl.program_id(0)
    per_part, blocks, _, units, columns = refs[0].shape

    @pl.when(step == 0)
    def _():
        for which, activation_ref in enumerate((own_ref, neighbour_ref)):
            for half in range(2):
                for k in range(TOP):
                    place = pl.ds(blocks * half, blocks)
                    part = activation_ref[place, k * units : (k + 1) * units]
                    part = part.reshape(blocks * units, part.shape[2]).astype(jnp.float32)
                    turned[which, half, k] = jnp.transpose(part).astype(turned.dtype)
        mixed[...] = hidden_ref[...]

    parities = odd_ref[0], 1 - odd_ref[0]
    for part in range(parts):
        for place in range(per_part):
            expert = (step * parts + part) * per_part + place
            here = [routes_ref[:, k : k + 1] == expert for k in range(TOP)]
            share = sum(jnp.where(here[k], route_weight_ref[:, k : k + 1], 0.0) for k in range(TOP))
            masks = [here[k].astype(jnp.bfloat16) for k in range(TOP)]
            total = jnp.zeros(mixed.shape, jnp.float32)
            for half in range(2):
                for which, parity in enumerate(parities):
                    rows = sum(turned[which, half, k] * masks[k] for k in range(TOP))
                    weight = half_refs[half][part][place, :, parity].reshape(blocks * units, columns)
                    total += jnp.dot(rows, weight, preferred_element_type=jnp.float32)
            mixed[...] += total * share

    @pl.when(step == pl.num_programs(0) - 1)
    def _():
        out_ref[...] = mixed[...].astype(out_ref.dtype)


SCALAR = pl.BlockSpec(memory_space=pltpu.SMEM)
HERE = pl.BlockSpec(memory_space=pltpu.VMEM)
LIMIT = pltpu.CompilerParams(vmem_limit_bytes=32 * 1024 * 1024)
LARGE = pltpu.CompilerParams(vmem_limit_bytes=52 * 1024 * 1024)
WIDE = pltpu.CompilerParams(vmem_limit_bytes=56 * 1024 * 1024)


def whole(*shape):
    return pl.BlockSpec(shape, lambda i, *_: (0,) * len(shape))


def cost(flops, size):
    return pl.CostEstimate(flops=flops, bytes_accessed=size, transcendentals=0)


def exchange(message, axis, groups=None):
    return lax.all_to_all(
        message, axis, split_axis=0, concat_axis=0, tiled=True, axis_index_groups=groups
    )


def spread(rows, axis, count, groups=None):
    return exchange(jnp.broadcast_to(rows[None], (count,) + rows.shape), axis, groups)


def local(
    queries,
    all_key_rows,
    all_value_rows,
    out_weight,
    residual,
    post_gain,
    routes,
    route_weight,
    gate_weight,
    up_weight,
    down_weight,
):
    tokens = queries.shape[0]
    local_heads = queries.shape[1] // HEAD_WIDTH
    group_width = QUERY_HEADS // KEY_VALUE_HEADS
    tensor_count = lax.axis_size("tensor")
    expert_count = lax.axis_size("expert")
    tensor_index = lax.axis_index("tensor")
    expert_index = lax.axis_index("expert")
    core = lax.axis_index("dp")
    columns = D // tensor_count
    odd = (tensor_index % 2).astype(jnp.int32)
    core = core.astype(jnp.int32)
    hidden_units = down_weight.shape[1]
    half_units = hidden_units // 2
    local_units = gate_weight.shape[2]

    first_blocks = D // columns

    span = 2048
    gate_or_up = pl.pallas_call(
        pack,
        out_shape=jax.ShapeDtypeStruct((first_blocks * local_units, columns), jnp.bfloat16),
        grid_spec=pltpu.PrefetchScalarGridSpec(
            num_scalar_prefetch=1,
            grid=(D // span,),
            in_specs=[
                pl.BlockSpec((local_units, span), lambda i, core_ref: (0, i * (1 - core_ref[0]))),
                pl.BlockSpec((local_units, span), lambda i, core_ref: (0, i * core_ref[0])),
            ],
            out_specs=pl.BlockSpec((span // columns * local_units, columns), lambda i, core_ref: (i, 0)),
        ),
        compiler_params=WIDE,
        name="pack",
    )(core.reshape(1), gate_weight[0].T, up_weight[0].T)
    down_half = lax.dynamic_slice_in_dim(down_weight[0], core * half_units, half_units, 0)

    shared = tensor_index * local_heads // group_width
    half_rows = out_weight.shape[0] // 2
    half_tokens = tokens // 2
    half_columns = columns // 2
    message_rows = half_rows + 2 * half_tokens
    half_spec = pl.BlockSpec(
        (half_tokens, HEAD_WIDTH), lambda i, core_ref, odd_ref, shared_ref: (odd_ref[0], shared_ref[0])
    )
    message = pl.pallas_call(
        compose,
        out_shape=jax.ShapeDtypeStruct((2 * expert_count, message_rows, half_columns), jnp.bfloat16),
        grid_spec=pltpu.PrefetchScalarGridSpec(
            num_scalar_prefetch=3,
            grid=(1,),
            in_specs=[
                pl.BlockSpec(
                    (half_rows, columns), lambda i, core_ref, odd_ref, shared_ref: (core_ref[0], 0)
                ),
                half_spec,
                half_spec,
            ],
            out_specs=HERE,
        ),
        compiler_params=LIMIT,
        name="compose",
    )(
        core.reshape(1),
        odd.reshape(1),
        shared.astype(jnp.int32).reshape(1),
        out_weight,
        all_key_rows,
        all_value_rows,
    )
    both = [
        [(2 * pair + side) * expert_count + place for side in range(2) for place in range(expert_count)]
        for pair in range(PAIRS)
    ]
    weights = lax.all_gather(gate_or_up, ("dp", "expert"), axis=0)
    down_weights = lax.all_gather(down_half, ("dp", "expert"), axis=0)
    gathered = exchange(message, ("tensor", "expert"), both)
    gathered_other = lax.ppermute(gathered, "dp", SWAP)

    attended = pl.pallas_call(
        attend,
        out_shape=jax.ShapeDtypeStruct((2, tokens, half_rows), jnp.bfloat16),
        grid=(1,),
        in_specs=[
            SCALAR,
            pl.BlockSpec((tokens, local_heads * HEAD_WIDTH), lambda i: (0, 0)),
            pl.BlockSpec(
                (2, expert_count, tokens, HEAD_WIDTH), lambda i: (0, 0, half_rows // tokens, 0)
            ),
        ],
        out_specs=pl.BlockSpec((2, tokens, half_rows), lambda i: (0, 0, 0)),
        compiler_params=WIDE,
        name="attend",
    )(
        expert_index.astype(jnp.int32).reshape(1),
        queries,
        gathered.reshape(2, expert_count, message_rows, half_columns),
    )

    attended_other = lax.ppermute(attended, "tensor", NEIGHBOUR)
    pair_shape = (2, PAIRS, 2, message_rows, half_columns)
    gathered, gathered_other = gathered.reshape(pair_shape), gathered_other.reshape(pair_shape)
    wide = 8

    def projected(source, rows, dtype, *before):
        weight_spec = pl.BlockSpec(
            (1, wide, 2, half_rows, half_columns),
            lambda i, core_ref, source_ref: (source_ref[0], i, 0, 0, 0),
        )
        return pl.pallas_call(
            functools.partial(project, bool(before)),
            out_shape=jax.ShapeDtypeStruct((PAIRS, tokens, columns), dtype),
            grid_spec=pltpu.PrefetchScalarGridSpec(
                num_scalar_prefetch=2,
                grid=(PAIRS // wide,),
                in_specs=[HERE, weight_spec, weight_spec] + [HERE] * len(before),
                out_specs=HERE,
            ),
            compiler_params=LIMIT,
            cost_estimate=cost(4 * tokens * half_rows * PAIRS * columns, 4 * half_rows * PAIRS * columns),
            name="project",
        )(core.reshape(1), source.reshape(1), rows, gathered, gathered_other, *before)

    kept = projected(odd, attended, jnp.float32)
    pair_sums = projected(1 - odd, attended_other, jnp.bfloat16, kept)
    partial_sums = exchange(pair_sums, "tensor", PARITY)
    head_total = jnp.sum(partial_sums.astype(jnp.float32), axis=0)
    pair_start = tensor_index // 2 * 2 * columns + odd * half_columns
    residual_share = jnp.concatenate(
        [
            lax.dynamic_slice_in_dim(residual, pair_start + side * columns, half_columns, 1)
            for side in range(2)
        ],
        axis=1,
    )
    hidden_share = residual_share.astype(jnp.float32) + head_total
    rows_own = spread(hidden_share.astype(jnp.bfloat16), "tensor", PAIRS, PARITY)
    rows_own, weights = lax.optimization_barrier((rows_own, weights))
    rows_other = lax.ppermute(rows_own, "tensor", NEIGHBOUR)
    weights = weights.reshape(2 * expert_count, PAIRS, 2, local_units, columns)

    per_step = 4
    gains = jnp.transpose(post_gain.reshape(PAIRS, 2, 2, half_columns), (0, 2, 1, 3)).reshape(
        PAIRS, 2, 1, columns
    )
    totals_types = [
        jax.ShapeDtypeStruct((2, expert_count * local_units, tokens), jnp.float32),
        jax.ShapeDtypeStruct((tokens, 1), jnp.float32),
    ]
    out_type = jax.ShapeDtypeStruct((TOP * local_units, tokens), jnp.bfloat16)

    def first_spec(which):
        return pl.BlockSpec(
            (expert_count, per_step, 1, local_units, columns),
            lambda i, parity_ref: (which, i, parity_ref[0], 0, 0),
        )

    def gated(parity, rows, *before):
        last = bool(before)
        scratch = [pltpu.VMEM((PAIRS, tokens, columns), jnp.bfloat16)]
        if last:
            scratch += [pltpu.VMEM(kind.shape, kind.dtype) for kind in totals_types]
        return pl.pallas_call(
            functools.partial(gate_up, last),
            out_shape=out_type if last else totals_types,
            grid_spec=pltpu.PrefetchScalarGridSpec(
                num_scalar_prefetch=1,
                grid=(PAIRS // per_step,),
                in_specs=[HERE, HERE, first_spec(0), first_spec(1)] + [HERE] * len(before),
                out_specs=HERE if last else [HERE] * 2,
                scratch_shapes=scratch,
            ),
            compiler_params=LIMIT,
            cost_estimate=cost(
                2 * tokens * 2 * expert_count * local_units * D // 2,
                2 * 2 * expert_count * local_units * D // 2,
            ),
            name="gate_up",
        )(parity.reshape(1), rows, gains, weights, weights, *before)

    before = gated(odd, rows_own)
    activation = gated(1 - odd, rows_other, *before, routes.T)

    activation_own = spread(activation, "tensor", PAIRS, PARITY)
    activation_other = lax.ppermute(activation_own, "tensor", NEIGHBOUR)
    parts = 2
    per_part = 2
    down_steps = expert_count // (parts * per_part)
    quarter = PAIRS // 2
    down_weights = down_weights.reshape(2 * expert_count, quarter, 2, local_units, columns)

    def down_spec(half, part):
        return pl.BlockSpec(
            (per_part, quarter, 2, local_units, columns),
            lambda i, odd_ref: ((half * down_steps + i) * parts + part, 0, 0, 0, 0),
        )

    shares = [
        lax.dynamic_slice(
            rows, (tensor_index // 2, 0, odd * half_columns), (1, tokens, half_columns)
        )[0].astype(jnp.float32)
        for rows in (rows_own, rows_other)
    ]
    hidden_here = jnp.where(
        odd == 0, jnp.concatenate(shares, axis=1), jnp.concatenate(shares[::-1], axis=1)
    )
    return pl.pallas_call(
        functools.partial(down, parts),
        out_shape=jax.ShapeDtypeStruct((tokens, columns), jnp.bfloat16),
        grid_spec=pltpu.PrefetchScalarGridSpec(
            num_scalar_prefetch=1,
            grid=(down_steps,),
            in_specs=[HERE] * 5
            + [down_spec(half, part) for half in range(2) for part in range(parts)],
            out_specs=whole(tokens, columns),
            scratch_shapes=[
                pltpu.VMEM((2, 2, TOP, tokens, quarter * local_units), jnp.bfloat16),
                pltpu.VMEM((tokens, columns), jnp.float32),
            ],
        ),
        compiler_params=LARGE,
        cost_estimate=cost(
            2 * tokens * expert_count * hidden_units * columns,
            2 * expert_count * hidden_units * columns,
        ),
        name="down",
    )(
        odd.reshape(1),
        activation_own,
        activation_other,
        routes,
        route_weight,
        hidden_here,
        *[down_weights] * (2 * parts),
    )


def solution(mesh):
    return jax.shard_map(
        local,
        mesh=mesh,
        in_specs=(
            P(("dp", "expert"), "tensor"),
            P(("dp", "expert"), None),
            P(("dp", "expert"), None),
            P("tensor", "expert"),
            P(("dp", "expert"), None),
            P(),
            P(("dp", "expert"), None),
            P(("dp", "expert"), None),
            P("expert", None, "tensor"),
            P("expert", None, "tensor"),
            P("expert", None, "tensor"),
        ),
        out_specs=P(("dp", "expert"), "tensor"),
        check_vma=False,
    )
```

```python
import functools

import jax
import jax.numpy as jnp
from jax import lax
from jax.experimental import pallas as pl
from jax.experimental.pallas import tpu as pltpu
from jax.sharding import PartitionSpec as P

D = 4096
QUERY_HEADS = 64
KEY_VALUE_HEADS = 4
HEAD_WIDTH = 128
TOP = 2
PAIRS = 8
SWAP = [(0, 1), (1, 0)]
NEIGHBOUR = [(i, i ^ 1) for i in range(2 * PAIRS)]
PARITY = [[2 * pair + odd for pair in range(PAIRS)] for odd in range(2)]
CHUNK = 1024
LOG2_E = 1.4426950408889634


CONTRACT_LAST = (((1,), (1,)), ((), ()))


def pack(core_ref, gate_ref, up_ref, out_ref):
    units = gate_ref.shape[0]
    columns = out_ref.shape[1]
    half = columns // 2

    def store(source_ref):
        for pair in range(gate_ref.shape[1] // (2 * columns)):
            for odd in range(2):
                row = (2 * pair + odd) * units
                for side in range(2):
                    start = (2 * pair + side) * columns + odd * half
                    out_ref[row : row + units, side * half : (side + 1) * half] = source_ref[
                        :, start : start + half
                    ]

    @pl.when(core_ref[0] == 0)
    def _():
        store(gate_ref)

    @pl.when(core_ref[0] != 0)
    def _():
        store(up_ref)


def compose(core_ref, odd_ref, shared_ref, weight_ref, key_ref, value_ref, out_ref):
    rows = weight_ref.shape[0]
    half = key_ref.shape[0]
    places = out_ref.shape[0] // 2
    width = out_ref.shape[2]
    for side in range(2):
        for place in range(side * places, (side + 1) * places):
            out_ref[place, :rows] = weight_ref[:, side * width : (side + 1) * width]
            out_ref[place, rows : rows + half] = key_ref[...]
            out_ref[place, rows + half :] = value_ref[...]


def attend(place_ref, query_ref, piece_ref, out_ref):
    tokens = query_ref.shape[0]
    heads = query_ref.shape[1] // HEAD_WIDTH
    rows = heads * tokens
    half = tokens // 2
    blocks = CHUNK // tokens
    place = place_ref[0]
    rate = HEAD_WIDTH ** (-0.5) * LOG2_E
    stacked = jnp.concatenate(
        [query_ref[:, HEAD_WIDTH * h : HEAD_WIDTH * (h + 1)] for h in range(heads)], axis=0
    )

    def take(step, carry, masked):
        row_max, total, summed = carry
        place_here = pl.ds(step * blocks, blocks)
        keys = piece_ref[:, place_here, :half].reshape(CHUNK, HEAD_WIDTH)
        values = piece_ref[:, place_here, half:].reshape(CHUNK, HEAD_WIDTH)
        scores = lax.dot_general(
            stacked, keys, CONTRACT_LAST, preferred_element_type=jnp.float32
        )
        if masked:
            token = lax.broadcasted_iota(jnp.int32, (rows, 1), 0) % tokens + place * tokens
            key = lax.broadcasted_iota(jnp.int32, (1, CHUNK), 1)
            odd_half, rest = key // (blocks * half), key % (blocks * half)
            key_place = (step * blocks + rest // half) * tokens + odd_half * half + rest % half
            scores = jnp.where(token >= key_place, scores, -1e30)
        new_max = jnp.maximum(row_max, jnp.max(scores, axis=1, keepdims=True))
        shrink = jnp.exp2((row_max - new_max) * rate)
        exponent = jnp.exp2((scores - new_max) * rate)
        total = total * shrink + jnp.sum(exponent, axis=1, keepdims=True)
        summed = summed * shrink + jnp.dot(
            exponent.astype(jnp.bfloat16), values, preferred_element_type=jnp.float32
        )
        return new_max, total, summed

    full = place // blocks
    carry = (
        jnp.full((rows, 1), -1e30, jnp.float32),
        jnp.zeros((rows, 1), jnp.float32),
        jnp.zeros((rows, HEAD_WIDTH), jnp.float32),
    )
    carry = lax.fori_loop(0, full, lambda step, held: take(step, held, False), carry)
    _, total, summed = take(full, carry, True)
    attended = (summed / total).astype(out_ref.dtype)
    halves = heads // 2
    for h in range(heads):
        out_ref[h // halves, :, HEAD_WIDTH * (h % halves) : HEAD_WIDTH * (h % halves + 1)] = (
            attended[tokens * h : tokens * (h + 1)]
        )


def project(last, core_ref, source_ref, attended_ref, own_ref, other_ref, *refs):
    core = core_ref[0]
    out_ref = refs[-1]
    for block in range(own_ref.shape[1]):
        own = jnp.concatenate([own_ref[0, block, 0], own_ref[0, block, 1]], axis=1)
        other = jnp.concatenate([other_ref[0, block, 0], other_ref[0, block, 1]], axis=1)
        total = jnp.dot(attended_ref[core], own, preferred_element_type=jnp.float32) + jnp.dot(
            attended_ref[1 - core], other, preferred_element_type=jnp.float32
        )
        if last:
            total += refs[0][block]
        out_ref[block] = total.astype(out_ref.dtype)


def gate_up(last, scalar_ref, rows_ref, gain_ref, gate_ref, up_ref, *refs):
    if last:
        before, before_square, routes_ref, out_ref, scaled, totals, square = refs
    else:
        totals, square, scaled = refs
    step = pl.program_id(0)
    experts, per_step, _, units, columns = gate_ref.shape
    pieces, tokens, _ = rows_ref.shape
    together = 2 * units

    @pl.when(step == 0)
    def _():
        squares = jnp.zeros((tokens, columns), jnp.float32)
        for piece in range(pieces):
            rows = rows_ref[piece].astype(jnp.float32)
            squares += rows * rows
            scaled[piece] = (rows * gain_ref[piece, scalar_ref[0]]).astype(jnp.bfloat16)
        sums = jnp.sum(squares, axis=1, keepdims=True)
        square[...] = before_square[...] + sums if last else sums

    def multiply(start):
        for which, weight_ref in enumerate((gate_ref, up_ref)):
            for expert in range(0, experts, 2):
                place = pl.ds(expert * units, together)
                product = None if start is None else start[which, place]
                for piece in range(per_step):
                    part = lax.dot_general(
                        weight_ref[expert : expert + 2, piece, 0].reshape(together, columns),
                        scaled[step * per_step + piece],
                        CONTRACT_LAST,
                        preferred_element_type=jnp.float32,
                    )
                    product = part if product is None else product + part
                totals[which, place] = product

    @pl.when(step == 0)
    def _():
        multiply(before if last else None)

    @pl.when(step > 0)
    def _():
        multiply(totals)

    if last:

        @pl.when(step == pl.num_programs(0) - 1)
        def _():
            scale = lax.rsqrt(square[...] / D + 1e-06)
            scale = jnp.transpose(jnp.broadcast_to(scale, (tokens, tokens)))[:1]
            chosen = [jnp.zeros((units, tokens), jnp.float32) for _ in range(TOP)]
            for expert in range(experts):
                gate_values = totals[0, expert * units : (expert + 1) * units] * scale
                up_values = totals[1, expert * units : (expert + 1) * units] * scale
                activation = gate_values / (1.0 + jnp.exp(-gate_values)) * up_values
                for k in range(TOP):
                    chosen[k] = jnp.where(routes_ref[k : k + 1] == expert, activation, chosen[k])
            for k in range(TOP):
                out_ref[k * units : (k + 1) * units] = chosen[k].astype(out_ref.dtype)


def turn(activation_ref, out_ref):
    units = activation_ref.shape[1] // TOP
    blocks = activation_ref.shape[0] // 2
    for half in range(2):
        for k in range(TOP):
            part = activation_ref[blocks * half : blocks * (half + 1), k * units : (k + 1) * units]
            part = part.reshape(blocks * units, part.shape[2]).astype(jnp.float32)
            out_ref[half, k] = jnp.transpose(part).astype(out_ref.dtype)


def down(ready, parts, scalar_ref, activation_ref, routes_ref, route_weight_ref, start_ref, *refs):
    half_refs = refs[:parts], refs[parts : 2 * parts]
    out_ref, mixed = refs[2 * parts : 2 * parts + 2]
    turned = activation_ref if ready else refs[-1]
    step = pl.program_id(0)
    per_part, blocks, _, units, columns = refs[0].shape

    @pl.when(step == 0)
    def _():
        if not ready:
            turn(activation_ref, turned)
        mixed[...] = start_ref[...]

    for part in range(parts):
        for place in range(per_part):
            expert = (step * parts + part) * per_part + place
            here = [routes_ref[:, k : k + 1] == expert for k in range(TOP)]
            share = sum(jnp.where(here[k], route_weight_ref[:, k : k + 1], 0.0) for k in range(TOP))
            masks = [here[k].astype(jnp.bfloat16) for k in range(TOP)]
            total = jnp.zeros(mixed.shape, jnp.float32)
            for half in range(2):
                rows = sum(turned[half, k] * masks[k] for k in range(TOP))
                weight = half_refs[half][part][place].reshape(blocks * units, columns)
                total += jnp.dot(rows, weight, preferred_element_type=jnp.float32)
            mixed[...] += total * share

    @pl.when(step == pl.num_programs(0) - 1)
    def _():
        out_ref[...] = mixed[...].astype(out_ref.dtype)


SCALAR = pl.BlockSpec(memory_space=pltpu.SMEM)
HERE = pl.BlockSpec(memory_space=pltpu.VMEM)
LIMIT = pltpu.CompilerParams(vmem_limit_bytes=32 * 1024 * 1024)
LARGE = pltpu.CompilerParams(vmem_limit_bytes=52 * 1024 * 1024)
WIDE = pltpu.CompilerParams(vmem_limit_bytes=56 * 1024 * 1024)


def whole(*shape):
    return pl.BlockSpec(shape, lambda i, *_: (0,) * len(shape))


def cost(flops, size):
    return pl.CostEstimate(flops=flops, bytes_accessed=size, transcendentals=0)


def exchange(message, axis, groups=None):
    return lax.all_to_all(
        message, axis, split_axis=0, concat_axis=0, tiled=True, axis_index_groups=groups
    )


def spread(rows, axis, count, groups=None):
    return exchange(jnp.broadcast_to(rows[None], (count,) + rows.shape), axis, groups)


def local(
    queries,
    all_key_rows,
    all_value_rows,
    out_weight,
    residual,
    post_gain,
    routes,
    route_weight,
    gate_weight,
    up_weight,
    down_weight,
):
    tokens = queries.shape[0]
    local_heads = queries.shape[1] // HEAD_WIDTH
    group_width = QUERY_HEADS // KEY_VALUE_HEADS
    tensor_count = lax.axis_size("tensor")
    expert_count = lax.axis_size("expert")
    tensor_index = lax.axis_index("tensor")
    expert_index = lax.axis_index("expert")
    core = lax.axis_index("dp")
    columns = D // tensor_count
    odd = (tensor_index % 2).astype(jnp.int32)
    core = core.astype(jnp.int32)
    hidden_units = down_weight.shape[1]
    half_units = hidden_units // 2
    local_units = gate_weight.shape[2]

    first_blocks = D // columns

    span = 2048
    gate_or_up = pl.pallas_call(
        pack,
        out_shape=jax.ShapeDtypeStruct((first_blocks * local_units, columns), jnp.bfloat16),
        grid_spec=pltpu.PrefetchScalarGridSpec(
            num_scalar_prefetch=1,
            grid=(D // span,),
            in_specs=[
                pl.BlockSpec((local_units, span), lambda i, core_ref: (0, i * (1 - core_ref[0]))),
                pl.BlockSpec((local_units, span), lambda i, core_ref: (0, i * core_ref[0])),
            ],
            out_specs=pl.BlockSpec((span // columns * local_units, columns), lambda i, core_ref: (i, 0)),
        ),
        compiler_params=WIDE,
        name="pack",
    )(core.reshape(1), gate_weight[0].T, up_weight[0].T)
    down_half = lax.dynamic_slice_in_dim(down_weight[0], core * half_units, half_units, 0)

    shared = tensor_index * local_heads // group_width
    half_rows = out_weight.shape[0] // 2
    half_tokens = tokens // 2
    half_columns = columns // 2
    message_rows = half_rows + 2 * half_tokens
    half_spec = pl.BlockSpec(
        (half_tokens, HEAD_WIDTH), lambda i, core_ref, odd_ref, shared_ref: (odd_ref[0], shared_ref[0])
    )
    message = pl.pallas_call(
        compose,
        out_shape=jax.ShapeDtypeStruct((2 * expert_count, message_rows, half_columns), jnp.bfloat16),
        grid_spec=pltpu.PrefetchScalarGridSpec(
            num_scalar_prefetch=3,
            grid=(1,),
            in_specs=[
                pl.BlockSpec(
                    (half_rows, columns), lambda i, core_ref, odd_ref, shared_ref: (core_ref[0], 0)
                ),
                half_spec,
                half_spec,
            ],
            out_specs=HERE,
        ),
        compiler_params=LIMIT,
        name="compose",
    )(
        core.reshape(1),
        odd.reshape(1),
        shared.astype(jnp.int32).reshape(1),
        out_weight,
        all_key_rows,
        all_value_rows,
    )
    both = [
        [(2 * pair + side) * expert_count + place for side in range(2) for place in range(expert_count)]
        for pair in range(PAIRS)
    ]
    weights = lax.all_gather(gate_or_up, ("dp", "expert"), axis=0)
    down_weights = lax.all_gather(down_half, ("dp", "expert"), axis=0)
    gathered = exchange(message, ("tensor", "expert"), both)
    gathered_other = lax.ppermute(gathered, "dp", SWAP)

    attended = pl.pallas_call(
        attend,
        out_shape=jax.ShapeDtypeStruct((2, tokens, half_rows), jnp.bfloat16),
        grid=(1,),
        in_specs=[
            SCALAR,
            pl.BlockSpec((tokens, local_heads * HEAD_WIDTH), lambda i: (0, 0)),
            pl.BlockSpec(
                (2, expert_count, tokens, HEAD_WIDTH), lambda i: (0, 0, half_rows // tokens, 0)
            ),
        ],
        out_specs=pl.BlockSpec((2, tokens, half_rows), lambda i: (0, 0, 0)),
        compiler_params=WIDE,
        name="attend",
    )(
        expert_index.astype(jnp.int32).reshape(1),
        queries,
        gathered.reshape(2, expert_count, message_rows, half_columns),
    )

    attended_other = lax.ppermute(attended, "tensor", NEIGHBOUR)
    pair_shape = (2, PAIRS, 2, message_rows, half_columns)
    gathered, gathered_other = gathered.reshape(pair_shape), gathered_other.reshape(pair_shape)
    wide = 8

    def projected(source, rows, dtype, *before):
        weight_spec = pl.BlockSpec(
            (1, wide, 2, half_rows, half_columns),
            lambda i, core_ref, source_ref: (source_ref[0], i, 0, 0, 0),
        )
        return pl.pallas_call(
            functools.partial(project, bool(before)),
            out_shape=jax.ShapeDtypeStruct((PAIRS, tokens, columns), dtype),
            grid_spec=pltpu.PrefetchScalarGridSpec(
                num_scalar_prefetch=2,
                grid=(PAIRS // wide,),
                in_specs=[HERE, weight_spec, weight_spec] + [HERE] * len(before),
                out_specs=HERE,
            ),
            compiler_params=LIMIT,
            cost_estimate=cost(4 * tokens * half_rows * PAIRS * columns, 4 * half_rows * PAIRS * columns),
            name="project",
        )(core.reshape(1), source.reshape(1), rows, gathered, gathered_other, *before)

    kept = projected(odd, attended, jnp.float32)
    pair_sums = projected(1 - odd, attended_other, jnp.bfloat16, kept)
    partial_sums = exchange(pair_sums, "tensor", PARITY)
    head_total = jnp.sum(partial_sums.astype(jnp.float32), axis=0)
    pair_start = tensor_index // 2 * 2 * columns + odd * half_columns
    residual_share = jnp.concatenate(
        [
            lax.dynamic_slice_in_dim(residual, pair_start + side * columns, half_columns, 1)
            for side in range(2)
        ],
        axis=1,
    )
    hidden_share = residual_share.astype(jnp.float32) + head_total
    rows_own = spread(hidden_share.astype(jnp.bfloat16), "tensor", PAIRS, PARITY)
    rows_own, weights = lax.optimization_barrier((rows_own, weights))
    rows_other = lax.ppermute(rows_own, "tensor", NEIGHBOUR)
    weights = weights.reshape(2 * expert_count, PAIRS, 2, local_units, columns)

    per_step = 4
    gains = jnp.transpose(post_gain.reshape(PAIRS, 2, 2, half_columns), (0, 2, 1, 3)).reshape(
        PAIRS, 2, 1, columns
    )
    totals_types = [
        jax.ShapeDtypeStruct((2, expert_count * local_units, tokens), jnp.float32),
        jax.ShapeDtypeStruct((tokens, 1), jnp.float32),
    ]
    out_type = jax.ShapeDtypeStruct((TOP * local_units, tokens), jnp.bfloat16)

    def first_spec(which):
        return pl.BlockSpec(
            (expert_count, per_step, 1, local_units, columns),
            lambda i, parity_ref: (which, i, parity_ref[0], 0, 0),
        )

    def gated(parity, rows, *before):
        last = bool(before)
        scratch = [pltpu.VMEM((PAIRS, tokens, columns), jnp.bfloat16)]
        if last:
            scratch += [pltpu.VMEM(kind.shape, kind.dtype) for kind in totals_types]
        return pl.pallas_call(
            functools.partial(gate_up, last),
            out_shape=out_type if last else totals_types,
            grid_spec=pltpu.PrefetchScalarGridSpec(
                num_scalar_prefetch=1,
                grid=(PAIRS // per_step,),
                in_specs=[HERE, HERE, first_spec(0), first_spec(1)] + [HERE] * len(before),
                out_specs=HERE if last else [HERE] * 2,
                scratch_shapes=scratch,
            ),
            compiler_params=LIMIT,
            cost_estimate=cost(
                2 * tokens * 2 * expert_count * local_units * D // 2,
                2 * 2 * expert_count * local_units * D // 2,
            ),
            name="gate_up",
        )(parity.reshape(1), rows, gains, weights, weights, *before)

    before = gated(odd, rows_own)
    activation = gated(1 - odd, rows_other, *before, routes.T)

    activation_own = spread(activation, "tensor", PAIRS, PARITY)
    activation_other = lax.ppermute(activation_own, "tensor", NEIGHBOUR)
    parts = 2
    per_part = 4
    down_steps = expert_count // (parts * per_part)
    quarter = PAIRS // 2
    down_weights = down_weights.reshape(2 * expert_count, quarter, 2, local_units, columns)
    turned_type = jax.ShapeDtypeStruct((2, TOP, tokens, quarter * local_units), jnp.bfloat16)

    def down_spec(half, part):
        return pl.BlockSpec(
            (per_part, quarter, 1, local_units, columns),
            lambda i, parity_ref: ((half * down_steps + i) * parts + part, 0, parity_ref[0], 0, 0),
        )

    def lowered(ready, parity, rows, start, dtype):
        scratch = [pltpu.VMEM((tokens, columns), jnp.float32)]
        if not ready:
            scratch.append(pltpu.VMEM(turned_type.shape, turned_type.dtype))
        return pl.pallas_call(
            functools.partial(down, ready, parts),
            out_shape=jax.ShapeDtypeStruct((tokens, columns), dtype),
            grid_spec=pltpu.PrefetchScalarGridSpec(
                num_scalar_prefetch=1,
                grid=(down_steps,),
                in_specs=[HERE] * 4
                + [down_spec(half, part) for half in range(2) for part in range(parts)],
                out_specs=whole(tokens, columns),
                scratch_shapes=scratch,
            ),
            compiler_params=LARGE,
            cost_estimate=cost(
                tokens * expert_count * hidden_units * columns,
                expert_count * hidden_units * columns,
            ),
            name="down",
        )(parity.reshape(1), rows, routes, route_weight, start, *[down_weights] * (2 * parts))

    turned_own = pl.pallas_call(
        turn,
        out_shape=turned_type,
        in_specs=[HERE],
        out_specs=HERE,
        compiler_params=LIMIT,
        name="turn",
    )(activation_own)
    turned_own, down_weights = lax.optimization_barrier((turned_own, down_weights))

    shares = [
        lax.dynamic_slice(
            rows, (tensor_index // 2, 0, odd * half_columns), (1, tokens, half_columns)
        )[0].astype(jnp.float32)
        for rows in (rows_own, rows_other)
    ]
    hidden_here = jnp.where(
        odd == 0, jnp.concatenate(shares, axis=1), jnp.concatenate(shares[::-1], axis=1)
    )
    mixed = lowered(True, odd, turned_own, hidden_here, jnp.float32)
    return lowered(False, 1 - odd, activation_other, mixed, jnp.bfloat16)


def solution(mesh):
    return jax.shard_map(
        local,
        mesh=mesh,
        in_specs=(
            P(("dp", "expert"), "tensor"),
            P(("dp", "expert"), None),
            P(("dp", "expert"), None),
            P("tensor", "expert"),
            P(("dp", "expert"), None),
            P(),
            P(("dp", "expert"), None),
            P(("dp", "expert"), None),
            P("expert", None, "tensor"),
            P("expert", None, "tensor"),
            P("expert", None, "tensor"),
        ),
        out_specs=P(("dp", "expert"), "tensor"),
        check_vma=False,
    )
```

```python
import functools

import jax
import jax.numpy as jnp
from jax import lax
from jax.experimental import pallas as pl
from jax.experimental.pallas import tpu as pltpu
from jax.sharding import PartitionSpec as P

D = 4096
QUERY_HEADS = 64
KEY_VALUE_HEADS = 4
HEAD_WIDTH = 128
TOP = 2
PAIRS = 8
SWAP = [(0, 1), (1, 0)]
NEIGHBOUR = [(i, i ^ 1) for i in range(2 * PAIRS)]
PARITY = [[2 * pair + odd for pair in range(PAIRS)] for odd in range(2)]
CHUNK = 1024
LOG2_E = 1.4426950408889634


CONTRACT_LAST = (((1,), (1,)), ((), ()))


def pack(core_ref, gate_ref, up_ref, out_ref):
    units = gate_ref.shape[0]
    columns = out_ref.shape[1]
    half = columns // 2

    def store(source_ref):
        for pair in range(gate_ref.shape[1] // (2 * columns)):
            for odd in range(2):
                row = (2 * pair + odd) * units
                for side in range(2):
                    start = (2 * pair + side) * columns + odd * half
                    out_ref[row : row + units, side * half : (side + 1) * half] = source_ref[
                        :, start : start + half
                    ]

    @pl.when(core_ref[0] == 0)
    def _():
        store(gate_ref)

    @pl.when(core_ref[0] != 0)
    def _():
        store(up_ref)


def compose(core_ref, odd_ref, shared_ref, weight_ref, key_ref, value_ref, out_ref):
    rows = weight_ref.shape[0]
    half = key_ref.shape[0]
    places = out_ref.shape[0] // 2
    width = out_ref.shape[2]
    for side in range(2):
        for place in range(side * places, (side + 1) * places):
            out_ref[place, :rows] = weight_ref[:, side * width : (side + 1) * width]
            out_ref[place, rows : rows + half] = key_ref[...]
            out_ref[place, rows + half :] = value_ref[...]


def attend(place_ref, query_ref, piece_ref, out_ref):
    tokens = query_ref.shape[0]
    heads = query_ref.shape[1] // HEAD_WIDTH
    rows = heads * tokens
    half = tokens // 2
    blocks = CHUNK // tokens
    place = place_ref[0]
    rate = HEAD_WIDTH ** (-0.5) * LOG2_E
    stacked = jnp.concatenate(
        [query_ref[:, HEAD_WIDTH * h : HEAD_WIDTH * (h + 1)] for h in range(heads)], axis=0
    )

    def take(step, carry, masked):
        row_max, total, summed = carry
        place_here = pl.ds(step * blocks, blocks)
        keys = piece_ref[:, place_here, :half].reshape(CHUNK, HEAD_WIDTH)
        values = piece_ref[:, place_here, half:].reshape(CHUNK, HEAD_WIDTH)
        scores = lax.dot_general(
            stacked, keys, CONTRACT_LAST, preferred_element_type=jnp.float32
        )
        if masked:
            token = lax.broadcasted_iota(jnp.int32, (rows, 1), 0) % tokens + place * tokens
            key = lax.broadcasted_iota(jnp.int32, (1, CHUNK), 1)
            odd_half, rest = key // (blocks * half), key % (blocks * half)
            key_place = (step * blocks + rest // half) * tokens + odd_half * half + rest % half
            scores = jnp.where(token >= key_place, scores, -1e30)
        new_max = jnp.maximum(row_max, jnp.max(scores, axis=1, keepdims=True))
        shrink = jnp.exp2((row_max - new_max) * rate)
        exponent = jnp.exp2((scores - new_max) * rate)
        total = total * shrink + jnp.sum(exponent, axis=1, keepdims=True)
        summed = summed * shrink + jnp.dot(
            exponent.astype(jnp.bfloat16), values, preferred_element_type=jnp.float32
        )
        return new_max, total, summed

    full = place // blocks
    carry = (
        jnp.full((rows, 1), -1e30, jnp.float32),
        jnp.zeros((rows, 1), jnp.float32),
        jnp.zeros((rows, HEAD_WIDTH), jnp.float32),
    )
    carry = lax.fori_loop(0, full, lambda step, held: take(step, held, False), carry)
    _, total, summed = take(full, carry, True)
    attended = (summed / total).astype(out_ref.dtype)
    halves = heads // 2
    for h in range(heads):
        out_ref[h // halves, :, HEAD_WIDTH * (h % halves) : HEAD_WIDTH * (h % halves + 1)] = (
            attended[tokens * h : tokens * (h + 1)]
        )


def project(last, core_ref, source_ref, attended_ref, own_ref, other_ref, *refs):
    core = core_ref[0]
    out_ref = refs[-1]
    for block in range(own_ref.shape[1]):
        own = jnp.concatenate([own_ref[0, block, 0], own_ref[0, block, 1]], axis=1)
        other = jnp.concatenate([other_ref[0, block, 0], other_ref[0, block, 1]], axis=1)
        total = jnp.dot(attended_ref[core], own, preferred_element_type=jnp.float32) + jnp.dot(
            attended_ref[1 - core], other, preferred_element_type=jnp.float32
        )
        if last:
            total += refs[0][block]
        out_ref[block] = total.astype(out_ref.dtype)


def gate_up(last, scalar_ref, rows_ref, gain_ref, gate_ref, up_ref, *refs):
    if last:
        before, before_square, routes_ref, out_ref, scaled, totals, square = refs
    else:
        totals, square, scaled = refs
    step = pl.program_id(0)
    experts, _, per_step, _, units, columns = gate_ref.shape
    pieces, tokens, _ = rows_ref.shape
    together = 2 * units

    @pl.when(step == 0)
    def _():
        squares = jnp.zeros((tokens, columns), jnp.float32)
        for piece in range(pieces):
            rows = rows_ref[piece].astype(jnp.float32)
            squares += rows * rows
            scaled[piece] = (rows * gain_ref[piece, scalar_ref[0]]).astype(jnp.bfloat16)
        sums = jnp.sum(squares, axis=1, keepdims=True)
        square[...] = before_square[...] + sums if last else sums

    def multiply(start):
        for which, weight_ref in enumerate((gate_ref, up_ref)):
            for expert in range(0, experts, 2):
                place = pl.ds(expert * units, together)
                product = None if start is None else start[which, place]
                for piece in range(per_step):
                    part = lax.dot_general(
                        weight_ref[expert : expert + 2, 0, piece, 0].reshape(together, columns),
                        scaled[step * per_step + piece],
                        CONTRACT_LAST,
                        preferred_element_type=jnp.float32,
                    )
                    product = part if product is None else product + part
                totals[which, place] = product

    @pl.when(step == 0)
    def _():
        multiply(before if last else None)

    @pl.when(step > 0)
    def _():
        multiply(totals)

    if last:

        @pl.when(step == pl.num_programs(0) - 1)
        def _():
            scale = lax.rsqrt(square[...] / D + 1e-06)
            scale = jnp.transpose(jnp.broadcast_to(scale, (tokens, tokens)))[:1]
            chosen = [jnp.zeros((units, tokens), jnp.float32) for _ in range(TOP)]
            for expert in range(experts):
                gate_values = totals[0, expert * units : (expert + 1) * units] * scale
                up_values = totals[1, expert * units : (expert + 1) * units] * scale
                activation = gate_values / (1.0 + jnp.exp(-gate_values)) * up_values
                for k in range(TOP):
                    chosen[k] = jnp.where(routes_ref[k : k + 1] == expert, activation, chosen[k])
            for k in range(TOP):
                out_ref[k * units : (k + 1) * units] = chosen[k].astype(out_ref.dtype)


def turn(activation_ref, out_ref):
    units = activation_ref.shape[1] // TOP
    blocks = activation_ref.shape[0] // 2
    for half in range(2):
        for k in range(TOP):
            part = activation_ref[blocks * half : blocks * (half + 1), k * units : (k + 1) * units]
            part = part.reshape(blocks * units, part.shape[2]).astype(jnp.float32)
            out_ref[half, k] = jnp.transpose(part).astype(out_ref.dtype)


def down(ready, parts, scalar_ref, activation_ref, routes_ref, route_weight_ref, start_ref, *refs):
    half_refs = refs[:parts], refs[parts : 2 * parts]
    out_ref, mixed = refs[2 * parts : 2 * parts + 2]
    turned = activation_ref if ready else refs[-1]
    step = pl.program_id(0)
    per_part, _, blocks, _, units, columns = refs[0].shape

    @pl.when(step == 0)
    def _():
        if not ready:
            turn(activation_ref, turned)
        mixed[...] = start_ref[...]

    for part in range(parts):
        for place in range(per_part):
            expert = (step * parts + part) * per_part + place
            here = [routes_ref[:, k : k + 1] == expert for k in range(TOP)]
            share = sum(jnp.where(here[k], route_weight_ref[:, k : k + 1], 0.0) for k in range(TOP))
            masks = [here[k].astype(jnp.bfloat16) for k in range(TOP)]
            total = jnp.zeros(mixed.shape, jnp.float32)
            for half in range(2):
                rows = sum(turned[half, k] * masks[k] for k in range(TOP))
                weight = half_refs[half][part][place].reshape(blocks * units, columns)
                total += jnp.dot(rows, weight, preferred_element_type=jnp.float32)
            mixed[...] += total * share

    @pl.when(step == pl.num_programs(0) - 1)
    def _():
        out_ref[...] = mixed[...].astype(out_ref.dtype)


SCALAR = pl.BlockSpec(memory_space=pltpu.SMEM)
HERE = pl.BlockSpec(memory_space=pltpu.VMEM)
LIMIT = pltpu.CompilerParams(vmem_limit_bytes=32 * 1024 * 1024)
LARGE = pltpu.CompilerParams(vmem_limit_bytes=52 * 1024 * 1024)
WIDE = pltpu.CompilerParams(vmem_limit_bytes=56 * 1024 * 1024)


def whole(*shape):
    return pl.BlockSpec(shape, lambda i, *_: (0,) * len(shape))


def cost(flops, size):
    return pl.CostEstimate(flops=flops, bytes_accessed=size, transcendentals=0)


def exchange(message, axis, groups=None):
    return lax.all_to_all(
        message, axis, split_axis=0, concat_axis=0, tiled=True, axis_index_groups=groups
    )


def spread(rows, axis, count, groups=None):
    return exchange(jnp.broadcast_to(rows[None], (count,) + rows.shape), axis, groups)


def local(
    queries,
    all_key_rows,
    all_value_rows,
    out_weight,
    residual,
    post_gain,
    routes,
    route_weight,
    gate_weight,
    up_weight,
    down_weight,
):
    tokens = queries.shape[0]
    local_heads = queries.shape[1] // HEAD_WIDTH
    group_width = QUERY_HEADS // KEY_VALUE_HEADS
    tensor_count = lax.axis_size("tensor")
    expert_count = lax.axis_size("expert")
    tensor_index = lax.axis_index("tensor")
    expert_index = lax.axis_index("expert")
    core = lax.axis_index("dp")
    columns = D // tensor_count
    odd = (tensor_index % 2).astype(jnp.int32)
    core = core.astype(jnp.int32)
    hidden_units = down_weight.shape[1]
    half_units = hidden_units // 2
    local_units = gate_weight.shape[2]

    first_blocks = D // columns

    span = 2048
    gate_or_up = pl.pallas_call(
        pack,
        out_shape=jax.ShapeDtypeStruct((first_blocks * local_units, columns), jnp.bfloat16),
        grid_spec=pltpu.PrefetchScalarGridSpec(
            num_scalar_prefetch=1,
            grid=(D // span,),
            in_specs=[
                pl.BlockSpec((local_units, span), lambda i, core_ref: (0, i * (1 - core_ref[0]))),
                pl.BlockSpec((local_units, span), lambda i, core_ref: (0, i * core_ref[0])),
            ],
            out_specs=pl.BlockSpec((span // columns * local_units, columns), lambda i, core_ref: (i, 0)),
        ),
        compiler_params=WIDE,
        name="pack",
    )(core.reshape(1), gate_weight[0].T, up_weight[0].T)
    down_half = lax.dynamic_slice_in_dim(down_weight[0], core * half_units, half_units, 0)

    shared = tensor_index * local_heads // group_width
    half_rows = out_weight.shape[0] // 2
    half_tokens = tokens // 2
    half_columns = columns // 2
    message_rows = half_rows + 2 * half_tokens
    half_spec = pl.BlockSpec(
        (half_tokens, HEAD_WIDTH), lambda i, core_ref, odd_ref, shared_ref: (odd_ref[0], shared_ref[0])
    )
    message = pl.pallas_call(
        compose,
        out_shape=jax.ShapeDtypeStruct((2 * expert_count, message_rows, half_columns), jnp.bfloat16),
        grid_spec=pltpu.PrefetchScalarGridSpec(
            num_scalar_prefetch=3,
            grid=(1,),
            in_specs=[
                pl.BlockSpec(
                    (half_rows, columns), lambda i, core_ref, odd_ref, shared_ref: (core_ref[0], 0)
                ),
                half_spec,
                half_spec,
            ],
            out_specs=HERE,
        ),
        compiler_params=LIMIT,
        name="compose",
    )(
        core.reshape(1),
        odd.reshape(1),
        shared.astype(jnp.int32).reshape(1),
        out_weight,
        all_key_rows,
        all_value_rows,
    )
    both = [
        [(2 * pair + side) * expert_count + place for side in range(2) for place in range(expert_count)]
        for pair in range(PAIRS)
    ]
    weights = lax.all_gather(gate_or_up, ("expert", "dp"), axis=0)
    down_weights = lax.all_gather(down_half, ("expert", "dp"), axis=0)
    gathered = exchange(message, ("tensor", "expert"), both)
    gathered_other = lax.ppermute(gathered, "dp", SWAP)

    attended = pl.pallas_call(
        attend,
        out_shape=jax.ShapeDtypeStruct((2, tokens, half_rows), jnp.bfloat16),
        grid=(1,),
        in_specs=[
            SCALAR,
            pl.BlockSpec((tokens, local_heads * HEAD_WIDTH), lambda i: (0, 0)),
            pl.BlockSpec(
                (2, expert_count, tokens, HEAD_WIDTH), lambda i: (0, 0, half_rows // tokens, 0)
            ),
        ],
        out_specs=pl.BlockSpec((2, tokens, half_rows), lambda i: (0, 0, 0)),
        compiler_params=WIDE,
        name="attend",
    )(
        expert_index.astype(jnp.int32).reshape(1),
        queries,
        gathered.reshape(2, expert_count, message_rows, half_columns),
    )

    attended_other = lax.ppermute(attended, "tensor", NEIGHBOUR)
    pair_shape = (2, PAIRS, 2, message_rows, half_columns)
    gathered, gathered_other = gathered.reshape(pair_shape), gathered_other.reshape(pair_shape)
    wide = 8

    def projected(source, rows, dtype, *before):
        weight_spec = pl.BlockSpec(
            (1, wide, 2, half_rows, half_columns),
            lambda i, core_ref, source_ref: (source_ref[0], i, 0, 0, 0),
        )
        return pl.pallas_call(
            functools.partial(project, bool(before)),
            out_shape=jax.ShapeDtypeStruct((PAIRS, tokens, columns), dtype),
            grid_spec=pltpu.PrefetchScalarGridSpec(
                num_scalar_prefetch=2,
                grid=(PAIRS // wide,),
                in_specs=[HERE, weight_spec, weight_spec] + [HERE] * len(before),
                out_specs=HERE,
            ),
            compiler_params=LIMIT,
            cost_estimate=cost(4 * tokens * half_rows * PAIRS * columns, 4 * half_rows * PAIRS * columns),
            name="project",
        )(core.reshape(1), source.reshape(1), rows, gathered, gathered_other, *before)

    kept = projected(odd, attended, jnp.float32)
    pair_sums = projected(1 - odd, attended_other, jnp.bfloat16, kept)
    partial_sums = exchange(pair_sums, "tensor", PARITY)
    head_total = jnp.sum(partial_sums.astype(jnp.float32), axis=0)
    pair_start = tensor_index // 2 * 2 * columns + odd * half_columns
    residual_share = jnp.concatenate(
        [
            lax.dynamic_slice_in_dim(residual, pair_start + side * columns, half_columns, 1)
            for side in range(2)
        ],
        axis=1,
    )
    hidden_share = residual_share.astype(jnp.float32) + head_total
    rows_own = spread(hidden_share.astype(jnp.bfloat16), "tensor", PAIRS, PARITY)
    rows_own, weights = lax.optimization_barrier((rows_own, weights))
    rows_other = lax.ppermute(rows_own, "tensor", NEIGHBOUR)
    weights = weights.reshape(expert_count, 2, PAIRS, 2, local_units, columns)

    per_step = 4
    gains = jnp.transpose(post_gain.reshape(PAIRS, 2, 2, half_columns), (0, 2, 1, 3)).reshape(
        PAIRS, 2, 1, columns
    )
    totals_types = [
        jax.ShapeDtypeStruct((2, expert_count * local_units, tokens), jnp.float32),
        jax.ShapeDtypeStruct((tokens, 1), jnp.float32),
    ]
    out_type = jax.ShapeDtypeStruct((TOP * local_units, tokens), jnp.bfloat16)

    def first_spec(which):
        return pl.BlockSpec(
            (expert_count, 1, per_step, 1, local_units, columns),
            lambda i, parity_ref: (0, which, i, parity_ref[0], 0, 0),
        )

    def gated(parity, rows, *before):
        last = bool(before)
        scratch = [pltpu.VMEM((PAIRS, tokens, columns), jnp.bfloat16)]
        if last:
            scratch += [pltpu.VMEM(kind.shape, kind.dtype) for kind in totals_types]
        return pl.pallas_call(
            functools.partial(gate_up, last),
            out_shape=out_type if last else totals_types,
            grid_spec=pltpu.PrefetchScalarGridSpec(
                num_scalar_prefetch=1,
                grid=(PAIRS // per_step,),
                in_specs=[HERE, HERE, first_spec(0), first_spec(1)] + [HERE] * len(before),
                out_specs=HERE if last else [HERE] * 2,
                scratch_shapes=scratch,
            ),
            compiler_params=LIMIT,
            cost_estimate=cost(
                2 * tokens * 2 * expert_count * local_units * D // 2,
                2 * 2 * expert_count * local_units * D // 2,
            ),
            name="gate_up",
        )(parity.reshape(1), rows, gains, weights, weights, *before)

    before = gated(odd, rows_own)
    activation = gated(1 - odd, rows_other, *before, routes.T)

    activation_own = spread(activation, "tensor", PAIRS, PARITY)
    activation_other = lax.ppermute(activation_own, "tensor", NEIGHBOUR)
    parts = 2
    per_part = 4
    down_steps = expert_count // (parts * per_part)
    quarter = PAIRS // 2
    down_weights = down_weights.reshape(expert_count, 2, quarter, 2, local_units, columns)
    turned_type = jax.ShapeDtypeStruct((2, TOP, tokens, quarter * local_units), jnp.bfloat16)

    def down_spec(half, part):
        return pl.BlockSpec(
            (per_part, 1, quarter, 1, local_units, columns),
            lambda i, parity_ref: (i * parts + part, half, 0, parity_ref[0], 0, 0),
        )

    def lowered(ready, parity, rows, start, dtype):
        scratch = [pltpu.VMEM((tokens, columns), jnp.float32)]
        if not ready:
            scratch.append(pltpu.VMEM(turned_type.shape, turned_type.dtype))
        return pl.pallas_call(
            functools.partial(down, ready, parts),
            out_shape=jax.ShapeDtypeStruct((tokens, columns), dtype),
            grid_spec=pltpu.PrefetchScalarGridSpec(
                num_scalar_prefetch=1,
                grid=(down_steps,),
                in_specs=[HERE] * 4
                + [down_spec(half, part) for half in range(2) for part in range(parts)],
                out_specs=whole(tokens, columns),
                scratch_shapes=scratch,
            ),
            compiler_params=LARGE,
            cost_estimate=cost(
                tokens * expert_count * hidden_units * columns,
                expert_count * hidden_units * columns,
            ),
            name="down",
        )(parity.reshape(1), rows, routes, route_weight, start, *[down_weights] * (2 * parts))

    turned_own = pl.pallas_call(
        turn,
        out_shape=turned_type,
        in_specs=[HERE],
        out_specs=HERE,
        compiler_params=LIMIT,
        name="turn",
    )(activation_own)
    turned_own, down_weights = lax.optimization_barrier((turned_own, down_weights))

    shares = [
        lax.dynamic_slice(
            rows, (tensor_index // 2, 0, odd * half_columns), (1, tokens, half_columns)
        )[0].astype(jnp.float32)
        for rows in (rows_own, rows_other)
    ]
    hidden_here = jnp.where(
        odd == 0, jnp.concatenate(shares, axis=1), jnp.concatenate(shares[::-1], axis=1)
    )
    mixed = lowered(True, odd, turned_own, hidden_here, jnp.float32)
    return lowered(False, 1 - odd, activation_other, mixed, jnp.bfloat16)


def solution(mesh):
    return jax.shard_map(
        local,
        mesh=mesh,
        in_specs=(
            P(("dp", "expert"), "tensor"),
            P(("dp", "expert"), None),
            P(("dp", "expert"), None),
            P("tensor", "expert"),
            P(("dp", "expert"), None),
            P(),
            P(("dp", "expert"), None),
            P(("dp", "expert"), None),
            P("expert", None, "tensor"),
            P("expert", None, "tensor"),
            P("expert", None, "tensor"),
        ),
        out_specs=P(("dp", "expert"), "tensor"),
        check_vma=False,
    )
```
